32 devices in a mesh: seq: 8 (over y, x, core), head: 4 (over z).
Axes of the slice: x: 2, y: 2, z: 4, core: 2. Of those that a mesh axis runs over, the one named last changes fastest.
Arguments:
- inputs: bfloat16 [4096, 1536], P(('seq', 'head')), may hold values from -6 to 6
- norm_gain_attn: bfloat16 [1536], P(('seq', 'head')), may hold values from 0.099609375 to 1.8984375
- qkv_weight: bfloat16 [1536, 2048], P(('seq', 'head')), may hold values from -0.15625 to 0.15625
- qkv_bias: bfloat16 [2048], P(('seq', 'head')), may hold values from -3 to 3
- out_weight: bfloat16 [1536, 1536], P('head', 'seq'), may hold values from -1.75 to 1.75
- norm_gain_mlp: bfloat16 [1536], P(('seq', 'head')), may hold values from 0.099609375 to 1.8984375
- gate_weight: bfloat16 [1536, 8960], P('seq', 'head'), may hold values from -0.15625 to 0.15625
- up_weight: bfloat16 [1536, 8960], P('seq', 'head'), may hold values from -0.15625 to 0.15625
- down_weight: bfloat16 [8960, 1536], P('head', 'seq'), may hold values from -0.0625 to 0.0625
- cotangent: bfloat16 [4096, 1536], P(('seq', 'head')), may hold values from -6 to 6
- segment_ids: int32 [4096], P(('seq', 'head')), may hold values from 0 to 2, as said below
- positions: int32 [4096], P(('seq', 'head')), may hold values from 0 to 3071, as said below
Outputs:
- output: bfloat16 [4096, 1536], P(('seq', 'head'))
- grad_inputs: bfloat16 [4096, 1536], P(('seq', 'head'))
- grad_gain_attn: float32 [1536], P(('seq', 'head'))
- grad_qkv: float32 [1536, 2048], P(('seq', 'head'))
- grad_bias: float32 [1792], P(('seq', 'head'))
- grad_value_bias: float32 [256], P(('seq', 'head'))
- grad_out: float32 [1536, 1536], P('head', 'seq')
- grad_gain_mlp: float32 [1536], P(('seq', 'head'))
- grad_gate: float32 [1536, 8960], P('seq', 'head')
- grad_up: float32 [1536, 8960], P('seq', 'head')
- grad_down: float32 [8960, 1536], P('head', 'seq')
The draws below stay inside these ranges and needn't reach their ends.
Inputs may be any that keep to these rules, and one draw needn't show every extreme that they name: `segment_ids`: the 2048 prompt tokens have segment 0; continuation c, for c from 1 to 2, has 1024 tokens of segment c. On each device the first half of its 128 rows are prompt tokens and the second half continuation tokens; every token of the group stands once. A prompt token's position is its place in the prompt; a continuation token's is 2048 plus its place in its continuation; with segment_ids, positions name each token once.
All inputs are finite; a program needn't handle non-finite values.
Results may differ from the reference program's by a relative error of at most 0.028.
Values may be sent and summed in bfloat16 or wider, within the bound.
No kernel may reach another device: no remote copies, remote signals or barrier semaphores. Data moves between devices by JAX's collectives and lax.ppermute only.
A program may use at most 768 MiB of HBM per device.

```python
import math
import jax
import jax.numpy as jnp
from jax import lax

D = 1536
HEADS = 12
KV_HEADS = 2
HD = 128
FF = 8960
TOK_DEV = 128
CLEN = 1024
QD = 1536
KD = 256
QKV = 2048
TOKENS = 4096
PROMPT = 2048
NCONT = 2


def token_layout(key):
    device_count = TOKENS // TOK_DEV
    half_page = TOK_DEV // 2
    prompt_pages = jax.random.permutation(jax.random.fold_in(key, 11), device_count).astype(jnp.int32)
    cont_pages = jax.random.permutation(jax.random.fold_in(key, 12), device_count).astype(jnp.int32)
    offsets = jnp.arange(half_page, dtype=jnp.int32)
    prompt_tok = prompt_pages[:, None] * half_page + offsets[None, :]
    cont_tok = cont_pages[:, None] * half_page + offsets[None, :]
    segment_all = jnp.concatenate([jnp.zeros_like(prompt_tok), cont_tok // CLEN + 1], axis=1).reshape(-1)
    place_all = jnp.concatenate([prompt_tok, PROMPT + cont_tok % CLEN], axis=1).reshape(-1)
    return (segment_all.astype(jnp.int32), place_all.astype(jnp.int32))


def draw_segment_ids(key, part):
    segment_all, place_all = token_layout(key)
    return segment_all


def draw_positions(key, part):
    segment_all, place_all = token_layout(key)
    return place_all


def steps_of(own_key, extent, split, smallest, top_value):
    level, own = 1.0, jax.random.fold_in(own_key, 6)
    for position, blocks in split:
        steps = jnp.exp(jax.random.uniform(jax.random.fold_in(own, position), (blocks,), jnp.float32, smallest / len(split), top_value / len(split)))
        level = level * jnp.repeat(steps, extent[position] // blocks).reshape([-1 if axis == position else 1 for axis in range(len(extent))])
    return level


def normal_values(rng, dims, width, bound, cuts=(), held_as=jnp.bfloat16):
    values = jax.random.normal(rng, dims, jnp.float32) * width
    if len(cuts) > 0:
        values = steps_of(rng, dims, cuts, -0.22, 0.18) * values
    return jnp.clip(values, min=-bound, max=bound).astype(held_as)


def setup_inputs(seed: int = 0) -> dict:
    seeds = jax.random.split(jax.random.key(seed), 13)
    return {
        "inputs": normal_values(seeds[0], (TOKENS, D), 1.0, 6.0, ((0, 32),)),
        "norm_gain_attn": jnp.clip(1.0 + 0.18 * jax.random.normal(seeds[1], (D,), jnp.float32), 0.099609375, 1.8984375).astype(jnp.bfloat16),
        "qkv_weight": normal_values(seeds[2], (D, QKV), D ** -0.5, 0.15625, ((0, 32),)),
        "qkv_bias": normal_values(seeds[3], (QKV,), 0.5, 3.0, ((0, 32),)),
        "out_weight": normal_values(seeds[4], (QD, D), (QD * 32 // TOKENS + 1) ** -0.5, 1.75, ((0, 4), (1, 8))),
        "norm_gain_mlp": jnp.clip(1.0 + 0.18 * jax.random.normal(seeds[5], (D,), jnp.float32), 0.099609375, 1.8984375).astype(jnp.bfloat16),
        "gate_weight": normal_values(seeds[6], (D, FF), D ** -0.5, 0.15625, ((0, 8), (1, 4))),
        "up_weight": normal_values(seeds[7], (D, FF), D ** -0.5, 0.15625, ((0, 8), (1, 4))),
        "down_weight": normal_values(seeds[8], (FF, D), FF ** -0.5, 0.0625, ((0, 4), (1, 8))),
        "cotangent": normal_values(seeds[9], (TOKENS, D), 1.0, 6.0, ((0, 32),)),
        "segment_ids": draw_segment_ids(jax.random.fold_in(seeds[12], 71), 0),
        "positions": draw_positions(jax.random.fold_in(seeds[12], 71), 0),
    }


EPS = 1e-06
ROPE_BASE = 1000000.0
PRECISE = lax.Precision.HIGHEST

@jax.custom_vjp
def low(v):
    return lax.optimization_barrier(v.astype(jnp.bfloat16)).astype(jnp.float32)

@jax.custom_vjp
def low_back(v):
    return v

def low_keep(v):
    return (low(v), None)

def low_pass(kept, grad):
    return (grad,)

def back_keep(v):
    return (v, None)

def back_low(kept, grad):
    return (low(grad),)
low.defvjp(low_keep, low_pass)
low_back.defvjp(back_keep, back_low)

def rms_scale(values):
    return lax.rsqrt(lax.optimization_barrier(jnp.mean(values * values, axis=-1, keepdims=True)) + EPS)

def rope_tables(positions):
    freq_index = jnp.arange(HD // 2, dtype=jnp.float32) * 2.0 / HD
    inverse = 1.0 / ROPE_BASE ** freq_index
    angles = positions.astype(jnp.float32)[:, None] * inverse[None, :]
    return (jnp.cos(angles)[:, None, :], jnp.sin(angles)[:, None, :])

def rotate(values, cosine_part, sine_part):
    front_half = values[..., :HD // 2]
    back_half = values[..., HD // 2:]
    return jnp.concatenate([front_half * cosine_part - back_half * sine_part, back_half * cosine_part + front_half * sine_part], axis=-1)

def sigmoid_of(values):
    return 1.0 / (1.0 + jnp.exp(-values))

def attend(queries, key_heads, value_heads, visible):
    block_rows = queries.shape[0]
    grouped = queries.reshape(block_rows, KV_HEADS, HEADS // KV_HEADS, HD)
    scores = jnp.einsum('qgjd,kgd->gjqk', grouped, key_heads, precision=PRECISE) * HD ** (-0.5)
    scores = low_back(scores)
    scores = jnp.where(visible[None, None], scores, -1e+30)
    row_max = lax.optimization_barrier(jnp.max(scores, axis=-1, keepdims=True))
    weights = jnp.exp(scores - row_max)
    probabilities = low(weights / lax.optimization_barrier(jnp.sum(weights, axis=-1, keepdims=True)))
    mixed_heads = jnp.einsum('gjqk,kgd->qgjd', probabilities, value_heads, precision=PRECISE)
    return mixed_heads.reshape(block_rows, HEADS, HD)

def attention(query_nat, key_nat, value_nat):
    block_rows = math.gcd(256, CLEN)
    prompt_keys = key_nat[:PROMPT]
    prompt_values = value_nat[:PROMPT]
    prompt_queries = query_nat[:PROMPT].reshape(PROMPT // block_rows, block_rows, HEADS, HD)

    def prompt_block(block_item):
        queries, number = block_item
        query_pos = number * block_rows + jnp.arange(block_rows, dtype=jnp.int32)
        key_pos = jnp.arange(PROMPT, dtype=jnp.int32)
        return attend(queries, prompt_keys, prompt_values, key_pos[None, :] <= query_pos[:, None])
    prompt_out = lax.map(jax.checkpoint(prompt_block), (prompt_queries, jnp.arange(PROMPT // block_rows, dtype=jnp.int32)))
    per_cont = CLEN // block_rows
    cont_queries = query_nat[PROMPT:].reshape(NCONT * per_cont, block_rows, HEADS, HD)

    def cont_block(block_item):
        queries, number = block_item
        first_row = (PROMPT + number // per_cont * CLEN).astype(jnp.int32)
        own_keys = lax.dynamic_slice_in_dim(key_nat, first_row, CLEN, 0)
        own_values = lax.dynamic_slice_in_dim(value_nat, first_row, CLEN, 0)
        local_pos = number % per_cont * block_rows + jnp.arange(block_rows, dtype=jnp.int32)
        causal = jnp.arange(CLEN, dtype=jnp.int32)[None, :] <= local_pos[:, None]
        visible = jnp.concatenate([jnp.ones((block_rows, PROMPT), dtype=bool), causal], axis=1)
        return attend(queries, jnp.concatenate([prompt_keys, own_keys], axis=0), jnp.concatenate([prompt_values, own_values], axis=0), visible)
    cont_out = lax.map(jax.checkpoint(cont_block), (cont_queries, jnp.arange(NCONT * per_cont, dtype=jnp.int32)))
    return jnp.concatenate([prompt_out.reshape(PROMPT, HEADS, HD), cont_out.reshape(PROMPT, HEADS, HD)], axis=0)

def reference(inputs, norm_gain_attn, qkv_weight, qkv_bias, out_weight, norm_gain_mlp, gate_weight, up_weight, down_weight, cotangent, segment_ids, positions):
    natural = (positions + jnp.where(segment_ids > 0, (segment_ids - 1) * CLEN, 0)).astype(jnp.int32)
    order_index = jnp.zeros((TOKENS,), jnp.int32).at[natural].set(jnp.arange(TOKENS, dtype=jnp.int32))
    cosine_part, sine_part = rope_tables(positions)

    def forward(inputs_f, gain_one, qkv_w, bias_all, out_w, gain_two, gate_w, up_w, down_w):
        normed_one = low(inputs_f * rms_scale(inputs_f) * gain_one)
        qkv_all = low_back(jnp.dot(normed_one, qkv_w, precision=PRECISE) + bias_all)
        queries = qkv_all[:, :QD].reshape(TOKENS, HEADS, HD)
        key_heads = qkv_all[:, QD:QD + KD].reshape(TOKENS, KV_HEADS, HD)
        value_heads = qkv_all[:, QD + KD:].reshape(TOKENS, KV_HEADS, HD)
        queries = low(low_back(rotate(queries, cosine_part, sine_part)))
        key_heads = low(low_back(rotate(key_heads, cosine_part, sine_part)))
        value_heads = low(low_back(value_heads))
        mixed_nat = attention(queries[order_index], key_heads[order_index], value_heads[order_index])
        mixed_out = low(low_back(mixed_nat[natural].reshape(TOKENS, QD)))
        hidden = inputs_f + low_back(jnp.dot(mixed_out, out_w, precision=PRECISE))
        normed_two = low(hidden * rms_scale(hidden) * gain_two)
        gate_pre = low_back(jnp.dot(normed_two, gate_w, precision=PRECISE))
        up_pre = low_back(jnp.dot(normed_two, up_w, precision=PRECISE))
        middle = low(gate_pre * sigmoid_of(gate_pre) * up_pre)
        return hidden + jnp.dot(middle, down_w, precision=PRECISE)
    result, pullback = jax.vjp(forward, inputs.astype(jnp.float32), norm_gain_attn.astype(jnp.float32), qkv_weight.astype(jnp.float32), qkv_bias.astype(jnp.float32), out_weight.astype(jnp.float32), norm_gain_mlp.astype(jnp.float32), gate_weight.astype(jnp.float32), up_weight.astype(jnp.float32), down_weight.astype(jnp.float32))
    gradients = pullback(cotangent.astype(jnp.float32))
    bias_grad = gradients[3]
    return (result.astype(jnp.bfloat16), gradients[0].astype(jnp.bfloat16), gradients[1], gradients[2], bias_grad[:QD + KD], bias_grad[QD + KD:], gradients[4], gradients[5], gradients[6], gradients[7], gradients[8])
```

```python
import functools

import jax
import jax.numpy as jnp
from jax import lax
from jax.experimental import pallas as pl
from jax.experimental.pallas import tpu as pltpu
from jax.sharding import PartitionSpec as P

HEADS = 12
KV_HEADS = 2
HD = 128
QD = 1536
KD = 256
QKV = 2048


EPS = 1e-06
ROPE_BASE = 1000000.0
MASKED = -1e30
SEG_STEP = 1 << 20

BF = jnp.bfloat16
F32 = jnp.float32


def bits_of(axis):
    return (lax.axis_size(axis) - 1).bit_length()


def bit_value(axis, bit):
    return (lax.axis_index(axis) >> bit) & 1


def swap(block, axis, bit):
    count = lax.axis_size(axis)
    return lax.ppermute(block, axis, [(j, j ^ (1 << bit)) for j in range(count)])


def from_next(block, axis, apart=1):
    count = lax.axis_size(axis)
    return lax.ppermute(block, axis, [(j, (j - apart) % count) for j in range(count)])


def to_next(block, axis):
    count = lax.axis_size(axis)
    return lax.ppermute(block, axis, [(j, (j + 1) % count) for j in range(count)])


def ring_gather(block, axis):
    blocks = [block]
    for _ in range(lax.axis_size(axis) - 1):
        blocks.append(from_next(blocks[-1], axis))
    return blocks


def ring_sum(pieces, axis):
    total = pieces[-1]
    for piece in pieces[-2::-1]:
        total = piece + to_next(total.astype(BF), axis).astype(F32)
    return total


def gather_ordered(block, steps):
    done = []
    ranks = sorted(steps, reverse=True)
    for axis, bit, rank in steps:
        other = swap(block, axis, bit)
        upper = bit_value(axis, bit) == 1
        low = jnp.where(upper, other, block)
        high = jnp.where(upper, block, other)
        place = sum(1 for known in done if known > rank)
        block = jnp.stack([low, high], axis=place)
        done.append(rank)
    del ranks
    return block


def sum_ordered(block, steps, wide):
    left = sorted((rank for _, _, rank in steps), reverse=True)
    for axis, bit, rank in steps:
        place = left.index(rank)
        low = lax.index_in_dim(block, 0, place, keepdims=False)
        high = lax.index_in_dim(block, 1, place, keepdims=False)
        upper = bit_value(axis, bit) == 1
        sent = jnp.where(upper, low, high)
        kept = jnp.where(upper, high, low)
        if wide:
            block = kept + swap(sent, axis, bit)
        else:
            block = kept.astype(F32) + swap(sent.astype(BF), axis, bit).astype(F32)
        left.pop(place)
    return block


def gather_xor(block, steps):
    blocks = {0: block}
    for axis, bit in steps:
        masks = sorted(blocks)
        moved = swap(jnp.stack([blocks[m] for m in masks]), axis, bit)
        for place, mask in enumerate(masks):
            blocks[mask | 1 << bit] = moved[place]
    return blocks


def sum_xor(blocks, steps):
    for axis, bit in steps:
        masks = sorted(blocks)
        sent = [m for m in masks if m >> bit & 1]
        moved = swap(jnp.stack([blocks[m].astype(BF) for m in sent]), axis, bit)
        blocks = {m: blocks[m].astype(F32) for m in masks if not m >> bit & 1}
        for place, mask in enumerate(sent):
            blocks[mask ^ 1 << bit] = blocks[mask ^ 1 << bit] + moved[place].astype(F32)
    return blocks[0]


def roll_blocks(stacked, shift, axis=0):
    count = stacked.shape[axis]
    return lax.dynamic_slice_in_dim(
        jnp.concatenate([stacked, stacked], axis=axis), shift, count, axis
    )


def rope_tables(positions):
    freq_index = jnp.arange(HD // 2, dtype=F32) * 2.0 / HD
    inverse = 1.0 / ROPE_BASE**freq_index
    angles = positions.astype(F32)[:, None] * inverse[None, :]
    return (jnp.cos(angles)[:, None, :], jnp.sin(angles)[:, None, :])


def rotate(values, cosine_part, sine_part):
    front_half = values[..., : HD // 2]
    back_half = values[..., HD // 2 :]
    return jnp.concatenate(
        [
            front_half * cosine_part - back_half * sine_part,
            back_half * cosine_part + front_half * sine_part,
        ],
        axis=-1,
    )


def rotate_back(grad_in, cosine_part, sine_part):
    return rotate(grad_in, cosine_part, -sine_part)


def inverse_norm(values):
    return lax.rsqrt(jnp.mean(values * values, axis=-1, keepdims=True) + EPS)


def dot_nn(left, right):
    return jnp.dot(left, right, preferred_element_type=F32)


def dot_nt(left, right):
    return lax.dot_general(left, right, (((1,), (1,)), ((), ())), preferred_element_type=F32)


def dot_tn(left, right):
    return lax.dot_general(left, right, (((0,), (0,)), ((), ())), preferred_element_type=F32)


def joined(block_ref, half):
    block = block_ref[:, half]
    return block.reshape(block.shape[0] * block.shape[1], block.shape[2])


def visible_of(key_code, query_code, half):
    seen = key_code <= query_code
    if half == 1:
        seen &= key_code >= (query_code // SEG_STEP) * SEG_STEP
    return seen


PAIRS = ((0, 0), (0, 1), (1, 1))


def attend_kernel(scale, q_ref, k_ref, v_ref, kc_ref, qc_ref, mixed_ref, lse_ref, top, total, acc):
    step = pl.program_id(0)

    @pl.when(step == 0)
    def _():
        top[...] = jnp.full(top.shape, MASKED, F32)
        total[...] = jnp.zeros(total.shape, F32)
        acc[...] = jnp.zeros(acc.shape, F32)

    for key_half, query_half in PAIRS:
        keys = joined(k_ref, key_half)
        values = joined(v_ref, key_half)
        scores = dot_nt(keys, q_ref[query_half]) * scale
        if key_half == query_half:
            seen = visible_of(joined(kc_ref, key_half), qc_ref[query_half], key_half)
            scores = jnp.where(seen, scores, MASKED)
        old = top[query_half]
        new = jnp.maximum(old, jnp.max(scores, axis=0, keepdims=True))
        weights = jnp.exp(scores - new)
        if key_half == query_half:
            weights = jnp.where(seen, weights, 0.0)
        factor = jnp.exp(old - new)
        top[query_half] = new
        total[query_half] = total[query_half] * factor + jnp.sum(weights, axis=0, keepdims=True)
        acc[query_half] = acc[query_half] * factor + dot_tn(values, weights.astype(BF))

    @pl.when(step == pl.num_programs(0) - 1)
    def _():
        for half in range(2):
            mixed_ref[half] = jnp.transpose(acc[half] / total[half])
            lse_ref[half] = top[half] + jnp.log(total[half])


def whole(shape):
    return pl.BlockSpec(shape, lambda i: (0,) * len(shape))


def per_step(shape, some):
    return pl.BlockSpec((some,) + shape[1:], lambda i: (i,) + (0,) * (len(shape) - 1))


SEQ_STEP = 2


def attend(queries, keys, values, key_code, query_code):
    _, rows, _ = queries.shape
    count = keys.shape[0]
    work = 3 * rows * keys.shape[0] * keys.shape[2]
    return pl.pallas_call(
        functools.partial(attend_kernel, HD**-0.5),
        grid=(count // SEQ_STEP,),
        in_specs=[
            whole(queries.shape),
            per_step(keys.shape, SEQ_STEP),
            per_step(values.shape, SEQ_STEP),
            per_step(key_code.shape, SEQ_STEP),
            whole(query_code.shape),
        ],
        out_specs=[whole((2, rows, HD)), whole((2, 1, rows))],
        out_shape=[
            jax.ShapeDtypeStruct((2, rows, HD), F32),
            jax.ShapeDtypeStruct((2, 1, rows), F32),
        ],
        scratch_shapes=[
            pltpu.VMEM((2, 1, rows), F32),
            pltpu.VMEM((2, 1, rows), F32),
            pltpu.VMEM((2, HD, rows), F32),
        ],
        compiler_params=pltpu.CompilerParams(vmem_limit_bytes=48 * 2**20),
        cost_estimate=pl.CostEstimate(
            flops=4 * HD * work, bytes_accessed=4 * 2**20, transcendentals=work
        ),
        name="attend",
    )(queries, keys, values, key_code, query_code)


def attend_back_kernel(
    scale, q_ref, do_ref, k_ref, v_ref, kc_ref, qc_ref, lse_ref, delta_ref, dq_ref, dk_ref, dv_ref, acc
):
    step = pl.program_id(0)

    @pl.when(step == 0)
    def _():
        acc[...] = jnp.zeros(acc.shape, F32)

    for key_half in range(2):
        keys = joined(k_ref, key_half)
        values = joined(v_ref, key_half)
        grad_keys, grad_values = None, None
        for query_half in range(key_half, 2):
            queries = q_ref[query_half]
            grads = do_ref[query_half]
            scores = dot_nt(keys, queries) * scale
            weights = jnp.exp(scores - lse_ref[query_half])
            if key_half == query_half:
                seen = visible_of(joined(kc_ref, key_half), qc_ref[query_half], key_half)
                weights = jnp.where(seen, weights, 0.0)
            grad_weights = dot_nt(values, grads)
            grad_scores = (weights * (grad_weights - delta_ref[query_half])).astype(BF)
            value_term = dot_nn(weights.astype(BF), grads)
            key_term = dot_nn(grad_scores, queries)
            grad_keys = key_term if grad_keys is None else grad_keys + key_term
            grad_values = value_term if grad_values is None else grad_values + value_term
            acc[query_half] += dot_tn(keys, grad_scores)
        shape = (dk_ref.shape[0],) + dk_ref.shape[2:]
        dk_ref[:, key_half] = (grad_keys * scale).reshape(shape).astype(dk_ref.dtype)
        dv_ref[:, key_half] = grad_values.reshape(shape).astype(dv_ref.dtype)

    @pl.when(step == pl.num_programs(0) - 1)
    def _():
        for half in range(2):
            dq_ref[half] = jnp.transpose(acc[half] * scale)


def attend_back(queries, grads, keys, values, key_code, query_code, log_total, delta):
    _, rows, _ = queries.shape
    count = keys.shape[0]
    work = 3 * rows * keys.shape[0] * keys.shape[2]
    return pl.pallas_call(
        functools.partial(attend_back_kernel, HD**-0.5),
        grid=(count // SEQ_STEP,),
        in_specs=[
            whole(queries.shape),
            whole(grads.shape),
            per_step(keys.shape, SEQ_STEP),
            per_step(values.shape, SEQ_STEP),
            per_step(key_code.shape, SEQ_STEP),
            whole(query_code.shape),
            whole(log_total.shape),
            whole(delta.shape),
        ],
        out_specs=[
            whole((2, rows, HD)),
            per_step(keys.shape, SEQ_STEP),
            per_step(values.shape, SEQ_STEP),
        ],
        out_shape=[
            jax.ShapeDtypeStruct((2, rows, HD), F32),
            jax.ShapeDtypeStruct(keys.shape, BF),
            jax.ShapeDtypeStruct(values.shape, BF),
        ],
        scratch_shapes=[pltpu.VMEM((2, HD, rows), F32)],
        compiler_params=pltpu.CompilerParams(vmem_limit_bytes=48 * 2**20),
        cost_estimate=pl.CostEstimate(
            flops=10 * HD * work, bytes_accessed=6 * 2**20, transcendentals=work
        ),
        name="attend_back",
    )(queries, grads, keys, values, key_code, query_code, log_total, delta)


def per_device(
    inputs,
    norm_gain_attn,
    qkv_weight,
    qkv_bias,
    out_weight,
    norm_gain_mlp,
    gate_weight,
    up_weight,
    down_weight,
    cotangent,
    segment_ids,
    positions,
):
    tok_rows = inputs.shape[0]
    width = inputs.shape[1]
    seq_dev = lax.axis_size("seq")
    heads_dev = lax.axis_size("head")
    heads_here = HEADS // heads_dev
    copies = heads_dev // KV_HEADS
    group_rows = heads_dev * tok_rows
    half_rows = group_rows // 2
    query_cols = heads_here * HD
    quarter_ff = gate_weight.shape[1]
    head_index = lax.axis_index("head")
    seq_index = lax.axis_index("seq")
    odd = head_index % 2 == 1
    seq_bits = bits_of("seq")
    head_bits = bits_of("head")
    far = list(range(1, seq_bits))
    one_way = [("seq", bit) for bit in far]
    other_way = one_way[::-1]
    near = [("seq", 0)]

    def ranked(steps):
        return [(axis, bit, bit) for axis, bit in steps]

    gain_cols = norm_gain_attn.shape[0]
    bias_cols = qkv_bias.shape[0]
    small = jnp.concatenate(
        [
            norm_gain_attn,
            norm_gain_mlp,
            qkv_bias,
            (positions >> 7).astype(BF),
            (positions & 127).astype(BF),
            segment_ids.astype(BF),
        ]
    )
    small_steps = [("head", bit, bit) for bit in range(head_bits)] + [
        ("seq", bit, bit + head_bits) for bit in range(seq_bits)
    ]
    small_all = gather_ordered(small, small_steps).reshape(seq_dev * heads_dev, small.shape[0])
    cuts, start = [], 0
    for size in (gain_cols, gain_cols, bias_cols, tok_rows, tok_rows, tok_rows):
        cuts.append(small_all[:, start : start + size])
        start += size
    gain_attn = cuts[0].reshape(-1).astype(F32)
    gain_mlp = cuts[1].reshape(-1).astype(F32)
    bias_all = cuts[2].reshape(-1).astype(F32)
    pos_all = (cuts[3].astype(jnp.int32) << 7) + cuts[4].astype(jnp.int32)
    seg_all = cuts[5].astype(jnp.int32)

    pos_all = roll_blocks(pos_all.reshape(seq_dev, heads_dev, tok_rows), head_index, 1)
    seg_all = roll_blocks(seg_all.reshape(seq_dev, heads_dev, tok_rows), head_index, 1)
    code_all = seg_all * SEG_STEP + pos_all
    query_pos = lax.dynamic_index_in_dim(pos_all, seq_index, 0, keepdims=False).reshape(-1)
    query_code = lax.dynamic_index_in_dim(code_all, seq_index, 0, keepdims=False)

    def halves_first(values):
        tail = values.shape[1:]
        return jnp.swapaxes(
            values.reshape((heads_dev, 2, tok_rows // 2) + tail), 0, 1
        ).reshape((2, half_rows) + tail)

    def halves_back(values):
        tail = values.shape[2:]
        return jnp.swapaxes(
            values.reshape((2, heads_dev, tok_rows // 2) + tail), 0, 1
        ).reshape((group_rows,) + tail)

    def to_heads(values):
        return jnp.swapaxes(halves_first(values), 1, 2).reshape(2, heads_here * half_rows, HD)

    def from_heads(values):
        return halves_back(jnp.swapaxes(values.reshape(2, heads_here, half_rows, HD), 1, 2))

    query_code = jnp.broadcast_to(
        halves_first(query_code.reshape(-1))[:, None, None, :], (2, 1, heads_here, half_rows)
    ).reshape(2, 1, heads_here * half_rows)
    key_code = jnp.stack(
        [
            lax.dynamic_index_in_dim(code_all, seq_index ^ mask, 0, keepdims=False)
            for mask in range(seq_dev)
        ]
    )
    key_code = jnp.swapaxes(
        key_code.reshape(seq_dev, heads_dev, 2, tok_rows // 2), 1, 2
    ).reshape(seq_dev, 2, half_rows, 1)

    pair_local = jnp.concatenate([gate_weight, up_weight], axis=1)
    pair_all = lax.all_gather(pair_local, "seq", axis=0, tiled=True)
    down_all = lax.all_gather(down_weight.T, "seq", axis=0, tiled=True)

    def head_columns(values, head):
        last = values.ndim - 1
        slot = head // copies
        return [
            lax.dynamic_slice_in_dim(values, head * query_cols, query_cols, last),
            lax.dynamic_slice_in_dim(values, QD + slot * HD, HD, last),
            lax.dynamic_slice_in_dim(values, QD + KD + slot * HD, HD, last),
        ]

    rows_of = [jnp.concatenate(head_columns(qkv_weight, head_index), axis=1)]
    for apart in range(1, heads_dev):
        target = (head_index - apart) % heads_dev
        block = jnp.concatenate(head_columns(qkv_weight, target), axis=1)
        rows_of.append(from_next(block, "head", apart))
    own_rows = roll_blocks(jnp.stack(rows_of), (heads_dev - head_index) % heads_dev)
    own_rows = own_rows.reshape(-1, query_cols + 2 * HD)
    query_weight = gather_ordered(own_rows[:, :query_cols], ranked(one_way + near)).reshape(
        width, query_cols
    )
    kv_weight = gather_ordered(own_rows[:, query_cols:], ranked(other_way + near)).reshape(
        width, 2 * HD
    )

    out_rows = jnp.concatenate([block.T for block in ring_gather(out_weight, "head")], axis=1)
    out_all = lax.all_gather(out_rows, "seq", axis=0, tiled=True)

    inputs_f = jnp.concatenate(ring_gather(inputs, "head")).astype(F32)
    inv_one = inverse_norm(inputs_f)
    normed_one = (inputs_f * inv_one * gain_attn).astype(BF)
    cosine_part, sine_part = rope_tables(query_pos)
    bias_here = head_columns(bias_all, head_index)
    queries = dot_nn(normed_one, query_weight) + bias_here[0]
    keys_values = dot_nn(normed_one, kv_weight) + jnp.concatenate(bias_here[1:])
    queries = rotate(
        queries.reshape(group_rows, heads_here, HD), cosine_part, sine_part
    ).astype(BF)
    keys = rotate(keys_values[:, None, :HD], cosine_part, sine_part)[:, 0].astype(BF)
    values = keys_values[:, HD:].astype(BF)
    keys_far = gather_xor(halves_first(keys), one_way)
    values_far = gather_xor(halves_first(values), other_way)
    far_masks = sorted(keys_far)
    kv_near = jnp.stack(
        [jnp.stack([blocks[mask] for mask in far_masks]) for blocks in (keys_far, values_far)]
    )
    kv_all = jnp.stack([kv_near, swap(kv_near, "seq", 0)], axis=2).reshape(
        2, seq_dev, 2, half_rows, HD
    )
    queries = to_heads(queries)
    mixed_f, log_total = attend(queries, kv_all[0], kv_all[1], key_code, query_code)
    mixed_f = from_heads(mixed_f)
    mixed = mixed_f.astype(BF).reshape(group_rows, query_cols)
    mixed_all = [
        jnp.concatenate([block[group_rows - far_by * tok_rows :], block[: group_rows - far_by * tok_rows]])
        for far_by, block in enumerate(ring_gather(mixed, "head"))
    ]
    hidden = inputs_f + dot_nt(jnp.concatenate(mixed_all, axis=1), out_all)

    inv_two = inverse_norm(hidden)
    normed_two = (hidden * inv_two * gain_mlp).astype(BF)
    cot_grp = jnp.concatenate(ring_gather(cotangent, "head"))
    pair_pre = dot_nn(normed_two, pair_all)
    gate_pre = pair_pre[:, :quarter_ff]
    up_pre = pair_pre[:, quarter_ff:]
    gate_sig = 1.0 / (1.0 + jnp.exp(-gate_pre))
    activated = gate_pre * gate_sig
    middle = (activated * up_pre).astype(BF)
    grad_middle = dot_nn(cot_grp, down_all)
    d_gate = grad_middle * up_pre * gate_sig * (1.0 + gate_pre * (1.0 - gate_sig))
    d_up = grad_middle * activated
    d_pair = jnp.concatenate([d_gate.astype(BF), d_up.astype(BF)], axis=1)
    d_normed_two = dot_nt(d_pair, pair_all)

    def split_rows(values):
        return [values[i * tok_rows : (i + 1) * tok_rows] for i in range(heads_dev)]

    d_normed_two = ring_sum(split_rows(d_normed_two), "head")
    own_hidden = hidden[:tok_rows]
    own_inv = inv_two[:tok_rows]
    scaled = d_normed_two * gain_mlp
    grad_gain_two = jnp.sum(d_normed_two * own_hidden * own_inv, axis=0)
    inner = jnp.mean(scaled * own_hidden, axis=-1, keepdims=True)
    d_hidden = cotangent.astype(F32) + own_inv * scaled - own_hidden * own_inv**3 * inner
    d_branch = d_hidden.astype(BF)

    d_mixed_own = dot_nn(d_branch, out_all).astype(BF)
    d_mixed = [d_mixed_own[:, :query_cols]]
    for apart in range(1, heads_dev):
        place = (heads_dev - apart) % heads_dev
        block = d_mixed_own[:, place * query_cols : (place + 1) * query_cols]
        d_mixed.append(from_next(block, "head", apart))
    d_mixed = jnp.concatenate(d_mixed).reshape(group_rows, heads_here, HD)
    delta = jnp.sum(d_mixed.astype(F32) * mixed_f, axis=-1)
    delta = jnp.swapaxes(halves_first(delta), 1, 2).reshape(2, 1, heads_here * half_rows)
    d_queries, d_keys_all, d_values_all = attend_back(
        queries, to_heads(d_mixed), kv_all[0], kv_all[1], key_code, query_code, log_total, delta
    )
    d_kv = jnp.stack([d_keys_all, d_values_all]).reshape(2, seq_dev // 2, 2, 2, half_rows, HD)
    d_kv = d_kv[:, :, 0].astype(F32) + swap(d_kv[:, :, 1], "seq", 0).astype(F32)
    d_keys = sum_xor({mask: d_kv[0, i] for i, mask in enumerate(far_masks)}, one_way[::-1])
    d_values = sum_xor({mask: d_kv[1, i] for i, mask in enumerate(far_masks)}, other_way[::-1])
    d_other = swap(jnp.where(odd, d_keys, d_values).astype(BF), "head", 0)
    d_kv_own = jnp.where(odd, d_values, d_keys).astype(F32)
    d_other = d_other.reshape(2, heads_dev, tok_rows // 2, HD)
    d_other = roll_blocks(d_other, jnp.where(odd, 1, heads_dev - 1), 1).reshape(2, half_rows, HD)
    d_kv_own = halves_back(d_kv_own + d_other.astype(F32)).astype(BF).astype(F32)
    d_queries = from_heads(d_queries).astype(BF).astype(F32)
    d_cols = jnp.concatenate(
        [
            rotate_back(d_queries, cosine_part, sine_part).reshape(group_rows, query_cols),
            jnp.where(
                odd, d_kv_own, rotate_back(d_kv_own[:, None, :], cosine_part, sine_part)[:, 0]
            ),
        ],
        axis=1,
    ).astype(BF)
    back_weight = jnp.concatenate(
        [query_weight, jnp.where(odd, kv_weight[:, HD:], kv_weight[:, :HD])], axis=1
    )
    d_normed_one = dot_nt(d_cols, back_weight)
    grad_gain_one = jnp.sum(d_normed_one * inputs_f * inv_one, axis=0)
    d_normed_one = ring_sum(split_rows(d_normed_one), "head")
    scaled = d_normed_one * gain_attn
    inner = jnp.mean(scaled * inputs_f[:tok_rows], axis=-1, keepdims=True)
    grad_inputs = (
        d_hidden + inv_one[:tok_rows] * scaled - inputs_f[:tok_rows] * inv_one[:tok_rows] ** 3 * inner
    ).astype(BF)

    grad_cols = dot_tn(normed_one, d_cols).astype(BF)
    grad_cols = grad_cols.reshape((2,) * seq_bits + (width // seq_dev, query_cols + HD))
    grad_cols = jnp.concatenate(
        [
            sum_ordered(grad_cols[..., : 2 * HD], ranked(near + one_way[::-1]), False),
            sum_ordered(grad_cols[..., 2 * HD :], ranked(near + other_way[::-1]), False),
        ],
        axis=1,
    )
    own_wide = width // (seq_dev * heads_dev)
    grad_blocks = grad_cols.reshape(heads_dev, own_wide, query_cols + HD)
    grad_qkv = jnp.zeros((own_wide, QKV), F32)
    for apart in range(heads_dev):
        source = (head_index + apart) % heads_dev
        target = (head_index - apart) % heads_dev
        block = lax.dynamic_index_in_dim(grad_blocks, target, 0, keepdims=False)
        if apart:
            block = from_next(block.astype(BF), "head", apart).astype(F32)
        kv_place = QD + source % 2 * KD + source // copies * HD
        grad_qkv = lax.dynamic_update_slice_in_dim(
            grad_qkv, block[:, :query_cols], source * query_cols, 1
        )
        grad_qkv = lax.dynamic_update_slice_in_dim(grad_qkv, block[:, query_cols:], kv_place, 1)

    branch_grp = jnp.concatenate(ring_gather(d_branch, "head"))
    grad_pair = lax.psum_scatter(
        dot_tn(normed_two, d_pair).astype(BF), "seq", scatter_dimension=0, tiled=True
    ).astype(F32)
    grad_down = lax.psum_scatter(
        dot_tn(cot_grp, middle).astype(BF), "seq", scatter_dimension=0, tiled=True
    ).astype(F32).T
    grad_out = lax.psum_scatter(
        dot_tn(branch_grp, mixed).astype(BF), "seq", scatter_dimension=0, tiled=True
    ).astype(F32).T

    output = ring_sum(split_rows(dot_nt(middle, down_all)), "head")
    output = (own_hidden + output).astype(BF)

    bias_cols_sum = jnp.sum(d_cols.astype(F32), axis=0)
    bias_sum = lax.dynamic_update_slice_in_dim(
        jnp.zeros((QKV,), F32), bias_cols_sum[:query_cols], head_index * query_cols, 0
    )
    bias_sum = lax.dynamic_update_slice_in_dim(
        bias_sum,
        bias_cols_sum[query_cols:],
        QD + head_index % 2 * KD + head_index // copies * HD,
        0,
    )
    devices = seq_dev * heads_dev
    small_grads = jnp.concatenate(
        [
            grad_gain_one.reshape(devices, -1),
            grad_gain_two.reshape(devices, -1),
            bias_sum[: QD + KD].reshape(devices, -1),
            bias_sum[QD + KD :].reshape(devices, -1),
        ],
        axis=1,
    )
    small_grads = sum_ordered(
        small_grads.reshape((2,) * (seq_bits + head_bits) + (-1,)), small_steps[::-1], True
    )
    one = gain_cols
    two = one + gain_cols
    three = two + (QD + KD) // devices
    return (
        output,
        grad_inputs,
        small_grads[:one],
        grad_qkv,
        small_grads[two:three],
        small_grads[three:],
        grad_out,
        small_grads[one:two],
        grad_pair[:, :quarter_ff],
        grad_pair[:, quarter_ff:],
        grad_down,
    )


def solution(mesh):
    both = ("seq", "head")
    in_specs = (
        P(both, None),
        P(both),
        P(both, None),
        P(both),
        P("head", "seq"),
        P(both),
        P("seq", "head"),
        P("seq", "head"),
        P("head", "seq"),
        P(both, None),
        P(both),
        P(both),
    )
    out_specs = (
        P(both, None),
        P(both, None),
        P(both),
        P(both, None),
        P(both),
        P(both),
        P("head", "seq"),
        P(both),
        P("seq", "head"),
        P("seq", "head"),
        P("head", "seq"),
    )
    return jax.shard_map(
        per_device, mesh=mesh, in_specs=in_specs, out_specs=out_specs, check_vma=False
    )
```

```python
import functools

import jax
import jax.numpy as jnp
from jax import lax
from jax.experimental import pallas as pl
from jax.experimental.layout import Layout, with_layout_constraint
from jax.experimental.pallas import tpu as pltpu
from jax.sharding import PartitionSpec as P

HEADS = 12
KV_HEADS = 2
HD = 128
QD = 1536
KD = 256
QKV = 2048


EPS = 1e-06
ROPE_BASE = 1000000.0
MASKED = -1e30
SEG_STEP = 1 << 20
TILE = 768
MIB = 2**20

BF = jnp.bfloat16
F32 = jnp.float32


def plain(values):
    return with_layout_constraint(values, Layout(major_to_minor=tuple(range(values.ndim))))


def bits_of(axis):
    return (lax.axis_size(axis) - 1).bit_length()


def bit_value(axis, bit):
    return (lax.axis_index(axis) >> bit) & 1


def send(block, axis, target):
    count = lax.axis_size(axis)
    return plain(lax.ppermute(plain(block), axis, [(j, target(j) % count) for j in range(count)]))


def swap(block, axis, bit):
    return send(block, axis, lambda j: j ^ (1 << bit))


def from_next(block, axis, apart=1):
    return send(block, axis, lambda j: j - apart)


def to_next(block, axis):
    return send(block, axis, lambda j: j + 1)


def tie_kernel(*refs):
    del refs


def tie_all(blocks, *others):
    count = len(blocks)
    return pl.pallas_call(
        tie_kernel,
        in_specs=[pl.BlockSpec(memory_space=pl.ANY)] * (count + len(others)),
        out_specs=[pl.BlockSpec(memory_space=pl.ANY)] * count,
        out_shape=[jax.ShapeDtypeStruct(block.shape, block.dtype) for block in blocks],
        input_output_aliases={i: i for i in range(count)},
        compiler_params=pltpu.CompilerParams(vmem_limit_bytes=MIB),
        name="tie",
    )(*blocks, *others)


def tie(block, *others):
    return tie_all([block], *others)[0]


def gather_blocks(block, axis, last=()):
    half = block.shape[0] // 2
    above = from_next(block, axis)
    below = to_next(block, axis)
    above, below = tie_all([above, below], *last)
    return [block, above, from_next(above[:half], axis), to_next(below[half:], axis), below]


def sum_first(far, axis):
    return from_next(far[0], axis), to_next(far[1], axis)


def sum_payload(ahead, behind, moved, last=()):
    half = ahead.shape[0] // 2
    from_above, from_below = tie_all(moved, *last)
    down = jnp.concatenate([behind[:half].astype(F32) + from_above.astype(F32), behind[half:].astype(F32)])
    up = jnp.concatenate([ahead[:half].astype(F32), ahead[half:].astype(F32) + from_below.astype(F32)])
    return down.astype(BF), up.astype(BF)


def gather_far(block, axis, last=()):
    count = lax.axis_size(axis) // 2
    if count != 4:
        blocks = [send(block, axis, lambda j: j ^ 2 * i) if i else plain(block) for i in range(count)]
        return jnp.stack(blocks), blocks[1:3]
    half = block.shape[0] // 2
    first = swap(block, axis, 1), swap(block, axis, 2)
    one, two = tie_all(first, *last)
    parts = [swap(one[:half], axis, 2), swap(two[half:], axis, 1)]
    return plain(jnp.stack([block, one, two, jnp.concatenate(parts)])), parts


def total(terms):
    result = terms[0].astype(F32)
    for term in terms[1:]:
        result = result + term.astype(F32)
    return result


def sum_step(terms, axis, bit, last=()):
    half = terms[0].shape[0] // 2
    sent = total([term[half:] for term in terms]).astype(BF)
    moved = swap(tie(sent, *last) if last else sent, axis, bit)
    return [term[:half] for term in terms] + [moved]


def sum_halving(terms, axis, bits):
    for bit in bits:
        terms = sum_step(terms, axis, bit)
    return total([term[0] for term in terms])


def sum_xor(blocks, axis, bits):
    blocks = dict(enumerate(blocks))
    for bit in bits:
        place = 1 << bit - 1
        sent = [m for m in sorted(blocks) if m & place]
        moved = swap(jnp.stack([blocks[m].astype(BF) for m in sent]), axis, bit)
        for i, m in enumerate(sent):
            blocks[m ^ place] = blocks[m ^ place] + moved[i].astype(F32)
            del blocks[m]
    return blocks[0], moved


def roll_blocks(stacked, shift, axis=0):
    count = stacked.shape[axis]
    return lax.dynamic_slice_in_dim(
        jnp.concatenate([stacked, stacked], axis=axis), shift, count, axis
    )


def dot_nn(left, right):
    return jnp.dot(left, right, preferred_element_type=F32)


def dot_nt(left, right):
    return lax.dot_general(left, right, (((1,), (1,)), ((), ())), preferred_element_type=F32)


def dot_tn(left, right):
    return lax.dot_general(left, right, (((0,), (0,)), ((), ())), preferred_element_type=F32)


def inverse_norm(values):
    return lax.rsqrt(jnp.mean(values * values, axis=-1, keepdims=True) + EPS)


def vmem():
    return pl.BlockSpec(memory_space=pltpu.VMEM)


def smem():
    return pl.BlockSpec(memory_space=pltpu.SMEM)


def anywhere():
    return pl.BlockSpec(memory_space=pl.ANY)


def shape_of(shape, dtype=BF):
    return jax.ShapeDtypeStruct(shape, dtype)


def fixed(shape):
    return pl.BlockSpec(shape, lambda *i: (0,) * len(shape))


def params(mib):
    return pltpu.CompilerParams(vmem_limit_bytes=mib * MIB)


def cost(micros):
    return pl.CostEstimate(flops=int(micros * 1153e6), bytes_accessed=0, transcendentals=0)


def cut(size, tile):
    return [(at, min(tile, size - at)) for at in range(0, size, tile)]


def start_blocks(own_ref, near_ref, other_ref, to_ref, sem):
    count = near_ref.shape[0]
    rows = to_ref.shape[0] // (2 * count)
    copies = []
    for side, source in enumerate((near_ref, other_ref)):
        for i in range(count):
            at = pl.multiple_of((own_ref[0] ^ (2 * i + side)) * rows, 16)
            copy = pltpu.make_async_copy(
                source.at[i, pl.ds(0, rows), :], to_ref.at[pl.ds(at, rows), :], sem.at[side, i]
            )
            copy.start()
            copies.append(copy)
    return copies


def masks_of(bits):
    masks = [0]
    for bit in bits[::-1]:
        masks += [mask | 1 << bit for mask in masks]
    return masks


def store_rows(refs, cols, values):
    at = 0
    for ref in refs:
        ref[:, cols] = values[at : at + ref.shape[0]].astype(ref.dtype)
        at += ref.shape[0]


def row_shapes(tok_rows, width):
    half = tok_rows // 2
    return [shape_of((tok_rows, width), F32), shape_of((tok_rows, width))] + [
        shape_of((rows, width)) for rows in (half, half, tok_rows)
    ]


def fill_rows(to_ref, parts):
    at = 0
    for part in parts:
        to_ref[at : at + part.shape[0], :] = part[...]
        at += part.shape[0]


def head_rows(tok_rows, blocks):
    half_block = tok_rows // 2
    return [
        (half, u * half_block, u * tok_rows + half * half_block, half_block)
        for u in range(blocks)
        for half in range(2)
    ]


def project_kernel(heads, own_ref, *refs):
    parts = refs[:5]
    gain_ref, bias_ref, cos_ref, sin_ref, near, other = refs[5:11]
    q_ref, kv_ref, x_ref, normed_ref, w_ref, sem = refs[11:]
    copies = start_blocks(own_ref, near, other, w_ref, sem)
    fill_rows(x_ref, parts)
    values = x_ref[...].astype(F32)
    normed_ref[...] = (values * inverse_norm(values) * gain_ref[...]).astype(BF)
    for copy in copies:
        copy.wait()
    joint = dot_nn(normed_ref[...], w_ref[...]) + bias_ref[...]
    tok_rows = parts[0].shape[0]
    blocks = x_ref.shape[0] // tok_rows
    half_rows = x_ref.shape[0] // 2
    for j in range(heads + 2):
        part = joint[:, j * HD : (j + 1) * HD]
        if j <= heads:
            part = part * cos_ref[...] + pltpu.roll(part, HD // 2, 1) * sin_ref[...]
        part = part.astype(BF)
        for half, low, row, count in head_rows(tok_rows, blocks):
            piece = part[row : row + count]
            if j < heads:
                q_ref[half, j * half_rows + low : j * half_rows + low + count, :] = piece
            else:
                kv_ref[j - heads, half, low : low + count, :] = piece


def project(own, parts, gain, bias, cos, sin, near, other, heads):
    width = parts[0].shape[1]
    rows = cos.shape[0]
    cols = near.shape[2]
    return pl.pallas_call(
        functools.partial(project_kernel, heads),
        in_specs=[smem()] + [vmem()] * 9 + [anywhere()] * 2,
        out_specs=[vmem()] * 5,
        out_shape=[
            shape_of((2, heads * rows // 2, HD)),
            shape_of((2, 2, rows // 2, HD)),
            shape_of((rows, width)),
            shape_of((rows, width)),
            shape_of((width, cols)),
        ],
        scratch_shapes=[pltpu.SemaphoreType.DMA((2, near.shape[0]))],
        compiler_params=params(60),
        cost_estimate=cost(2.8),
        name="project",
    )(own, *parts, gain, bias, cos, sin, near, other)


def project_back_kernel(heads, orders, own_ref, head_ref, *refs):
    dq_ref, dkv_ref, cos_ref, sin_ref, normed_ref, x_ref, w_ref, mixed_ref = refs[:8]
    parts = refs[8:13]
    gain_two_ref = refs[13]
    dn_refs = refs[14:19]
    cols_kept, cols_sent, outs_kept, outs_sent = refs[19:23]
    cols, branch, wide, wide_out, bias_v, small_v = refs[23:]
    rows = cos_ref.shape[0]
    half_rows = rows // 2
    tok_rows = parts[0].shape[0]
    blocks = rows // tok_rows
    head = head_ref[0]
    odd = (head & 1) == 1
    for half, low, row, count in head_rows(tok_rows, blocks):
        here = slice(row, row + count)
        for j in range(heads + 1):
            if j < heads:
                start = j * half_rows + low
                part = dq_ref[half, start : start + count, :]
            else:
                part = dkv_ref[half, low : low + count, :]
            part = part.astype(BF).astype(F32)
            turned = part * cos_ref[here, :] - pltpu.roll(part, HD // 2, 1) * sin_ref[here, :]
            if j == heads:
                turned = jnp.where(odd, part, turned)
            cols[here, j * HD : (j + 1) * HD] = turned.astype(BF)
    last = heads * HD
    bias = jnp.sum(cols[...].astype(F32), axis=0, keepdims=True)
    bias_v[...] = jnp.zeros(bias_v.shape, F32)
    bias_v[:, pl.ds(pl.multiple_of(head * last, HD), last)] = bias[:, :last]
    copies = (QD // last) // KV_HEADS
    slot = QD + (head & 1) * KD + (head // copies) * HD
    bias_v[:, pl.ds(pl.multiple_of(slot, HD), HD)] = bias[:, last:]
    key_w = jnp.where(odd, w_ref[:, last + HD :], w_ref[:, last : last + HD])
    grad = dot_nt(cols[:, :last], w_ref[:, :last]) + dot_nt(cols[:, last:], key_w)
    store_rows(dn_refs, slice(None), grad)
    values = x_ref[...].astype(F32)
    gain_one = jnp.sum(grad * (values * inverse_norm(values)), axis=0, keepdims=True)
    seq_dev = small_v.shape[0]
    small_v[...] = jnp.zeros(small_v.shape, BF)
    for row, vectors in enumerate(
        ((gain_one, gain_two_ref[...]), (bias_v[:, : QD + KD], bias_v[:, QD + KD :]))
    ):
        for i in range(seq_dev):
            at = 0
            for vector in vectors:
                size = vector.shape[1] // seq_dev
                small_v[i, row : row + 1, at : at + size] = vector[:, i * size : (i + 1) * size].astype(BF)
                at += size
    count = outs_kept.shape[1]
    fill_rows(branch, parts)
    wide[...] = dot_tn(normed_ref[...], cols[...]).astype(BF)
    wide_out[...] = dot_tn(branch[...], mixed_ref[...]).astype(BF)
    for i in range(cols_kept.shape[0]):
        for source, targets, order in (
            (wide, (cols_kept, cols_sent), orders[0]),
            (wide_out, (outs_kept, outs_sent), orders[1]),
        ):
            for side, to in enumerate(targets):
                block = own_ref[0] ^ order[i] ^ side
                to[i, :count] = source[pl.ds(pl.multiple_of(block * count, 16), count), :]
                if source is wide:
                    to[i, count:] = small_v[block]


MORE_ROWS = 16


def project_back(own, head, orders, dq, dkv, cos, sin, normed, x, w, mixed, parts, gain_two):
    rows, width = normed.shape
    heads = dq.shape[1] // (rows // 2)
    cols = (heads + 1) * HD
    tok_rows = parts[0].shape[0]
    far = len(orders[0])
    part_rows = width // (2 * far)
    return pl.pallas_call(
        functools.partial(project_back_kernel, heads, orders),
        in_specs=[smem()] * 2 + [vmem()] * 14,
        out_specs=[vmem()] * 9,
        out_shape=[
            *row_shapes(tok_rows, width),
            shape_of((far, part_rows + MORE_ROWS, cols)),
            shape_of((far, part_rows + MORE_ROWS, cols)),
            shape_of((far, part_rows, heads * HD)),
            shape_of((far, part_rows, heads * HD)),
        ],
        scratch_shapes=[
            pltpu.VMEM((rows, cols), BF),
            pltpu.VMEM((rows, width), BF),
            pltpu.VMEM((width, cols), BF),
            pltpu.VMEM((width, heads * HD), BF),
            pltpu.VMEM((1, QKV), F32),
            pltpu.VMEM((2 * far, MORE_ROWS, cols), BF),
        ],
        compiler_params=params(60),
        cost_estimate=cost(4.5),
        name="project_back",
    )(own, head, dq, dkv, cos, sin, normed, x, w, mixed, *parts, gain_two)


def visible_of(key_code, query_code, half):
    seen = key_code <= query_code
    if half == 1:
        seen &= key_code >= (query_code // SEG_STEP) * SEG_STEP
    return seen


PAIRS = ((0, 0), (0, 1), (1, 1))
SEQ_STEP = 2


def pick_side(first_steps, near_ref, other_ref, which, half):
    near = near_ref[:, which, half]
    other = other_ref[:, which, half]
    block = jnp.where(pl.program_id(0) < first_steps, near, other)
    return block.reshape(block.shape[0] * block.shape[1], block.shape[2])


def codes(code_ref, half):
    block = code_ref[:, half]
    return block.reshape(block.shape[0] * block.shape[1], 1)


def attend_kernel(scale, first_steps, tok_rows, q_ref, near_ref, other_ref, kc_ref, qc_ref, *refs):
    mixed_ref, wide_ref, lse_ref, top, total, acc = refs[-6:]
    step = pl.program_id(0)

    @pl.when(step == 0)
    def _():
        top[...] = jnp.full(top.shape, MASKED, F32)
        total[...] = jnp.zeros(total.shape, F32)
        acc[...] = jnp.zeros(acc.shape, F32)

    for key_half, query_half in PAIRS:
        keys = pick_side(first_steps, near_ref, other_ref, 0, key_half)
        values = pick_side(first_steps, near_ref, other_ref, 1, key_half)
        scores = dot_nt(keys, q_ref[query_half]) * scale
        if key_half == query_half:
            seen = visible_of(codes(kc_ref, key_half), qc_ref[query_half], key_half)
            scores = jnp.where(seen, scores, MASKED)
        old = top[query_half]
        new = jnp.maximum(old, jnp.max(scores, axis=0, keepdims=True))
        weights = jnp.exp(scores - new)
        if key_half == query_half:
            weights = jnp.where(seen, weights, 0.0)
        factor = jnp.exp(old - new)
        top[query_half] = new
        total[query_half] = total[query_half] * factor + jnp.sum(weights, axis=0, keepdims=True)
        acc[query_half] = acc[query_half] * factor + dot_tn(values, weights.astype(BF))

    @pl.when(step == pl.num_programs(0) - 1)
    def _():
        blocks = mixed_ref.shape[0] // tok_rows
        half_rows = mixed_ref.shape[0] // 2
        for half in range(2):
            wide_ref[half] = jnp.transpose(acc[half] / total[half])
            lse_ref[half] = top[half] + jnp.log(total[half])
        for half, low, row, count in head_rows(tok_rows, blocks):
            for j in range(mixed_ref.shape[1] // HD):
                at = j * half_rows + low
                mixed_ref[row : row + count, j * HD : (j + 1) * HD] = wide_ref[
                    half, at : at + count, :
                ].astype(BF)


def side_specs(shape, first_steps):
    block = (SEQ_STEP,) + shape[1:]
    rest = (0,) * (len(shape) - 1)
    return [
        pl.BlockSpec(block, lambda i: (jnp.minimum(i, first_steps - 1),) + rest),
        pl.BlockSpec(block, lambda i: (jnp.maximum(i - first_steps, 0),) + rest),
    ]


def code_spec(shape):
    return pl.BlockSpec((SEQ_STEP,) + shape[1:], lambda i: (i,) + (0,) * (len(shape) - 1))


def attend(queries, near, other, key_code, query_code, tok_rows, others):
    _, rows, _ = queries.shape
    half_rows = near.shape[3]
    heads = rows // half_rows
    first_steps = near.shape[0] // SEQ_STEP
    return pl.pallas_call(
        functools.partial(attend_kernel, HD**-0.5, first_steps, tok_rows),
        grid=(2 * first_steps,),
        in_specs=[fixed(queries.shape)]
        + side_specs(near.shape, first_steps)
        + [code_spec(key_code.shape), fixed(query_code.shape)]
        + [anywhere()] * len(others),
        out_specs=[fixed((2 * half_rows, heads * HD)), fixed((2, rows, HD)), fixed((2, 1, rows))],
        out_shape=[
            shape_of((2 * half_rows, heads * HD)),
            shape_of((2, rows, HD), F32),
            shape_of((2, 1, rows), F32),
        ],
        scratch_shapes=[
            pltpu.VMEM((2, 1, rows), F32),
            pltpu.VMEM((2, 1, rows), F32),
            pltpu.VMEM((2, HD, rows), F32),
        ],
        compiler_params=params(60),
        cost_estimate=cost(3),
        name="attend",
    )(queries, near, other, key_code, query_code, *others)


def attend_back_kernel(scale, first_steps, others, q_ref, *refs):
    grads = refs[:4]
    wide_ref, near_ref, other_ref, kc_ref, qc_ref, lse_ref = refs[4:10]
    dq_ref, own_ref, sent_ref, acc, do, delta = refs[10 + others :]
    step = pl.program_id(0)
    half_rows = near_ref.shape[3]
    tok_rows = grads[0].shape[0]

    @pl.when(step == 0)
    def _():
        acc[...] = jnp.zeros(acc.shape, F32)
        for u, grad in enumerate(grads):
            for half, low, row, count in head_rows(tok_rows, 1):
                for j in range(grad.shape[1] // HD):
                    at = j * half_rows + u * (tok_rows // 2)
                    do[half, at : at + count, :] = grad[row : row + count, j * HD : (j + 1) * HD]
        for half in range(2):
            product = do[half].astype(F32) * wide_ref[half]
            delta[half] = jnp.sum(jnp.transpose(product), axis=0, keepdims=True)

    results = []
    for key_half in range(2):
        keys = pick_side(first_steps, near_ref, other_ref, 0, key_half)
        values = pick_side(first_steps, near_ref, other_ref, 1, key_half)
        grad_keys, grad_values = None, None
        for query_half in range(key_half, 2):
            queries = q_ref[query_half]
            grad = do[query_half]
            scores = dot_nt(keys, queries) * scale
            weights = jnp.exp(scores - lse_ref[query_half])
            if key_half == query_half:
                seen = visible_of(codes(kc_ref, key_half), qc_ref[query_half], key_half)
                weights = jnp.where(seen, weights, 0.0)
            grad_weights = dot_nt(values, grad)
            grad_scores = (weights * (grad_weights - delta[query_half])).astype(BF)
            value_term = dot_nn(weights.astype(BF), grad)
            key_term = dot_nn(grad_scores, queries)
            grad_keys = key_term if grad_keys is None else grad_keys + key_term
            grad_values = value_term if grad_values is None else grad_values + value_term
            acc[query_half] += dot_tn(keys, grad_scores)
        shape = (SEQ_STEP, half_rows, HD)
        results.append((grad_keys * scale).reshape(shape).astype(BF))
        results.append(grad_values.reshape(shape).astype(BF))

    def store(ref):
        for key_half in range(2):
            ref[:, 0, key_half] = results[2 * key_half]
            ref[:, 1, key_half] = results[2 * key_half + 1]

    pl.when(step < first_steps)(lambda: store(own_ref))
    pl.when(step >= first_steps)(lambda: store(sent_ref))

    @pl.when(step == pl.num_programs(0) - 1)
    def _():
        for half in range(2):
            dq_ref[half] = jnp.transpose(acc[half] * scale)


def attend_back(queries, grads, wide, near, other, key_code, query_code, log_total, others):
    _, rows, _ = queries.shape
    first_steps = near.shape[0] // SEQ_STEP
    sides = side_specs(near.shape, first_steps)
    return pl.pallas_call(
        functools.partial(attend_back_kernel, HD**-0.5, first_steps, len(others)),
        grid=(2 * first_steps,),
        in_specs=[fixed(queries.shape)]
        + [fixed(grad.shape) for grad in grads]
        + [fixed(wide.shape)]
        + sides
        + [code_spec(key_code.shape), fixed(query_code.shape), fixed(log_total.shape)]
        + [anywhere()] * len(others),
        out_specs=[fixed((2, rows, HD))] + sides,
        out_shape=[shape_of((2, rows, HD), F32), shape_of(near.shape), shape_of(near.shape)],
        scratch_shapes=[
            pltpu.VMEM((2, HD, rows), F32),
            pltpu.VMEM((2, rows, HD), BF),
            pltpu.VMEM((2, 1, rows), F32),
        ],
        compiler_params=params(60),
        cost_estimate=cost(5.2),
        name="attend_back",
    )(queries, *grads, wide, near, other, key_code, query_code, log_total, *others)


OUT_TILE = 256
FEED_TILE = 512


def feed_forward_kernel(own_ref, gain_ref, *refs):
    x_hbm = refs[0]
    cot_parts = refs[1:6]
    mixed_parts = refs[6:11]
    near_w, other_w, joined_w = refs[11:14]
    refs = refs[14:]
    normed_ref, hidden_ref, middle_ref, dg_ref, du_ref, cot_ref = refs[:6]
    dx_refs = refs[6:11]
    x_v, out_v, gate_v, up_v, down_v, mixed_v, normed_v, middle_v, dg_v, du_v, cot_v = refs[11:22]
    in_sem, cot_sem, out_sem, w_sem, s_sem = refs[22:]
    rows, width = x_v.shape
    units = gate_v.shape[1]
    tok_rows = hidden_ref.shape[0]
    half = tok_rows // 2
    blocks = rows // tok_rows
    chunks = cut(units, FEED_TILE)
    cols = mixed_parts[0].shape[1]

    def begin(source, target, sem):
        copy = pltpu.make_async_copy(source, target, sem)
        copy.start()
        return copy

    first = [begin(x_hbm, x_v, in_sem.at[0])]
    for t, part, low in (
        (0, mixed_parts[0], 0),
        (1, mixed_parts[1], 0),
        (2, mixed_parts[2], 0),
        (2, mixed_parts[3], blocks // 2),
        (3, mixed_parts[4], 0),
    ):
        for b in range(part.shape[0] // tok_rows):
            u = (low + b + t) % blocks
            first.append(
                begin(
                    part.at[pl.ds(b * tok_rows, tok_rows), :],
                    mixed_v.at[pl.ds(u * tok_rows, tok_rows), pl.ds(t * cols, cols)],
                    in_sem.at[len(first)],
                )
            )
    first += start_blocks(own_ref, near_w, other_w, out_v, out_sem)
    cots, step = [], cot_parts[2].shape[0]
    for part in cot_parts:
        for low in range(0, part.shape[0], step):
            i = len(cots)
            cots.append(
                begin(
                    part.at[pl.ds(low, half), :], cot_v.at[pl.ds(i * half, half), :], cot_sem.at[i]
                )
            )
    loads = [
        [
            begin(
                joined_w.at[:, pl.ds(j * units + at, size)], dst.at[:, pl.ds(at, size)], w_sem.at[i, j]
            )
            for j, dst in enumerate((gate_v, up_v, down_v))
        ]
        for i, (at, size) in enumerate(chunks)
    ]
    for copy in first:
        copy.wait()
    hidden = x_v[...].astype(F32) + dot_nt(mixed_v[...], out_v[...])
    hidden_ref[...] = hidden[:tok_rows]
    normed_v[...] = (hidden * inverse_norm(hidden) * gain_ref[...]).astype(BF)
    for copy in cots:
        copy.wait()
    stores = [begin(normed_v, normed_ref, s_sem.at[0]), begin(cot_v, cot_ref, s_sem.at[1])]
    for i, (at, size) in enumerate(chunks):
        for copy in loads[i]:
            copy.wait()
        here = slice(at, at + size)
        gate = dot_nn(normed_v[...], gate_v[:, here])
        up = dot_nn(normed_v[...], up_v[:, here])
        grad = dot_nn(cot_v[...], down_v[:, here])
        sig = 1.0 / (1.0 + jnp.exp(-gate))
        active = gate * sig
        middle_v[:, here] = (active * up).astype(BF)
        dg_v[:, here] = (grad * up * sig * (1.0 + gate * (1.0 - sig))).astype(BF)
        du_v[:, here] = (grad * active).astype(BF)
    for j, (src, dst) in enumerate(((dg_v, dg_ref), (du_v, du_ref), (middle_v, middle_ref))):
        stores.append(begin(src, dst, s_sem.at[2 + j]))
    for at, size in cut(width, OUT_TILE):
        here = slice(at, at + size)
        grad = dot_nt(dg_v[...], gate_v[here, :]) + dot_nt(du_v[...], up_v[here, :])
        store_rows(dx_refs, here, grad)
    for copy in stores:
        copy.wait()


def feed_forward(own, x, gain, cot_parts, mixed_parts, near, other, joined_all, tok_rows):
    rows, width = x.shape
    units = joined_all.shape[1] // 3
    blocks = rows // tok_rows
    hidden_like = shape_of((rows, units))
    return pl.pallas_call(
        feed_forward_kernel,
        in_specs=[smem(), vmem()] + [anywhere()] * 14,
        out_specs=[anywhere(), vmem()] + [anywhere()] * 4 + [vmem()] * 5,
        out_shape=[
            shape_of((rows, width)),
            shape_of((tok_rows, width), F32),
            hidden_like,
            hidden_like,
            hidden_like,
            shape_of((rows, width)),
            *row_shapes(tok_rows, width),
        ],
        scratch_shapes=[
            pltpu.VMEM((rows, width), BF),
            pltpu.VMEM((width, QD), BF),
            pltpu.VMEM((width, units), BF),
            pltpu.VMEM((width, units), BF),
            pltpu.VMEM((width, units), BF),
            pltpu.VMEM((rows, QD), BF),
            pltpu.VMEM((rows, width), BF),
            pltpu.VMEM((rows, units), BF),
            pltpu.VMEM((rows, units), BF),
            pltpu.VMEM((rows, units), BF),
            pltpu.VMEM((rows, width), BF),
            pltpu.SemaphoreType.DMA((1 + blocks * blocks,)),
            pltpu.SemaphoreType.DMA((2 * blocks,)),
            pltpu.SemaphoreType.DMA((2, near.shape[0])),
            pltpu.SemaphoreType.DMA((len(cut(units, FEED_TILE)), 3)),
            pltpu.SemaphoreType.DMA((5,)),
        ],
        compiler_params=params(60),
        cost_estimate=cost(16),
        name="feed_forward",
    )(own, gain, x, *cot_parts, *mixed_parts, near, other, joined_all)


def down_grads_kernel(blocks, own_ref, c_ref, down_w, middle_ref, down_ref, out_ref, turned, acc):
    step = pl.program_id(0)

    @pl.when(step == 0)
    def _():
        turned[...] = jnp.transpose(c_ref[...])
        acc[...] = jnp.zeros(acc.shape, F32)

    down_ref[...] = dot_nn(turned[...], middle_ref[...]).astype(BF)
    acc[...] += dot_nt(middle_ref[...], down_w[...])

    @pl.when(step == pl.num_programs(0) - 1)
    def _():
        rows = acc.shape[0] // blocks
        for t in range(blocks):
            at = pl.multiple_of(lax.rem(own_ref[0] + t, blocks) * rows, 16)
            out_ref[pl.ds(at, rows), :] = acc[t * rows : (t + 1) * rows, :].astype(BF)


def down_grads(own, cot, middle, joined_all, blocks):
    rows, full = cot.shape
    units = middle.shape[1]
    steps = units // TILE

    def tiles(rows, first=0):
        return pl.BlockSpec((rows, TILE), lambda i, own: (0, first + i))

    return pl.pallas_call(
        functools.partial(down_grads_kernel, blocks),
        grid_spec=pltpu.PrefetchScalarGridSpec(
            num_scalar_prefetch=1,
            grid=(steps,),
            in_specs=[fixed(cot.shape), tiles(full, 2 * steps), tiles(rows)],
            out_specs=[tiles(full), fixed((rows, full))],
            scratch_shapes=[pltpu.VMEM((full, rows), BF), pltpu.VMEM((rows, full), F32)],
        ),
        out_shape=[shape_of((full, units)), shape_of((rows, full))],
        compiler_params=params(60),
        cost_estimate=cost(6.3),
        name="down_grads",
    )(own, cot, joined_all, middle)


def pair_grads_kernel(orders, others, own_ref, *refs):
    xs, gates, ups = refs[:2], refs[2:4], refs[4:6]
    outs, (one, two, turned) = refs[6 + others : -3], refs[-3:]
    count = len(outs) // 2
    blocks = len(orders[0])
    rows = one.shape[0] // blocks
    tokens = xs[0].shape[0]

    @pl.when(pl.program_id(0) == 0)
    def _():
        for side, x_ref in enumerate(xs):
            turned[...] = jnp.transpose(x_ref[...])
            where = slice(side * tokens, (side + 1) * tokens)
            for j in range(blocks):
                here = slice(j * rows, (j + 1) * rows)
                for to, which in ((one, 0), (two, 1)):
                    at = pl.multiple_of((own_ref[0] ^ orders[which][j]) * rows, 16)
                    to[here, where] = turned[pl.ds(at, rows), :]

    for left, grads, (low, high, sent) in ((one, gates, outs[:count]), (two, ups, outs[count:])):
        result = dot_nn(left[:, :tokens], grads[0][...]) + dot_nn(left[:, tokens:], grads[1][...])
        half = 2 * low.shape[0]
        low[...] = result[: half // 2].astype(BF)
        high[...] = result[half // 2 : half].astype(BF)
        sent[...] = result[half:].astype(BF)


def pair_grads(own, orders, xs, gates, ups, others):
    rows, full = xs[0].shape
    units = gates[0].shape[1]

    def tiles(rows):
        return pl.BlockSpec((rows, TILE), lambda i, order: (0, i))

    return pl.pallas_call(
        functools.partial(pair_grads_kernel, orders, len(others)),
        grid_spec=pltpu.PrefetchScalarGridSpec(
            num_scalar_prefetch=1,
            grid=(units // TILE,),
            in_specs=[fixed(xs[0].shape)] * 2 + [tiles(rows)] * 4 + [anywhere()] * len(others),
            out_specs=([tiles(full // 8)] * 2 + [tiles(full // 4)]) * 2,
            scratch_shapes=[pltpu.VMEM((full // 2, 2 * rows), BF)] * 2
            + [pltpu.VMEM((full, rows), BF)],
        ),
        out_shape=([shape_of((full // 8, units))] * 2 + [shape_of((full // 4, units))]) * 2,
        compiler_params=params(60),
        cost_estimate=cost(6.3),
        name="pair_grads",
    )(own, *xs, *gates, *ups, *others)


def norm_back_kernel(others, own_ref, *refs):
    near_w, other_w = refs[6:8]
    refs = refs[:6] + refs[8 + others :]
    first_ref, down_ref, up_ref, hidden_ref, gain_ref, cot_ref, dh_ref, branch_ref = refs[:8]
    mixed_refs = refs[8:-3]
    gain_grad_ref, out_v, sem = refs[-3:]
    copies = start_blocks(own_ref, near_w, other_w, out_v, sem)
    grad = first_ref[...] + down_ref[...].astype(F32) + up_ref[...].astype(F32)
    hidden = hidden_ref[...]
    inv = inverse_norm(hidden)
    scaled = grad * gain_ref[...]
    gain_grad_ref[...] = jnp.sum(grad * (hidden * inv), axis=0, keepdims=True)
    inner = jnp.mean(scaled * hidden, axis=-1, keepdims=True)
    d_hidden = cot_ref[...].astype(F32) + inv * scaled - hidden * (inv * inv * inv * inner)
    dh_ref[...] = d_hidden
    branch_ref[...] = d_hidden.astype(BF)
    for copy in copies:
        copy.wait()
    d_mixed = dot_nn(branch_ref[...], out_v[...]).astype(BF)
    cols = mixed_refs[0].shape[1]
    for t, ref in enumerate(mixed_refs):
        ref[...] = d_mixed[:, t * cols : (t + 1) * cols]


def norm_back(own, first, down, up, hidden, gain, cotangent, near, other, blocks, others):
    rows, width = hidden.shape
    return pl.pallas_call(
        functools.partial(norm_back_kernel, len(others)),
        in_specs=[smem()] + [vmem()] * 6 + [anywhere()] * (2 + len(others)),
        out_specs=[vmem()] * (3 + blocks),
        out_shape=[shape_of((rows, width), F32), shape_of((rows, width))]
        + [shape_of((rows, QD // blocks))] * blocks
        + [shape_of((1, width), F32)],
        scratch_shapes=[
            pltpu.VMEM((width, QD), BF),
            pltpu.SemaphoreType.DMA((2, near.shape[0])),
        ],
        compiler_params=params(60),
        cost_estimate=cost(2.3),
        name="norm_back",
    )(own, first, down, up, hidden, gain, cotangent, near, other, *others)


def per_device(
    inputs,
    norm_gain_attn,
    qkv_weight,
    qkv_bias,
    out_weight,
    norm_gain_mlp,
    gate_weight,
    up_weight,
    down_weight,
    cotangent,
    segment_ids,
    positions,
):
    tok_rows = inputs.shape[0]
    width = inputs.shape[1]
    seq_dev = lax.axis_size("seq")
    heads_dev = lax.axis_size("head")
    heads_here = HEADS // heads_dev
    copies = heads_dev // KV_HEADS
    group_rows = heads_dev * tok_rows
    half_rows = group_rows // 2
    query_cols = heads_here * HD
    head_index = lax.axis_index("head")
    seq_index = lax.axis_index("seq")
    odd = head_index % 2 == 1
    seq_bits = bits_of("seq")
    head_bits = bits_of("head")
    far = seq_dev // 2
    bits_down = list(range(seq_bits - 1, 0, -1))
    bits_up = bits_down[::-1]
    orders = (masks_of(bits_down), masks_of(bits_up))
    seq_own = seq_index.astype(jnp.int32).reshape(1)
    head_own = head_index.astype(jnp.int32).reshape(1)

    units = gate_weight.shape[1]
    padded = -(-units // TILE) * TILE
    joined = jnp.concatenate(
        [
            jnp.pad(part, ((0, 0), (0, padded - units)))
            for part in (gate_weight, up_weight, down_weight.T)
        ],
        axis=1,
    )
    joined_all = plain(lax.all_gather(plain(joined), "seq", axis=0, tiled=True))


    gain_cols = norm_gain_attn.shape[0]
    bias_cols = qkv_bias.shape[0]
    cols_here = query_cols + 2 * HD
    small = jnp.concatenate(
        [
            norm_gain_attn,
            norm_gain_mlp,
            qkv_bias,
            (positions >> 7).astype(BF),
            (positions & 127).astype(BF),
            segment_ids.astype(BF),
        ]
    )
    small_row = jnp.pad(small[None], ((0, MORE_ROWS - 1), (0, cols_here - small.shape[0])))

    def head_columns(values, head):
        last = values.ndim - 1
        slot = head // copies
        return [
            lax.dynamic_slice_in_dim(values, head * query_cols, query_cols, last),
            lax.dynamic_slice_in_dim(values, QD + slot * HD, HD, last),
            lax.dynamic_slice_in_dim(values, QD + KD + slot * HD, HD, last),
        ]

    rows_of = []
    for apart in range(heads_dev):
        target = (head_index - apart) % heads_dev
        block = jnp.concatenate(head_columns(qkv_weight, target), axis=1)
        block = jnp.concatenate([block, small_row])
        rows_of.append(from_next(block, "head", apart) if apart else block)
    own_wide = qkv_weight.shape[0]
    own_rows = own_wide * heads_dev
    inputs_parts = gather_blocks(tie(inputs, *rows_of[1:]), "head")
    rows_of = roll_blocks(jnp.stack(rows_of), (heads_dev - head_index) % heads_dev)
    small_grp = rows_of[:, own_wide]
    cols_own = jnp.concatenate(
        [
            rows_of[:, :own_wide].reshape(own_rows, cols_here),
            jnp.pad(small_grp, ((0, 2 * MORE_ROWS - heads_dev), (0, 0))),
        ]
    )
    cols_near, _ = gather_far(plain(cols_own), "seq", inputs_parts[2:4])
    cols_other = swap(cols_near, "seq", 0)

    def cut_small(values):
        cuts, start = [], 0
        for size in (gain_cols, gain_cols, bias_cols, tok_rows, tok_rows, tok_rows):
            cuts.append(values[..., start : start + size])
            start += size
        return cuts

    def places(cuts):
        pos = (cuts[3].astype(jnp.int32) << 7) + cuts[4].astype(jnp.int32)
        pos = roll_blocks(pos, head_index, pos.ndim - 2)
        seg = roll_blocks(cuts[5].astype(jnp.int32), head_index, pos.ndim - 2)
        return pos, seg * SEG_STEP + pos

    small_all = jnp.concatenate(
        [part[:, own_rows : own_rows + heads_dev] for part in (cols_near, cols_other)]
    )
    cuts = cut_small(small_all)
    _, key_code = places(cuts)
    query_pos, query_code = places(cut_small(small_grp))
    query_pos = query_pos.reshape(-1)

    def in_order(values):
        masks = [seq_index ^ j for j in range(seq_dev)]
        return jnp.stack(
            [
                lax.dynamic_index_in_dim(values, (m & 1) * far + (m >> 1), 0, keepdims=False)
                for m in masks
            ]
        ).reshape(-1)

    gain_attn = in_order(cuts[0]).reshape(1, -1).astype(F32)
    gain_mlp = in_order(cuts[1]).reshape(1, -1).astype(F32)
    bias_all = in_order(cuts[2]).astype(F32)

    def halves_first(values):
        tail = values.shape[1:]
        return jnp.swapaxes(
            values.reshape((heads_dev, 2, tok_rows // 2) + tail), 0, 1
        ).reshape((2, half_rows) + tail)

    query_code = jnp.broadcast_to(
        halves_first(query_code.reshape(-1))[:, None, None, :], (2, 1, heads_here, half_rows)
    ).reshape(2, 1, heads_here * half_rows)
    key_code = jnp.swapaxes(
        key_code.reshape(seq_dev, heads_dev, 2, tok_rows // 2), 1, 2
    ).reshape(seq_dev, 2, half_rows, 1)
    freq_index = jnp.arange(HD // 2, dtype=F32) * 2.0 / HD
    angles = query_pos.astype(F32)[:, None] * (1.0 / ROPE_BASE**freq_index)[None, :]
    cosine, sine = jnp.cos(angles), jnp.sin(angles)
    cosine_part = jnp.concatenate([cosine, cosine], axis=1)
    sine_part = jnp.concatenate([-sine, sine], axis=1)

    bias_here = jnp.concatenate(head_columns(bias_all, head_index))[None]
    queries, kv_own, inputs_grp, normed_one, cols_weight = project(
        seq_own,
        inputs_parts,
        gain_attn,
        bias_here,
        cosine_part,
        sine_part,
        cols_near,
        cols_other,
        heads_here,
    )
    half = tok_rows // 2
    out_flat = out_weight.reshape(-1, width)
    out_half = out_flat.shape[0] // 2
    out_pad = -out_half % 16
    cot_mixed = jnp.concatenate(
        [
            part
            for i in range(2)
            for part in (
                cotangent[i * half : (i + 1) * half],
                jnp.pad(out_flat[i * out_half : (i + 1) * out_half], ((0, out_pad), (0, 0))),
            )
        ]
    )
    cot_late = tie(plain(cot_mixed), inputs_parts[2], inputs_parts[3])
    cot_parts = gather_blocks(cot_late, "head", [queries])
    kv_near, _ = gather_far(kv_own, "seq", cot_parts[2:4])
    kv_other = swap(kv_near, "seq", 0)

    halves = jnp.concatenate(cot_parts).reshape(2 * heads_dev, half + out_half + out_pad, width)
    out_rows = plain(halves[:, half : half + out_half].reshape(QD, -1).T)
    out_first = tie(out_rows, kv_other)
    mixed, mixed_wide, log_total = attend(
        queries, kv_near, kv_other, key_code, query_code, tok_rows, []
    )
    out_near, out_came = gather_far(out_first, "seq", [mixed])
    mixed_parts = gather_blocks(mixed, "head", out_came)
    out_other = swap(tie(out_near, mixed_parts[1], mixed_parts[4]), "seq", 0)

    normed_two, own_hidden, middle, d_gate, d_up, cot_grp, *d_two = feed_forward(
        seq_own,
        inputs_grp,
        gain_mlp,
        cot_parts,
        mixed_parts,
        out_near,
        out_other,
        joined_all,
        tok_rows,
    )

    others = [swap(part, "seq", 0) for part in (normed_two, d_gate, d_up)]
    down_term, out_term = down_grads(
        head_own, cot_grp, middle, joined_all, heads_dev
    )
    moved = sum_first(d_two[2:4], "head")
    down_late = tie(down_term, *moved)
    down_sum = plain(lax.psum_scatter(plain(down_late), "seq", scatter_dimension=0, tiled=True))
    down, up = sum_payload(d_two[1], d_two[4], moved, others)
    parts = [
        part.reshape(-1, width // seq_dev, part.shape[1])
        for part in pair_grads(
            seq_own,
            orders,
            (normed_two, others[0]),
            (d_gate, others[1]),
            (d_up, others[2]),
            [down, up, down_late],
        )
    ]
    gate_low, gate_high, *gate_sent = parts[: len(parts) // 2]
    up_low, up_high, *up_sent = parts[len(parts) // 2 :]
    d_hidden, d_branch, *d_mixed_own, grad_gain_two = norm_back(
        seq_own,
        d_two[0],
        from_next(down, "head"),
        to_next(up, "head"),
        own_hidden,
        gain_mlp,
        cotangent,
        out_near,
        out_other,
        heads_dev,
        [gate_low],
    )
    d_mixed = [d_mixed_own[0]]
    for apart in range(1, heads_dev):
        d_mixed.append(from_next(d_mixed_own[heads_dev - apart], "head", apart))

    def move(t, *earlier):
        return (
            swap(tie(gate_sent[t], *earlier), "seq", bits_down[0]),
            swap(tie(up_sent[t], *earlier), "seq", bits_up[0]),
        )

    moved = [move(t, d_branch) for t in range(len(gate_sent))]
    branch_above = from_next(tie(d_branch, *d_mixed[1:]), "head")
    branch_below = to_next(tie(d_branch, *d_mixed[1:]), "head")
    d_queries, d_kv_own, d_kv_sent = attend_back(
        queries,
        d_mixed,
        mixed_wide,
        kv_near,
        kv_other,
        key_code,
        query_code,
        log_total,
        [],
    )
    d_kv_moved = swap(tie(d_kv_sent, branch_above, branch_below), "seq", 0)
    branch_above = tie(branch_above, d_queries)
    branch_below = tie(branch_below, d_queries)
    branch_parts = [
        d_branch,
        branch_above,
        from_next(branch_above[:half], "head"),
        to_next(branch_below[half:], "head"),
        branch_below,
    ]
    d_kv_moved = tie(d_kv_moved, *moved[-1], branch_parts[2], branch_parts[3])
    out_late = tie(out_term, down_sum)
    out_sum = plain(lax.psum_scatter(plain(out_late), "head", scatter_dimension=0, tiled=True))
    output = (own_hidden + out_sum.astype(F32)).astype(BF)
    d_kv = total([d_kv_own, d_kv_moved])
    d_keys, keys_last = sum_xor([d_kv[i, 0] for i in range(far)], "seq", bits_down)
    d_values, values_last = sum_xor([d_kv[i, 1] for i in range(far)], "seq", bits_up)
    d_other_raw = jnp.where(odd, d_keys, d_values).astype(BF)
    d_other_raw = swap(
        tie(d_other_raw, down_sum), "head", 0
    )
    d_other = d_other_raw.reshape(2, heads_dev, tok_rows // 2, HD)
    d_other = roll_blocks(d_other, jnp.where(odd, 1, heads_dev - 1), 1).reshape(2, half_rows, HD)
    d_kv_total = jnp.where(odd, d_values, d_keys) + d_other.astype(F32)


    def second(low, high, which, bit):
        half = high.shape[0]
        parts = [tie(pair[which], keys_last, values_last) for pair in moved]
        sent = total([high, jnp.concatenate([part[half:] for part in parts], axis=2)]).astype(BF)
        come = swap(sent, "seq", bit)
        return [low, jnp.concatenate([part[:half] for part in parts], axis=2), come]

    gate_terms = second(gate_low, gate_high, 0, bits_down[1])
    up_terms = second(up_low, up_high, 1, bits_up[1])
    *d_one, cols_kept, cols_sent, outs_kept, outs_sent = project_back(
        seq_own,
        head_own,
        orders,
        d_queries,
        d_kv_total,
        cosine_part,
        sine_part,
        normed_one,
        inputs_grp,
        cols_weight,
        mixed,
        branch_parts,
        grad_gain_two,
    )
    gate_terms[-1] = tie(gate_terms[-1], d_one[0])
    up_terms[-1] = tie(up_terms[-1], d_one[0])
    moved = sum_first(tie_all(d_one[2:4], gate_terms[-1], up_terms[-1]), "head")
    cols_moved, outs_moved = swap(cols_sent, "seq", 0), swap(outs_sent, "seq", 0)
    down, up = sum_payload(d_one[1], d_one[4], moved, [cols_moved, outs_moved])
    cols_terms = sum_step([cols_kept, cols_moved], "seq", bits_down[0])
    outs_terms = sum_step([outs_kept, outs_moved], "seq", bits_up[0])
    down, up = from_next(down, "head"), to_next(up, "head")
    d_normed_one = total([d_one[0], tie(down, cols_terms[-1], outs_terms[-1]), up])
    grad_cols = sum_halving(cols_terms, "seq", bits_down[1:]).astype(BF)
    grad_outs = sum_halving(outs_terms, "seq", bits_up[1:])
    inputs_f = inputs.astype(F32)
    inv_one = inverse_norm(inputs_f)
    scaled = d_normed_one * gain_attn
    inner = jnp.mean(scaled * inputs_f, axis=-1, keepdims=True)
    grad_inputs = (d_hidden + inv_one * scaled - inputs_f * (inv_one**3 * inner)).astype(BF)

    grad_out = grad_outs.T
    cols_wide = query_cols + HD
    more_rows = jnp.broadcast_to(grad_cols[own_rows:], (heads_dev, MORE_ROWS, cols_wide))
    grad_blocks = jnp.concatenate(
        [grad_cols[:own_rows].reshape(heads_dev, own_wide, cols_wide), more_rows], axis=1
    )
    grad_qkv = jnp.zeros((own_wide, QKV), F32)
    small_parts = []
    for apart in range(heads_dev):
        source = (head_index + apart) % heads_dev
        target = (head_index - apart) % heads_dev
        block = lax.dynamic_index_in_dim(grad_blocks, target, 0, keepdims=False)
        if apart:
            block = from_next(block, "head", apart)
        small_parts.append(block[own_wide : own_wide + 2])
        block = block[:own_wide].astype(F32)
        kv_place = QD + source % 2 * KD + source // copies * HD
        grad_qkv = lax.dynamic_update_slice_in_dim(
            grad_qkv, block[:, :query_cols], source * query_cols, 1
        )
        grad_qkv = lax.dynamic_update_slice_in_dim(grad_qkv, block[:, query_cols:], kv_place, 1)
    small_grads = total(small_parts)

    def own_part(row, start, size):
        return lax.dynamic_slice(small_grads, (row, start + head_index * size), (1, size)).reshape(size)

    key_bias = (QD + KD) // (seq_dev * heads_dev)
    value_bias = KD // (seq_dev * heads_dev)

    gate_sum = sum_halving(gate_terms, "seq", bits_down[2:])
    up_sum = sum_halving(up_terms, "seq", bits_up[2:])

    return (
        output,
        grad_inputs,
        own_part(0, 0, gain_cols),
        grad_qkv,
        own_part(1, 0, key_bias),
        own_part(1, heads_dev * key_bias, value_bias),
        grad_out,
        own_part(0, heads_dev * gain_cols, gain_cols),
        gate_sum[:, :units],
        up_sum[:, :units],
        down_sum[:, :units].T.astype(F32),
    )


def solution(mesh):
    both = ("seq", "head")
    in_specs = (
        P(both, None),
        P(both),
        P(both, None),
        P(both),
        P("head", "seq"),
        P(both),
        P("seq", "head"),
        P("seq", "head"),
        P("head", "seq"),
        P(both, None),
        P(both),
        P(both),
    )
    out_specs = (
        P(both, None),
        P(both, None),
        P(both),
        P(both, None),
        P(both),
        P(both),
        P("head", "seq"),
        P(both),
        P("seq", "head"),
        P("seq", "head"),
        P("head", "seq"),
    )
    return jax.shard_map(
        per_device, mesh=mesh, in_specs=in_specs, out_specs=out_specs, check_vma=False
    )
```

```python
import functools
import math

import jax
import jax.numpy as jnp
from jax import lax
from jax.experimental import pallas as pl
from jax.experimental.layout import Layout, with_layout_constraint
from jax.experimental.pallas import tpu as pltpu
from jax.sharding import PartitionSpec as P

HEADS = 12
KV_HEADS = 2
HD = 128
QD = 1536
KD = 256
QKV = 2048


EPS = 1e-06
ROPE_BASE = 1000000.0
MASKED = -1e30
LOWEST = -1e29
SEG_STEP = 1 << 20
TILE = 768
MIB = 2**20

TUNE = dict(x1=10, x2=30, mx=10, c2=8, g0=25, g1=10, wm=10, ct=15, project=7, project_back=9, attend=16, attend_back=18, feed_forward=36, down_product=8, pair_grads=7, norm_back=5.5, payload=2)

BF = jnp.bfloat16
F32 = jnp.float32


def plain(values):
    return with_layout_constraint(values, Layout(major_to_minor=tuple(range(values.ndim))))


def bits_of(axis):
    return (lax.axis_size(axis) - 1).bit_length()


def bit_value(axis, bit):
    return (lax.axis_index(axis) >> bit) & 1


def send(block, axis, target):
    count = lax.axis_size(axis)
    return plain(lax.ppermute(plain(block), axis, [(j, target(j) % count) for j in range(count)]))


def swap(block, axis, bit):
    return send(block, axis, lambda j: j ^ (1 << bit))


def from_next(block, axis, apart=1):
    return send(block, axis, lambda j: j - apart)


def to_next(block, axis):
    return send(block, axis, lambda j: j + 1)


def tie_kernel(*refs):
    del refs


def tie_all(blocks, *others, micros=0):
    count = len(blocks)
    return pl.pallas_call(
        tie_kernel,
        in_specs=[pl.BlockSpec(memory_space=pl.ANY)] * (count + len(others)),
        out_specs=[pl.BlockSpec(memory_space=pl.ANY)] * count,
        out_shape=[jax.ShapeDtypeStruct(block.shape, block.dtype) for block in blocks],
        input_output_aliases={i: i for i in range(count)},
        compiler_params=pltpu.CompilerParams(
            vmem_limit_bytes=60 * MIB if max(block.size for block in blocks) > MIB else MIB
        ),
        cost_estimate=cost(micros),
        name="tie",
    )(*blocks, *others)


def tie(block, *others):
    return tie_all([block], *others)[0]


def gather_blocks(block, axis, last=(), micros=0):
    half = block.shape[0] // 2
    above = from_next(block, axis)
    below = to_next(block, axis)
    above, below = tie_all([above, below], *last, micros=micros)
    return [block, above, from_next(above[:half], axis), to_next(below[half:], axis), below]


def sum_first(far, axis):
    return from_next(far[0], axis), to_next(far[1], axis)


def payload_kernel(ahead_ref, behind_ref, above_ref, below_ref, *refs):
    down_ref, up_ref = refs[-2:]
    half = ahead_ref.shape[0] // 2
    down_ref[:half, :] = (behind_ref[:half, :].astype(F32) + above_ref[...].astype(F32)).astype(BF)
    down_ref[half:, :] = behind_ref[half:, :]
    up_ref[:half, :] = ahead_ref[:half, :]
    up_ref[half:, :] = (ahead_ref[half:, :].astype(F32) + below_ref[...].astype(F32)).astype(BF)


def sum_payload(ahead, behind, moved, others=()):
    return pl.pallas_call(
        payload_kernel,
        in_specs=[vmem()] * 4 + [anywhere()] * len(others),
        out_specs=[vmem()] * 2,
        out_shape=[shape_of(ahead.shape)] * 2,
        compiler_params=params(16),
        cost_estimate=cost(TUNE["payload"]),
        name="payload",
    )(ahead, behind, *moved, *others)


def far_first(block, axis):
    return swap(block, axis, 1), swap(block, axis, 2)


def far_last(block, first, axis, last=()):
    count = lax.axis_size(axis) // 2
    one, two = tie_all(first, *last)
    if count == 4:
        half = block.shape[0] // 2
        parts = [swap(one[:half], axis, 2), swap(two[half:], axis, 1)]
        blocks = [block, one, two, jnp.concatenate(parts)]
    else:
        more = [send(block, axis, lambda j: j ^ 2 * i) for i in range(3, count)]
        blocks, parts = [block, one, two, *more], [one]
    return plain(jnp.stack(blocks)), parts


def total(terms):
    result = terms[0].astype(F32)
    for term in terms[1:]:
        result = result + term.astype(F32)
    return result


def sum_step(terms, axis, bit, last=()):
    half = terms[0].shape[0] // 2
    sent = total([term[half:] for term in terms]).astype(BF)
    moved = swap(tie(sent, *last) if last else sent, axis, bit)
    return [term[:half] for term in terms] + [moved]


def sum_halving(terms, axis, bits):
    for bit in bits:
        terms = sum_step(terms, axis, bit)
    return total([term[0] for term in terms])


def sum_xor(blocks, axis, bits):
    blocks = dict(enumerate(blocks))
    for bit in bits:
        place = 1 << bit - 1
        sent = [m for m in sorted(blocks) if m & place]
        moved = swap(jnp.stack([blocks[m].astype(BF) for m in sent]), axis, bit)
        for i, m in enumerate(sent):
            blocks[m ^ place] = blocks[m ^ place] + moved[i].astype(F32)
            del blocks[m]
    return blocks[0], moved


def roll_blocks(stacked, shift, axis=0):
    count = stacked.shape[axis]
    return lax.dynamic_slice_in_dim(
        jnp.concatenate([stacked, stacked], axis=axis), shift, count, axis
    )


def dot_nn(left, right):
    return jnp.dot(left, right, preferred_element_type=F32)


def dot_nt(left, right):
    return lax.dot_general(left, right, (((1,), (1,)), ((), ())), preferred_element_type=F32)


def dot_tn(left, right):
    return lax.dot_general(left, right, (((0,), (0,)), ((), ())), preferred_element_type=F32)


def inverse_norm(values):
    return lax.rsqrt(jnp.mean(values * values, axis=-1, keepdims=True) + EPS)


def vmem():
    return pl.BlockSpec(memory_space=pltpu.VMEM)


def smem():
    return pl.BlockSpec(memory_space=pltpu.SMEM)


def anywhere():
    return pl.BlockSpec(memory_space=pl.ANY)


def shape_of(shape, dtype=BF):
    return jax.ShapeDtypeStruct(shape, dtype)


def fixed(shape):
    return pl.BlockSpec(shape, lambda *i: (0,) * len(shape))


def params(mib):
    return pltpu.CompilerParams(vmem_limit_bytes=mib * MIB)


def cost(micros):
    return pl.CostEstimate(flops=int(micros * 1153e6), bytes_accessed=0, transcendentals=0)


def cut(size, tile):
    return [(at, min(tile, size - at)) for at in range(0, size, tile)]


def start_blocks(own_ref, near_ref, other_ref, to_ref, sem):
    count = near_ref.shape[0]
    rows = to_ref.shape[0] // (2 * count)
    copies = []
    for side, source in enumerate((near_ref, other_ref)):
        for i in range(count):
            at = pl.multiple_of((own_ref[0] ^ (2 * i + side)) * rows, 16)
            copy = pltpu.make_async_copy(
                source.at[i, pl.ds(0, rows), :], to_ref.at[pl.ds(at, rows), :], sem.at[side, i]
            )
            copy.start()
            copies.append(copy)
    return copies


def masks_of(bits):
    masks = [0]
    for bit in bits[::-1]:
        masks += [mask | 1 << bit for mask in masks]
    return masks


def store_rows(refs, cols, values):
    at = 0
    for ref in refs:
        ref[:, cols] = values[at : at + ref.shape[0], :].astype(ref.dtype)
        at += ref.shape[0]


def row_shapes(tok_rows, width):
    half = tok_rows // 2
    return [shape_of((tok_rows, width), F32), shape_of((tok_rows, width))] + [
        shape_of((rows, width)) for rows in (half, half, tok_rows)
    ]


def fill_rows(to_ref, parts):
    size = parts[0].shape[0]
    at = 0
    for part, rows in zip(parts, (size, size, size // 2, size // 2, size)):
        to_ref[at : at + rows, :] = part[:rows, :]
        at += rows


def head_rows(tok_rows, blocks):
    half_block = tok_rows // 2
    return [
        (half, u * half_block, u * tok_rows + half * half_block, half_block)
        for u in range(blocks)
        for half in range(2)
    ]


def project_kernel(heads, own_ref, *refs):
    parts = refs[:5]
    gain_ref, bias_ref, cos_ref, sin_ref, near, other = refs[5:11]
    q_ref, kv_ref, x_ref, normed_ref, w_ref, sem = refs[11:]
    copies = start_blocks(own_ref, near, other, w_ref, sem)
    fill_rows(x_ref, parts)
    values = x_ref[...].astype(F32)
    normed_ref[...] = (values * inverse_norm(values) * gain_ref[...]).astype(BF)
    for copy in copies:
        copy.wait()
    joint = dot_nn(normed_ref[...], w_ref[...]) + bias_ref[...]
    tok_rows = parts[0].shape[0]
    blocks = x_ref.shape[0] // tok_rows
    half_rows = x_ref.shape[0] // 2
    for j in range(heads + 2):
        part = joint[:, j * HD : (j + 1) * HD]
        if j <= heads:
            part = part * cos_ref[...] + pltpu.roll(part, HD // 2, 1) * sin_ref[...]
        part = part.astype(BF)
        for half, low, row, count in head_rows(tok_rows, blocks):
            piece = part[row : row + count]
            if j < heads:
                q_ref[half, j * half_rows + low : j * half_rows + low + count, :] = piece
            else:
                kv_ref[j - heads, half, low : low + count, :] = piece


def project(own, parts, gain, bias, cos, sin, near, other, heads):
    width = parts[0].shape[1]
    rows = cos.shape[0]
    cols = near.shape[2]
    return pl.pallas_call(
        functools.partial(project_kernel, heads),
        in_specs=[smem()] + [vmem()] * 9 + [anywhere()] * 2,
        out_specs=[vmem()] * 5,
        out_shape=[
            shape_of((2, heads * rows // 2, HD)),
            shape_of((2, 2, rows // 2, HD)),
            shape_of((rows, width)),
            shape_of((rows, width)),
            shape_of((width, cols)),
        ],
        scratch_shapes=[pltpu.SemaphoreType.DMA((2, near.shape[0]))],
        compiler_params=params(60),
        cost_estimate=cost(TUNE["project"]),
        name="project",
    )(own, *parts, gain, bias, cos, sin, near, other)


def project_back_kernel(heads, orders, others, own_ref, head_ref, *refs):
    refs = refs[:14] + refs[14 + others :]
    dq_ref, dkv_ref, cos_ref, sin_ref, normed_ref, x_ref, w_ref, mixed_ref = refs[:8]
    parts = refs[8:13]
    gain_two_ref = refs[13]
    dn_refs = refs[14:19]
    cols_kept, outs_kept, wide_sent = refs[19:22]
    cols, branch, wide, wide_out, bias_v, small_v = refs[22:]
    rows = cos_ref.shape[0]
    half_rows = rows // 2
    tok_rows = parts[0].shape[0]
    blocks = rows // tok_rows
    head = head_ref[0]
    odd = (head & 1) == 1
    for half, low, row, count in head_rows(tok_rows, blocks):
        here = slice(row, row + count)
        for j in range(heads + 1):
            if j < heads:
                start = j * half_rows + low
                part = dq_ref[half, start : start + count, :]
            else:
                part = dkv_ref[half, low : low + count, :]
            part = part.astype(BF).astype(F32)
            turned = part * cos_ref[here, :] - pltpu.roll(part, HD // 2, 1) * sin_ref[here, :]
            if j == heads:
                turned = jnp.where(odd, part, turned)
            cols[here, j * HD : (j + 1) * HD] = turned.astype(BF)
    last = heads * HD
    bias = jnp.sum(cols[...].astype(F32), axis=0, keepdims=True)
    bias_v[...] = jnp.zeros(bias_v.shape, F32)
    bias_v[:, pl.ds(pl.multiple_of(head * last, HD), last)] = bias[:, :last]
    copies = (QD // last) // KV_HEADS
    slot = QD + (head & 1) * KD + (head // copies) * HD
    bias_v[:, pl.ds(pl.multiple_of(slot, HD), HD)] = bias[:, last:]
    key_w = jnp.where(odd, w_ref[:, last + HD :], w_ref[:, last : last + HD])
    grad = dot_nt(cols[:, :last], w_ref[:, :last]) + dot_nt(cols[:, last:], key_w)
    store_rows(dn_refs, slice(None), grad)
    values = x_ref[...].astype(F32)
    gain_one = jnp.sum(grad * (values * inverse_norm(values)), axis=0, keepdims=True)
    seq_dev = small_v.shape[0]
    small_v[...] = jnp.zeros(small_v.shape, BF)
    for row, vectors in enumerate(
        ((gain_one, gain_two_ref[...]), (bias_v[:, : QD + KD], bias_v[:, QD + KD :]))
    ):
        for i in range(seq_dev):
            at = 0
            for vector in vectors:
                size = vector.shape[1] // seq_dev
                small_v[i, row : row + 1, at : at + size] = vector[:, i * size : (i + 1) * size].astype(BF)
                at += size
    count = outs_kept.shape[1]
    fill_rows(branch, parts)
    wide[...] = dot_tn(normed_ref[...], cols[...]).astype(BF)
    wide_out[...] = dot_tn(branch[...], mixed_ref[...]).astype(BF)
    split = cols.shape[1]
    wide_sent[:, count:, split:] = jnp.zeros((wide_sent.shape[0], MORE_ROWS, wide_sent.shape[2] - split), BF)
    for i in range(cols_kept.shape[0]):
        for source, order, kept, lanes in (
            (wide, orders[0], cols_kept, slice(0, split)),
            (wide_out, orders[1], outs_kept, slice(split, wide_sent.shape[2])),
        ):
            for side in range(2):
                block = own_ref[0] ^ order[i] ^ side
                rows = source[pl.ds(pl.multiple_of(block * count, 16), count), :]
                if side == 0:
                    kept[i, :count] = rows
                else:
                    wide_sent[i, :count, lanes] = rows
                if source is wide:
                    small = small_v[block]
                    if side == 0:
                        kept[i, count:] = small
                    else:
                        wide_sent[i, count:, lanes] = small


MORE_ROWS = 16


def project_back(own, head, orders, dq, dkv, cos, sin, normed, x, w, mixed, parts, gain_two, others):
    rows, width = normed.shape
    heads = dq.shape[1] // (rows // 2)
    cols = (heads + 1) * HD
    tok_rows = parts[0].shape[0]
    far = len(orders[0])
    part_rows = width // (2 * far)
    return pl.pallas_call(
        functools.partial(project_back_kernel, heads, orders, len(others)),
        in_specs=[smem()] * 2 + [vmem()] * 14 + [anywhere()] * len(others),
        out_specs=[vmem()] * 8,
        out_shape=[
            *row_shapes(tok_rows, width),
            shape_of((far, part_rows + MORE_ROWS, cols)),
            shape_of((far, part_rows, heads * HD)),
            shape_of((far, part_rows + MORE_ROWS, cols + heads * HD)),
        ],
        scratch_shapes=[
            pltpu.VMEM((rows, cols), BF),
            pltpu.VMEM((rows, width), BF),
            pltpu.VMEM((width, cols), BF),
            pltpu.VMEM((width, heads * HD), BF),
            pltpu.VMEM((1, QKV), F32),
            pltpu.VMEM((2 * far, MORE_ROWS, cols), BF),
        ],
        compiler_params=params(60),
        cost_estimate=cost(TUNE["project_back"]),
        name="project_back",
    )(own, head, dq, dkv, cos, sin, normed, x, w, mixed, *parts, gain_two, *others)


def visible_of(key_code, query_code, half):
    seen = key_code <= query_code
    if half == 1:
        seen &= key_code >= (query_code & -SEG_STEP)
    return seen


PAIRS = ((0, 0), (0, 1), (1, 1))
SEQ_STEP = 4


def pick_side(first_steps, near_ref, other_ref, which, half):
    near = near_ref[:, which, half]
    other = other_ref[:, which, half]
    block = jnp.where(pl.program_id(0) < first_steps, near, other)
    return block.reshape(block.shape[0] * block.shape[1], block.shape[2])


def codes(code_ref, half):
    block = code_ref[:, half]
    return block.reshape(block.shape[0] * block.shape[1], 1)


def attend_kernel(scale, first_steps, tok_rows, q_ref, near_ref, other_ref, kc_ref, qc_ref, *refs):
    mixed_ref, wide_ref, lse_ref, top, total, acc = refs[-6:]
    step = pl.program_id(0)

    @pl.when(step == 0)
    def _():
        top[...] = jnp.full(top.shape, LOWEST, F32)
        total[...] = jnp.zeros(total.shape, F32)
        acc[...] = jnp.zeros(acc.shape, F32)

    for key_half, query_half in PAIRS:
        keys = pick_side(first_steps, near_ref, other_ref, 0, key_half)
        values = pick_side(first_steps, near_ref, other_ref, 1, key_half)
        scores = dot_nt(keys, q_ref[query_half])
        if key_half == query_half:
            seen = visible_of(codes(kc_ref, key_half), qc_ref[query_half], key_half)
            scores = jnp.where(seen, scores, MASKED)
        old = top[query_half]
        new = jnp.maximum(old, jnp.max(scores, axis=0, keepdims=True))
        weights = jnp.exp2((scores - new) * scale)
        factor = jnp.exp2((old - new) * scale)
        top[query_half] = new
        total[query_half] = total[query_half] * factor + jnp.sum(weights, axis=0, keepdims=True)
        acc[query_half] = acc[query_half] * factor + dot_tn(values, weights.astype(BF))

    @pl.when(step == pl.num_programs(0) - 1)
    def _():
        blocks = mixed_ref.shape[0] // tok_rows
        half_rows = mixed_ref.shape[0] // 2
        for half in range(2):
            wide_ref[half] = jnp.transpose(acc[half] / total[half])
            lse_ref[half] = top[half] * scale + jnp.log2(total[half])
        for half, low, row, count in head_rows(tok_rows, blocks):
            for j in range(mixed_ref.shape[1] // HD):
                at = j * half_rows + low
                mixed_ref[row : row + count, j * HD : (j + 1) * HD] = wide_ref[
                    half, at : at + count, :
                ].astype(BF)


def side_specs(shape, first_steps):
    block = (SEQ_STEP,) + shape[1:]
    rest = (0,) * (len(shape) - 1)
    return [
        pl.BlockSpec(block, lambda i: (jnp.minimum(i, first_steps - 1),) + rest),
        pl.BlockSpec(block, lambda i: (jnp.maximum(i - first_steps, 0),) + rest),
    ]


def code_spec(shape):
    return pl.BlockSpec((SEQ_STEP,) + shape[1:], lambda i: (i,) + (0,) * (len(shape) - 1))


def attend(queries, near, other, key_code, query_code, tok_rows, others):
    _, rows, _ = queries.shape
    half_rows = near.shape[3]
    heads = rows // half_rows
    first_steps = near.shape[0] // SEQ_STEP
    return pl.pallas_call(
        functools.partial(attend_kernel, HD**-0.5 * math.log2(math.e), first_steps, tok_rows),
        grid=(2 * first_steps,),
        in_specs=[fixed(queries.shape)]
        + side_specs(near.shape, first_steps)
        + [code_spec(key_code.shape), fixed(query_code.shape)]
        + [anywhere()] * len(others),
        out_specs=[fixed((2 * half_rows, heads * HD)), fixed((2, rows, HD)), fixed((2, 1, rows))],
        out_shape=[
            shape_of((2 * half_rows, heads * HD)),
            shape_of((2, rows, HD), F32),
            shape_of((2, 1, rows), F32),
        ],
        scratch_shapes=[
            pltpu.VMEM((2, 1, rows), F32),
            pltpu.VMEM((2, 1, rows), F32),
            pltpu.VMEM((2, HD, rows), F32),
        ],
        compiler_params=params(60),
        cost_estimate=cost(TUNE["attend"]),
        name="attend",
    )(queries, near, other, key_code, query_code, *others)


def attend_back_kernel(scale, first_steps, others, q_ref, *refs):
    grads = refs[:4]
    wide_ref, near_ref, other_ref, kc_ref, qc_ref, lse_ref = refs[4:10]
    dq_ref, own_ref, sent_ref, acc, do, delta = refs[10 + others :]
    step = pl.program_id(0)
    half_rows = near_ref.shape[3]
    tok_rows = grads[0].shape[0]

    @pl.when(step == 0)
    def _():
        acc[...] = jnp.zeros(acc.shape, F32)
        for u, grad in enumerate(grads):
            for half, low, row, count in head_rows(tok_rows, 1):
                for j in range(grad.shape[1] // HD):
                    at = j * half_rows + u * (tok_rows // 2)
                    do[half, at : at + count, :] = grad[row : row + count, j * HD : (j + 1) * HD]
        for half in range(2):
            product = do[half].astype(F32) * wide_ref[half]
            delta[half] = jnp.sum(jnp.transpose(product), axis=0, keepdims=True)

    results = []
    for key_half in range(2):
        keys = pick_side(first_steps, near_ref, other_ref, 0, key_half)
        values = pick_side(first_steps, near_ref, other_ref, 1, key_half)
        grad_keys, grad_values = None, None
        for query_half in range(key_half, 2):
            queries = q_ref[query_half]
            grad = do[query_half]
            scores = dot_nt(keys, queries) * (scale * math.log2(math.e))
            weights = jnp.exp2(scores - lse_ref[query_half])
            if key_half == query_half:
                seen = visible_of(codes(kc_ref, key_half), qc_ref[query_half], key_half)
                weights = jnp.where(seen, weights, 0.0)
            grad_weights = dot_nt(values, grad)
            grad_scores = (weights * (grad_weights - delta[query_half])).astype(BF)
            value_term = dot_nn(weights.astype(BF), grad)
            key_term = dot_nn(grad_scores, queries)
            grad_keys = key_term if grad_keys is None else grad_keys + key_term
            grad_values = value_term if grad_values is None else grad_values + value_term
            acc[query_half] += dot_tn(keys, grad_scores)
        shape = (SEQ_STEP, half_rows, HD)
        results.append((grad_keys * scale).reshape(shape).astype(BF))
        results.append(grad_values.reshape(shape).astype(BF))

    def store(ref):
        for key_half in range(2):
            ref[:, 0, key_half] = results[2 * key_half]
            ref[:, 1, key_half] = results[2 * key_half + 1]

    pl.when(step < first_steps)(lambda: store(own_ref))
    pl.when(step >= first_steps)(lambda: store(sent_ref))

    @pl.when(step == pl.num_programs(0) - 1)
    def _():
        for half in range(2):
            dq_ref[half] = jnp.transpose(acc[half] * scale)


def attend_back(queries, grads, wide, near, other, key_code, query_code, log_total, others):
    _, rows, _ = queries.shape
    first_steps = near.shape[0] // SEQ_STEP
    sides = side_specs(near.shape, first_steps)
    return pl.pallas_call(
        functools.partial(attend_back_kernel, HD**-0.5, first_steps, len(others)),
        grid=(2 * first_steps,),
        in_specs=[fixed(queries.shape)]
        + [fixed(grad.shape) for grad in grads]
        + [fixed(wide.shape)]
        + sides
        + [code_spec(key_code.shape), fixed(query_code.shape), fixed(log_total.shape)]
        + [anywhere()] * len(others),
        out_specs=[fixed((2, rows, HD))] + sides,
        out_shape=[shape_of((2, rows, HD), F32), shape_of(near.shape), shape_of(near.shape)],
        scratch_shapes=[
            pltpu.VMEM((2, HD, rows), F32),
            pltpu.VMEM((2, rows, HD), BF),
            pltpu.VMEM((2, 1, rows), F32),
        ],
        compiler_params=params(60),
        cost_estimate=cost(TUNE["attend_back"]),
        name="attend_back",
    )(queries, *grads, wide, near, other, key_code, query_code, log_total, *others)


OUT_TILE = 256
FEED_TILE = 512


def feed_forward_kernel(own_ref, gain_ref, *refs):
    x_hbm = refs[0]
    cot_parts = refs[1:6]
    mixed_parts = refs[6:11]
    near_w, other_w, joined_w = refs[11:14]
    refs = refs[14:]
    acts_ref, hidden_ref, middle_ref, cot_ref = refs[:4]
    dx_refs = refs[4:9]
    x_v, out_v, gate_v, up_v, down_v, mixed_v, normed_v, middle_v, dg_v, du_v, cot_v = refs[9:20]
    in_sem, cot_sem, out_sem, w_sem, s_sem = refs[20:]
    rows, width = x_v.shape
    units = gate_v.shape[1]
    tok_rows = hidden_ref.shape[0]
    half = tok_rows // 2
    blocks = rows // tok_rows
    chunks = cut(units, FEED_TILE)
    cols = mixed_parts[0].shape[1]

    def begin(source, target, sem):
        copy = pltpu.make_async_copy(source, target, sem)
        copy.start()
        return copy

    first = [begin(x_hbm, x_v, in_sem.at[0])]
    for t, part, low in (
        (0, mixed_parts[0], 0),
        (1, mixed_parts[1], 0),
        (2, mixed_parts[2], 0),
        (2, mixed_parts[3], blocks // 2),
        (3, mixed_parts[4], 0),
    ):
        for b in range(part.shape[0] // tok_rows):
            u = (low + b + t) % blocks
            first.append(
                begin(
                    part.at[pl.ds(b * tok_rows, tok_rows), :],
                    mixed_v.at[pl.ds(u * tok_rows, tok_rows), pl.ds(t * cols, cols)],
                    in_sem.at[len(first)],
                )
            )
    first += start_blocks(own_ref, near_w, other_w, out_v, out_sem)
    cots, step = [], cot_parts[2].shape[0]
    for part in cot_parts:
        for low in range(0, part.shape[0], step):
            i = len(cots)
            cots.append(
                begin(
                    part.at[pl.ds(low, half), :], cot_v.at[pl.ds(i * half, half), :], cot_sem.at[i]
                )
            )
    for copy in first:
        copy.wait()
    loads = [
        [
            begin(
                joined_w.at[:, pl.ds(j * units + at, size)], dst.at[:, pl.ds(at, size)], w_sem.at[i, j]
            )
            for j, dst in enumerate((gate_v, up_v, down_v))
        ]
        for i, (at, size) in enumerate(chunks)
    ]
    hidden = x_v[...].astype(F32) + dot_nt(mixed_v[...], out_v[...])
    hidden_ref[...] = hidden[:tok_rows]
    normed_v[...] = (hidden * inverse_norm(hidden) * gain_ref[...]).astype(BF)
    for copy in cots:
        copy.wait()
    normed_to = acts_ref.at[:, pl.ds(2 * units, width)]
    stores = [begin(normed_v, normed_to, s_sem.at[0]), begin(cot_v, cot_ref, s_sem.at[1])]
    for i, (at, size) in enumerate(chunks):
        for copy in loads[i]:
            copy.wait()
        here = slice(at, at + size)
        gate = dot_nn(normed_v[...], gate_v[:, here])
        up = dot_nn(normed_v[...], up_v[:, here])
        grad = dot_nn(cot_v[...], down_v[:, here])
        sig = 1.0 / (1.0 + jnp.exp(-gate))
        active = gate * sig
        middle_v[:, here] = (active * up).astype(BF)
        dg_v[:, here] = (grad * up * sig * (1.0 + gate * (1.0 - sig))).astype(BF)
        du_v[:, here] = (grad * active).astype(BF)
    for j, (src, dst) in enumerate(
        (
            (dg_v, acts_ref.at[:, pl.ds(0, units)]),
            (du_v, acts_ref.at[:, pl.ds(units, units)]),
            (middle_v, middle_ref),
        )
    ):
        stores.append(begin(src, dst, s_sem.at[2 + j]))
    for at, size in cut(width, OUT_TILE):
        here = slice(at, at + size)
        grad = dot_nt(dg_v[...], gate_v[here, :]) + dot_nt(du_v[...], up_v[here, :])
        store_rows(dx_refs, here, grad)
    for copy in stores:
        copy.wait()


def feed_forward(own, x, gain, cot_parts, mixed_parts, near, other, joined_all, tok_rows):
    rows, width = x.shape
    units = joined_all.shape[1] // 3
    blocks = rows // tok_rows
    return pl.pallas_call(
        feed_forward_kernel,
        in_specs=[smem(), vmem()] + [anywhere()] * 14,
        out_specs=[anywhere(), vmem()] + [anywhere()] * 2 + [vmem()] * 5,
        out_shape=[
            shape_of((rows, 2 * units + width)),
            shape_of((tok_rows, width), F32),
            shape_of((rows, units)),
            shape_of((rows, width)),
            *row_shapes(tok_rows, width),
        ],
        scratch_shapes=[
            pltpu.VMEM((rows, width), BF),
            pltpu.VMEM((width, QD), BF),
            pltpu.VMEM((width, units), BF),
            pltpu.VMEM((width, units), BF),
            pltpu.VMEM((width, units), BF),
            pltpu.VMEM((rows, QD), BF),
            pltpu.VMEM((rows, width), BF),
            pltpu.VMEM((rows, units), BF),
            pltpu.VMEM((rows, units), BF),
            pltpu.VMEM((rows, units), BF),
            pltpu.VMEM((rows, width), BF),
            pltpu.SemaphoreType.DMA((1 + blocks * blocks,)),
            pltpu.SemaphoreType.DMA((2 * blocks,)),
            pltpu.SemaphoreType.DMA((2, near.shape[0])),
            pltpu.SemaphoreType.DMA((len(cut(units, FEED_TILE)), 3)),
            pltpu.SemaphoreType.DMA((5,)),
        ],
        compiler_params=params(60),
        cost_estimate=cost(TUNE["feed_forward"]),
        name="feed_forward",
    )(own, gain, x, *cot_parts, *mixed_parts, near, other, joined_all)


def down_product_kernel(down_w, middle_ref, *refs):
    acc = refs[-1]
    step = pl.program_id(0)

    @pl.when(step == 0)
    def _():
        acc[...] = jnp.zeros(acc.shape, F32)

    acc[...] += dot_nt(middle_ref[...], down_w[...])

    @pl.when(step == pl.num_programs(0) - 1)
    def _():
        store_rows(refs[:-1], slice(None), acc)


def down_product(middle, joined_all, tok_rows):
    rows, units = middle.shape
    full = joined_all.shape[0]
    steps = units // TILE
    outs = row_shapes(tok_rows, full)
    return pl.pallas_call(
        down_product_kernel,
        grid=(steps,),
        in_specs=[
            pl.BlockSpec((full, TILE), lambda i: (0, 2 * steps + i)),
            pl.BlockSpec((rows, TILE), lambda i: (0, i)),
        ],
        out_specs=[fixed(out.shape) for out in outs],
        out_shape=outs,
        scratch_shapes=[pltpu.VMEM((rows, full), F32)],
        compiler_params=params(60),
        cost_estimate=cost(TUNE["down_product"]),
        name="down_product",
    )(joined_all, middle)


def pair_grads_kernel(orders, others, own_ref, *refs):
    xs, gates, ups = refs[:6:3], refs[1:6:3], refs[2:6:3]
    cot_ref, middle_ref = refs[6:8]
    *outs, down_ref = refs[8 + others : -4]
    one, two, turned, cot_t = refs[-4:]
    count = len(outs) // 2
    blocks = len(orders[0])
    rows = one.shape[0] // blocks
    tokens = xs[0].shape[0]

    @pl.when(pl.program_id(0) == 0)
    def _():
        cot_t[...] = jnp.transpose(cot_ref[...])
        for side, x_ref in enumerate(xs):
            turned[...] = jnp.transpose(x_ref[...])
            where = slice(side * tokens, (side + 1) * tokens)
            for j in range(blocks):
                here = slice(j * rows, (j + 1) * rows)
                for to, which in ((one, 0), (two, 1)):
                    at = pl.multiple_of((own_ref[0] ^ orders[which][j]) * rows, 16)
                    to[here, where] = turned[pl.ds(at, rows), :]

    for left, grads, quarters in ((one, gates, outs[:count]), (two, ups, outs[count:])):
        result = dot_nn(left[:, :tokens], grads[0][...]) + dot_nn(left[:, tokens:], grads[1][...])
        store_rows(quarters, slice(None), result)
    down_ref[...] = dot_nn(cot_t[...], middle_ref[...]).astype(BF)


def pair_grads(own, orders, acts, cot, middle, others):
    rows, width = cot.shape
    full = width
    units = (acts[0].shape[1] - width) // 2
    steps = units // TILE

    def tiles(rows, first=0):
        return pl.BlockSpec((rows, TILE), lambda i, own: (0, first + i))

    one_side = [
        pl.BlockSpec((rows, width), lambda i, own: (0, 2 * units // width)),
        tiles(rows),
        tiles(rows, steps),
    ]
    return pl.pallas_call(
        functools.partial(pair_grads_kernel, orders, len(others)),
        grid_spec=pltpu.PrefetchScalarGridSpec(
            num_scalar_prefetch=1,
            grid=(steps,),
            in_specs=one_side * 2 + [fixed(cot.shape), tiles(rows)] + [anywhere()] * len(others),
            out_specs=[tiles(full // 8)] * 8 + [tiles(full)],
            scratch_shapes=[pltpu.VMEM((full // 2, 2 * rows), BF)] * 2
            + [pltpu.VMEM((full, rows), BF)] * 2,
        ),
        out_shape=[shape_of((full // 8, units))] * 8 + [shape_of((full, units))],
        compiler_params=params(60),
        cost_estimate=cost(TUNE["pair_grads"]),
        name="pair_grads",
    )(own, *[side for side in acts for _ in range(3)], cot, middle, *others)


def norm_back_kernel(others, own_ref, *refs):
    near_w, other_w = refs[6:8]
    refs = refs[:6] + refs[8 + others :]
    first_ref, down_ref, up_ref, hidden_ref, gain_ref, cot_ref, dh_ref, branch_ref = refs[:8]
    mixed_refs = refs[8:-3]
    gain_grad_ref, out_v, sem = refs[-3:]
    copies = start_blocks(own_ref, near_w, other_w, out_v, sem)
    grad = first_ref[...] + down_ref[...].astype(F32) + up_ref[...].astype(F32)
    hidden = hidden_ref[...]
    inv = inverse_norm(hidden)
    scaled = grad * gain_ref[...]
    gain_grad_ref[...] = jnp.sum(grad * (hidden * inv), axis=0, keepdims=True)
    inner = jnp.mean(scaled * hidden, axis=-1, keepdims=True)
    d_hidden = cot_ref[...].astype(F32) + inv * scaled - hidden * (inv * inv * inv * inner)
    dh_ref[...] = d_hidden
    branch_ref[...] = d_hidden.astype(BF)
    for copy in copies:
        copy.wait()
    d_mixed = dot_nn(branch_ref[...], out_v[...]).astype(BF)
    cols = mixed_refs[0].shape[1]
    for t, ref in enumerate(mixed_refs):
        ref[...] = d_mixed[:, t * cols : (t + 1) * cols]


def norm_back(own, first, down, up, hidden, gain, cotangent, near, other, blocks, others):
    rows, width = hidden.shape
    return pl.pallas_call(
        functools.partial(norm_back_kernel, len(others)),
        in_specs=[smem()] + [vmem()] * 6 + [anywhere()] * (2 + len(others)),
        out_specs=[vmem()] * (3 + blocks),
        out_shape=[shape_of((rows, width), F32), shape_of((rows, width))]
        + [shape_of((rows, QD // blocks))] * blocks
        + [shape_of((1, width), F32)],
        scratch_shapes=[
            pltpu.VMEM((width, QD), BF),
            pltpu.SemaphoreType.DMA((2, near.shape[0])),
        ],
        compiler_params=params(60),
        cost_estimate=cost(TUNE["norm_back"]),
        name="norm_back",
    )(own, first, down, up, hidden, gain, cotangent, near, other, *others)


def per_device(
    inputs,
    norm_gain_attn,
    qkv_weight,
    qkv_bias,
    out_weight,
    norm_gain_mlp,
    gate_weight,
    up_weight,
    down_weight,
    cotangent,
    segment_ids,
    positions,
):
    tok_rows = inputs.shape[0]
    width = inputs.shape[1]
    seq_dev = lax.axis_size("seq")
    heads_dev = lax.axis_size("head")
    heads_here = HEADS // heads_dev
    copies = heads_dev // KV_HEADS
    group_rows = heads_dev * tok_rows
    half_rows = group_rows // 2
    query_cols = heads_here * HD
    head_index = lax.axis_index("head")
    seq_index = lax.axis_index("seq")
    odd = head_index % 2 == 1
    seq_bits = bits_of("seq")
    head_bits = bits_of("head")
    far = seq_dev // 2
    bits_down = list(range(seq_bits - 1, 0, -1))
    bits_up = bits_down[::-1]
    orders = (masks_of(bits_down), masks_of(bits_up))
    seq_own = seq_index.astype(jnp.int32).reshape(1)
    head_own = head_index.astype(jnp.int32).reshape(1)

    units = gate_weight.shape[1]
    padded = -(-units // TILE) * TILE
    joined = jnp.concatenate(
        [
            jnp.pad(part, ((0, 0), (0, padded - units)))
            for part in (gate_weight, up_weight, down_weight.T)
        ],
        axis=1,
    )
    joined_all = plain(lax.all_gather(plain(joined), "seq", axis=0, tiled=True))


    gain_cols = norm_gain_attn.shape[0]
    bias_cols = qkv_bias.shape[0]
    cols_here = query_cols + 2 * HD
    small = jnp.concatenate(
        [
            norm_gain_attn,
            norm_gain_mlp,
            qkv_bias,
            (positions >> 7).astype(BF),
            (positions & 127).astype(BF),
            segment_ids.astype(BF),
        ]
    )
    small_row = jnp.pad(small[None], ((0, MORE_ROWS - 1), (0, cols_here - small.shape[0])))

    def head_columns(values, head):
        last = values.ndim - 1
        slot = head // copies
        return [
            lax.dynamic_slice_in_dim(values, head * query_cols, query_cols, last),
            lax.dynamic_slice_in_dim(values, QD + slot * HD, HD, last),
            lax.dynamic_slice_in_dim(values, QD + KD + slot * HD, HD, last),
        ]

    rows_of = []
    for apart in range(heads_dev):
        target = (head_index - apart) % heads_dev
        block = jnp.concatenate(head_columns(qkv_weight, target), axis=1)
        block = jnp.concatenate([block, small_row])
        rows_of.append(from_next(block, "head", apart) if apart else block)
    own_wide = qkv_weight.shape[0]
    own_rows = own_wide * heads_dev
    inputs_parts = gather_blocks(tie(inputs, *rows_of[1:]), "head", micros=TUNE["x1"])
    rows_of = roll_blocks(jnp.stack(rows_of), (heads_dev - head_index) % heads_dev)
    small_grp = rows_of[:, own_wide]
    cols_own = jnp.concatenate(
        [
            rows_of[:, :own_wide].reshape(own_rows, cols_here),
            jnp.pad(small_grp, ((0, 2 * MORE_ROWS - heads_dev), (0, 0))),
        ]
    )
    cols_own = plain(cols_own)
    cols_near, _ = far_last(cols_own, far_first(cols_own, "seq"), "seq")
    inputs_parts[2:4] = tie_all(inputs_parts[2:4], micros=TUNE["x2"])
    cols_other = swap(tie(cols_near, *inputs_parts[2:4]), "seq", 0)

    def cut_small(values):
        cuts, start = [], 0
        for size in (gain_cols, gain_cols, bias_cols, tok_rows, tok_rows, tok_rows):
            cuts.append(values[..., start : start + size])
            start += size
        return cuts

    def places(cuts):
        pos = (cuts[3].astype(jnp.int32) << 7) + cuts[4].astype(jnp.int32)
        pos = roll_blocks(pos, head_index, pos.ndim - 2)
        seg = roll_blocks(cuts[5].astype(jnp.int32), head_index, pos.ndim - 2)
        return pos, seg * SEG_STEP + pos

    small_all = jnp.concatenate(
        [part[:, own_rows : own_rows + heads_dev] for part in (cols_near, cols_other)]
    )
    cuts = cut_small(small_all)
    _, key_code = places(cuts)
    query_pos, query_code = places(cut_small(small_grp))
    query_pos = query_pos.reshape(-1)

    def in_order(values):
        masks = [seq_index ^ j for j in range(seq_dev)]
        return jnp.stack(
            [
                lax.dynamic_index_in_dim(values, (m & 1) * far + (m >> 1), 0, keepdims=False)
                for m in masks
            ]
        ).reshape(-1)

    gain_attn = in_order(cuts[0]).reshape(1, -1).astype(F32)
    gain_mlp = in_order(cuts[1]).reshape(1, -1).astype(F32)
    bias_all = in_order(cuts[2]).astype(F32)

    def halves_first(values):
        tail = values.shape[1:]
        return jnp.swapaxes(
            values.reshape((heads_dev, 2, tok_rows // 2) + tail), 0, 1
        ).reshape((2, half_rows) + tail)

    query_code = jnp.broadcast_to(
        halves_first(query_code.reshape(-1))[:, None, None, :], (2, 1, heads_here, half_rows)
    ).reshape(2, 1, heads_here * half_rows)
    key_code = jnp.swapaxes(
        key_code.reshape(seq_dev, heads_dev, 2, tok_rows // 2), 1, 2
    ).reshape(seq_dev, 2, half_rows, 1)
    freq_index = jnp.arange(HD // 2, dtype=F32) * 2.0 / HD
    angles = query_pos.astype(F32)[:, None] * (1.0 / ROPE_BASE**freq_index)[None, :]
    cosine, sine = jnp.cos(angles), jnp.sin(angles)
    cosine_part = jnp.concatenate([cosine, cosine], axis=1)
    sine_part = jnp.concatenate([-sine, sine], axis=1)

    bias_here = jnp.concatenate(head_columns(bias_all, head_index))[None]
    queries, kv_own, inputs_grp, normed_one, cols_weight = project(
        seq_own,
        inputs_parts,
        gain_attn,
        bias_here,
        cosine_part,
        sine_part,
        cols_near,
        cols_other,
        heads_here,
    )
    half = tok_rows // 2
    out_flat = out_weight.reshape(-1, width)
    out_half = out_flat.shape[0] // 2
    out_pad = -out_half % 16
    cot_mixed = jnp.concatenate(
        [
            part
            for i in range(2)
            for part in (
                cotangent[i * half : (i + 1) * half],
                jnp.pad(out_flat[i * out_half : (i + 1) * out_half], ((0, out_pad), (0, 0))),
            )
        ]
    )
    cot_late = tie(plain(cot_mixed), inputs_parts[2], inputs_parts[3])
    kv_first = far_first(kv_own, "seq")
    cot_parts = gather_blocks(cot_late, "head", kv_first)
    kv_near, _ = far_last(kv_own, kv_first, "seq")
    cot_parts[2:4] = tie_all(cot_parts[2:4], micros=TUNE["c2"])
    kv_other = swap(kv_near, "seq", 0)

    mixed, mixed_wide, log_total = attend(
        queries, kv_near, kv_other, key_code, query_code, tok_rows, cot_parts[2:4]
    )
    late = tie_all([cot_mixed, *cot_parts[1:]], mixed)
    halves = jnp.concatenate(late).reshape(2 * heads_dev, half + out_half + out_pad, width)
    out_rows = plain(halves[:, half : half + out_half].reshape(QD, -1).T)
    out_first = far_first(out_rows, "seq")
    mixed_parts = gather_blocks(mixed, "head", micros=TUNE["mx"])
    out_near, _ = far_last(out_rows, out_first, "seq", [mixed_parts[1], mixed_parts[4]])
    out_other = swap(tie(out_near, *mixed_parts[2:4]), "seq", 0)

    acts, own_hidden, middle, cot_grp, *d_two = feed_forward(
        seq_own,
        inputs_grp,
        gain_mlp,
        cot_parts,
        mixed_parts,
        out_near,
        out_other,
        joined_all,
        tok_rows,
    )

    acts_moved = swap(acts, "seq", 0)
    moved = sum_first(d_two[2:4], "head")
    out_term = down_product(middle, joined_all, tok_rows)
    down, up = sum_payload(d_two[1], d_two[4], moved, others=[out_term[0]])
    *parts, down_term = pair_grads(seq_own, orders, (acts, acts_moved), cot_grp, middle, [down, up])
    parts = [part.reshape(-1, width // seq_dev, padded) for part in parts]
    gate_low, gate_high, *gate_sent = parts[:4]
    up_low, up_high, *up_sent = parts[4:]
    d_hidden, d_branch, *d_mixed_own, grad_gain_two = norm_back(
        seq_own,
        d_two[0],
        from_next(down, "head"),
        to_next(up, "head"),
        own_hidden,
        gain_mlp,
        cotangent,
        out_near,
        out_other,
        heads_dev,
        [gate_low],
    )
    d_mixed = [d_mixed_own[0]]
    for apart in range(1, heads_dev):
        d_mixed.append(from_next(d_mixed_own[heads_dev - apart], "head", apart))

    gate_moved = [swap(gate_sent[1], "seq", bits_down[0])]
    up_moved = [swap(up_sent[1], "seq", bits_up[0])]
    gate_moved[0], up_moved[0] = tie_all([gate_moved[0], up_moved[0]], micros=TUNE["g0"])
    down_late = tie(down_term, *d_mixed[1:])
    down_sum = plain(lax.psum_scatter(plain(down_late), "seq", scatter_dimension=0, tiled=True))
    gate_moved.append(swap(tie(gate_sent[0], *d_mixed[1:], gate_moved[0], up_moved[0]), "seq", bits_down[0]))
    up_moved.append(swap(tie(up_sent[0], *d_mixed[1:], gate_moved[0], up_moved[0]), "seq", bits_up[0]))
    branch_late = tie(d_branch, *d_mixed[1:])
    above, below = from_next(branch_late, "head"), to_next(branch_late, "head")
    d_queries, d_kv_own, d_kv_sent = attend_back(
        queries,
        d_mixed,
        mixed_wide,
        kv_near,
        kv_other,
        key_code,
        query_code,
        log_total,
        [gate_moved[0], up_moved[0]],
    )
    d_kv_moved = swap(tie(d_kv_sent, above, below), "seq", 0)
    half = tok_rows // 2
    above, below = tie_all([above, below], d_queries)
    above_far = from_next(jnp.concatenate([above[:half], out_term[2]]), "head")
    below_far = to_next(jnp.concatenate([below[half:], out_term[3]]), "head")
    down, up = sum_payload(out_term[1], out_term[4], [above_far[half:], below_far[half:]])
    out_moved = [from_next(down, "head"), to_next(up, "head")]
    branch_parts = [d_branch, above, above_far, below_far, below]
    output = total([own_hidden, out_term[0], *out_moved]).astype(BF)
    gate_moved[1], up_moved[1] = tie_all([gate_moved[1], up_moved[1]], micros=TUNE["g1"])
    d_kv_moved = tie(d_kv_moved, gate_moved[1], up_moved[1])
    d_kv = total([d_kv_own, d_kv_moved])
    d_keys, keys_last = sum_xor([d_kv[i, 0] for i in range(far)], "seq", bits_down)
    d_values, values_last = sum_xor([d_kv[i, 1] for i in range(far)], "seq", bits_up)
    d_other_raw = jnp.where(odd, d_keys, d_values).astype(BF)
    d_other_sent = d_other_raw
    d_other_raw = swap(d_other_sent, "head", 0)
    d_other = d_other_raw.reshape(2, heads_dev, tok_rows // 2, HD)
    d_other = roll_blocks(d_other, jnp.where(odd, 1, heads_dev - 1), 1).reshape(2, half_rows, HD)
    d_kv_total = jnp.where(odd, d_values, d_keys) + d_other.astype(F32)


    def second(low, high, moved, bit):
        high_moved, low_moved = tie_all(moved, d_other_sent)
        return [low, low_moved, swap(total([high, high_moved]).astype(BF), "seq", bit)]

    gate_terms = second(gate_low, gate_high, gate_moved, bits_down[1])
    up_terms = second(up_low, up_high, up_moved, bits_up[1])
    *d_one, cols_kept, outs_kept, wide_sent = project_back(
        seq_own,
        head_own,
        orders,
        d_queries,
        d_kv_total,
        cosine_part,
        sine_part,
        normed_one,
        inputs_grp,
        cols_weight,
        mixed,
        branch_parts,
        grad_gain_two,
        [down_sum, *out_moved],
    )
    moved = sum_first(d_one[2:4], "head")
    wide_moved = tie_all([swap(wide_sent, "seq", 0)], micros=TUNE["wm"])[0]
    down, up = sum_payload(d_one[1], d_one[4], moved, others=[wide_moved])
    gate_terms[-1], up_terms[-1] = tie(gate_terms[-1], down), tie(up_terms[-1], down)
    cols_moved = wide_moved[:, :, : query_cols + HD]
    outs_moved = wide_moved[:, :own_rows, query_cols + HD :]
    cols_terms = sum_step([cols_kept, cols_moved], "seq", bits_down[0])
    outs_terms = sum_step([outs_kept, outs_moved], "seq", bits_up[0])
    cols_terms[-1], outs_terms[-1] = tie_all([cols_terms[-1], outs_terms[-1]], micros=TUNE["ct"])
    down, up = from_next(down, "head"), to_next(up, "head")
    d_normed_one = total([d_one[0], tie(down, cols_terms[-1], outs_terms[-1]), up])
    grad_cols = sum_halving(cols_terms, "seq", bits_down[1:]).astype(BF)
    grad_outs = sum_halving(outs_terms, "seq", bits_up[1:])
    inputs_f = inputs.astype(F32)
    inv_one = inverse_norm(inputs_f)
    scaled = d_normed_one * gain_attn
    inner = jnp.mean(scaled * inputs_f, axis=-1, keepdims=True)
    grad_inputs = (d_hidden + inv_one * scaled - inputs_f * (inv_one**3 * inner)).astype(BF)

    grad_out = grad_outs.T
    cols_wide = query_cols + HD
    more_rows = jnp.broadcast_to(grad_cols[own_rows:], (heads_dev, MORE_ROWS, cols_wide))
    grad_blocks = jnp.concatenate(
        [grad_cols[:own_rows].reshape(heads_dev, own_wide, cols_wide), more_rows], axis=1
    )
    grad_qkv = jnp.zeros((own_wide, QKV), F32)
    small_parts = []
    for apart in range(heads_dev):
        source = (head_index + apart) % heads_dev
        target = (head_index - apart) % heads_dev
        block = lax.dynamic_index_in_dim(grad_blocks, target, 0, keepdims=False)
        if apart:
            block = from_next(block, "head", apart)
        small_parts.append(block[own_wide : own_wide + 2])
        block = block[:own_wide].astype(F32)
        kv_place = QD + source % 2 * KD + source // copies * HD
        grad_qkv = lax.dynamic_update_slice_in_dim(
            grad_qkv, block[:, :query_cols], source * query_cols, 1
        )
        grad_qkv = lax.dynamic_update_slice_in_dim(grad_qkv, block[:, query_cols:], kv_place, 1)
    small_grads = total(small_parts)

    def own_part(row, start, size):
        return lax.dynamic_slice(small_grads, (row, start + head_index * size), (1, size)).reshape(size)

    key_bias = (QD + KD) // (seq_dev * heads_dev)
    value_bias = KD // (seq_dev * heads_dev)

    gate_sum = sum_halving(gate_terms, "seq", bits_down[2:])
    up_sum = sum_halving(up_terms, "seq", bits_up[2:])

    return (
        output,
        grad_inputs,
        own_part(0, 0, gain_cols),
        grad_qkv,
        own_part(1, 0, key_bias),
        own_part(1, heads_dev * key_bias, value_bias),
        grad_out,
        own_part(0, heads_dev * gain_cols, gain_cols),
        gate_sum[:, :units],
        up_sum[:, :units],
        down_sum[:, :units].T.astype(F32),
    )


def solution(mesh):
    both = ("seq", "head")
    in_specs = (
        P(both, None),
        P(both),
        P(both, None),
        P(both),
        P("head", "seq"),
        P(both),
        P("seq", "head"),
        P("seq", "head"),
        P("head", "seq"),
        P(both, None),
        P(both),
        P(both),
    )
    out_specs = (
        P(both, None),
        P(both, None),
        P(both),
        P(both, None),
        P(both),
        P(both),
        P("head", "seq"),
        P(both),
        P("seq", "head"),
        P("seq", "head"),
        P("head", "seq"),
    )
    return jax.shard_map(
        per_device, mesh=mesh, in_specs=in_specs, out_specs=out_specs, check_vma=False
    )
```

```python
import functools
import math

import jax
import jax.numpy as jnp
from jax import lax
from jax.experimental import pallas as pl
from jax.experimental.layout import Layout, with_layout_constraint
from jax.experimental.pallas import tpu as pltpu
from jax.sharding import PartitionSpec as P

HEADS = 12
KV_HEADS = 2
HD = 128
MORE_ROWS = 16
QD = 1536
KD = 256
QKV = 2048


EPS = 1e-06
ROPE_BASE = 1000000.0
MASKED = -1e30
LOWEST = -1e29
SEG_STEP = 1 << 20
TILE = 768
MIB = 2**20

TUNE = dict(x1=10, x2=30, mx=10, c2=8, g1=25, wm=0, ct=0, s2=20, project=7, project_back=9, attend=16, attend_back=18, feed_forward=36, down_product=8, pair_grads=7, wide_grads=11, norm_back=5.5, payload=2, far=25)

BF = jnp.bfloat16
F32 = jnp.float32


def plain(values):
    return with_layout_constraint(values, Layout(major_to_minor=tuple(range(values.ndim))))


def bits_of(axis):
    return (lax.axis_size(axis) - 1).bit_length()


def bit_value(axis, bit):
    return (lax.axis_index(axis) >> bit) & 1


def send(block, axis, target):
    count = lax.axis_size(axis)
    return plain(lax.ppermute(plain(block), axis, [(j, target(j) % count) for j in range(count)]))


def swap(block, axis, bit):
    return send(block, axis, lambda j: j ^ (1 << bit))


def from_next(block, axis, apart=1):
    return send(block, axis, lambda j: j - apart)


def to_next(block, axis):
    return send(block, axis, lambda j: j + 1)


def tie_kernel(*refs):
    del refs


def tie_all(blocks, *others, micros=0):
    count = len(blocks)
    return pl.pallas_call(
        tie_kernel,
        in_specs=[pl.BlockSpec(memory_space=pl.ANY)] * (count + len(others)),
        out_specs=[pl.BlockSpec(memory_space=pl.ANY)] * count,
        out_shape=[jax.ShapeDtypeStruct(block.shape, block.dtype) for block in blocks],
        input_output_aliases={i: i for i in range(count)},
        compiler_params=pltpu.CompilerParams(
            vmem_limit_bytes=60 * MIB if max(block.size for block in blocks) > MIB else MIB
        ),
        cost_estimate=cost(micros),
        name="tie",
    )(*blocks, *others)


def tie(block, *others):
    return tie_all([block], *others)[0]


def gather_blocks(block, axis, last=(), micros=0):
    above = from_next(block, axis)
    below = to_next(block, axis)
    above, below = tie_all([above, below], *last, micros=micros)
    return [block, above, from_next(above, axis), below]


def payload_kernel(behind_ref, moved_ref, *refs):
    refs[-1][...] = (behind_ref[...].astype(F32) + moved_ref[...].astype(F32)).astype(BF)


def sum_payload(behind, moved, others=()):
    return pl.pallas_call(
        payload_kernel,
        in_specs=[vmem()] * 2 + [anywhere()] * len(others),
        out_specs=vmem(),
        out_shape=shape_of(behind.shape),
        compiler_params=params(16),
        cost_estimate=cost(TUNE["payload"]),
        name="payload",
    )(behind, moved, *others)


def far_first(block, axis):
    return swap(block, axis, 1), swap(block, axis, 2)


def far_last(block, first, axis, last=()):
    count = lax.axis_size(axis) // 2
    one, two = tie_all(first, *last)
    if count == 4:
        half = block.shape[0] // 2
        parts = [swap(one[:half], axis, 2), swap(two[half:], axis, 1)]
        blocks = [block, one, two, jnp.concatenate(parts)]
    else:
        more = [send(block, axis, lambda j: j ^ 2 * i) for i in range(3, count)]
        blocks, parts = [block, one, two, *more], [one]
    return plain(jnp.stack(blocks)), parts


def total(terms):
    result = terms[0].astype(F32)
    for term in terms[1:]:
        result = result + term.astype(F32)
    return result


def sum_step(terms, axis, bit, last=()):
    half = terms[0].shape[0] // 2
    sent = total([term[half:] for term in terms]).astype(BF)
    moved = swap(tie(sent, *last) if last else sent, axis, bit)
    return [term[:half] for term in terms] + [moved]


def sum_halving(terms, axis, bits):
    for bit in bits:
        terms = sum_step(terms, axis, bit)
    return total([term[0] for term in terms])


def sum_xor(blocks, axis, bits):
    blocks = dict(enumerate(blocks))
    for bit in bits:
        place = 1 << bit - 1
        sent = [m for m in sorted(blocks) if m & place]
        moved = swap(jnp.stack([blocks[m].astype(BF) for m in sent]), axis, bit)
        for i, m in enumerate(sent):
            blocks[m ^ place] = blocks[m ^ place] + moved[i].astype(F32)
            del blocks[m]
    return blocks[0], moved


def roll_blocks(stacked, shift, axis=0):
    count = stacked.shape[axis]
    return lax.dynamic_slice_in_dim(
        jnp.concatenate([stacked, stacked], axis=axis), shift, count, axis
    )


def dot_nn(left, right):
    return jnp.dot(left, right, preferred_element_type=F32)


def dot_nt(left, right):
    return lax.dot_general(left, right, (((1,), (1,)), ((), ())), preferred_element_type=F32)


def dot_tn(left, right):
    return lax.dot_general(left, right, (((0,), (0,)), ((), ())), preferred_element_type=F32)


def inverse_norm(values):
    return lax.rsqrt(jnp.mean(values * values, axis=-1, keepdims=True) + EPS)


def vmem():
    return pl.BlockSpec(memory_space=pltpu.VMEM)


def smem():
    return pl.BlockSpec(memory_space=pltpu.SMEM)


def anywhere():
    return pl.BlockSpec(memory_space=pl.ANY)


def shape_of(shape, dtype=BF):
    return jax.ShapeDtypeStruct(shape, dtype)


def fixed(shape):
    return pl.BlockSpec(shape, lambda *i: (0,) * len(shape))


def params(mib):
    return pltpu.CompilerParams(vmem_limit_bytes=mib * MIB)


def cost(micros):
    return pl.CostEstimate(flops=int(micros * 1153e6), bytes_accessed=0, transcendentals=0)


def cut(size, tile):
    return [(at, min(tile, size - at)) for at in range(0, size, tile)]


def start_blocks(own_ref, near_ref, other_ref, to_ref, sem):
    count = near_ref.shape[0]
    rows = to_ref.shape[0] // (2 * count)
    copies = []
    for side, source in enumerate((near_ref, other_ref)):
        for i in range(count):
            at = pl.multiple_of((own_ref[0] ^ (2 * i + side)) * rows, 16)
            copy = pltpu.make_async_copy(
                source.at[i, pl.ds(0, rows), :], to_ref.at[pl.ds(at, rows), :], sem.at[side, i]
            )
            copy.start()
            copies.append(copy)
    return copies


def masks_of(bits):
    masks = [0]
    for bit in bits[::-1]:
        masks += [mask | 1 << bit for mask in masks]
    return masks


def store_rows(refs, cols, values):
    at = 0
    for ref in refs:
        ref[:, cols] = values[at : at + ref.shape[0], :].astype(ref.dtype)
        at += ref.shape[0]


def row_shapes(tok_rows, width):
    return [shape_of((tok_rows, width), F32)] + [shape_of((tok_rows, width))] * 3


def fill_rows(to_ref, parts):
    size = parts[0].shape[0]
    for t, part in enumerate(parts):
        to_ref[t * size : (t + 1) * size, :] = part[:size, :]


def head_rows(tok_rows, blocks):
    half_block = tok_rows // 2
    return [
        (half, u * half_block, u * tok_rows + half * half_block, half_block)
        for u in range(blocks)
        for half in range(2)
    ]


def arrange_kernel(head_ref, *refs):
    to_ref = refs[-1]
    count = len(refs) - 1
    rows = refs[0].shape[0] - MORE_ROWS
    line = lax.broadcasted_iota(jnp.int32, (MORE_ROWS, to_ref.shape[1]), 0)
    small = jnp.zeros(line.shape, F32)
    for apart, ref in enumerate(refs[:-1]):
        place = lax.rem(head_ref[0] + apart, count)
        to_ref[pl.ds(pl.multiple_of(place * rows, rows), rows), :] = ref[:rows, :]
        small = jnp.where(line == place, ref[rows : rows + 1, :].astype(F32), small)
    to_ref[count * rows : count * rows + MORE_ROWS, :] = small.astype(BF)
    to_ref[count * rows + MORE_ROWS :, :] = jnp.zeros(line.shape, BF)


def arrange(head, blocks):
    rows, cols = blocks[0].shape
    if (rows - MORE_ROWS) % 16:
        count = len(blocks)
        ordered = roll_blocks(jnp.stack(blocks), (count - head[0]) % count)
        small = jnp.pad(ordered[:, rows - MORE_ROWS], ((0, 2 * MORE_ROWS - count), (0, 0)))
        return jnp.concatenate([ordered[:, : rows - MORE_ROWS].reshape(-1, cols), small])
    return pl.pallas_call(
        arrange_kernel,
        in_specs=[smem()] + [vmem()] * len(blocks),
        out_specs=vmem(),
        out_shape=shape_of((len(blocks) * (rows - MORE_ROWS) + 2 * MORE_ROWS, cols)),
        compiler_params=params(60),
        cost_estimate=cost(1),
        name="arrange",
    )(head, *blocks)


def project_kernel(heads, gain_cols, bias_cols, own_ref, head_ref, *refs):
    parts = refs[:4]
    cos_ref, sin_ref, near, other = refs[4:8]
    q_ref, kv_ref, x_ref, normed_ref, w_ref, small_v, gain_v, all_v, bias_v, sem, small_sem = refs[8:]
    rows = w_ref.shape[0] // small_v.shape[0]
    smalls = []
    for side, source in enumerate((near, other)):
        for i in range(source.shape[0]):
            copy = pltpu.make_async_copy(
                source.at[i, pl.ds(rows, MORE_ROWS), :],
                small_v.at[own_ref[0] ^ (2 * i + side)],
                small_sem.at[side, i],
            )
            copy.start()
            smalls.append(copy)
    copies = start_blocks(own_ref, near, other, w_ref, sem)
    for copy in smalls:
        copy.wait()
    devices = gain_v.shape[1] // gain_cols
    per = devices // small_v.shape[0]
    for d in range(devices):
        row = small_v[d // per, d % per : d % per + 1, :].astype(F32)
        gain_v[:, d * gain_cols : (d + 1) * gain_cols] = row[:, :gain_cols]
        all_v[:, d * bias_cols : (d + 1) * bias_cols] = row[:, 2 * gain_cols : 2 * gain_cols + bias_cols]
    head = head_ref[0]
    last = heads * HD
    slot = (head // ((QD // last) // KV_HEADS)) * HD
    bias_v[:, :last] = all_v[:, pl.ds(pl.multiple_of(head * last, HD), last)]
    bias_v[:, last : last + HD] = all_v[:, pl.ds(pl.multiple_of(QD + slot, HD), HD)]
    bias_v[:, last + HD :] = all_v[:, pl.ds(pl.multiple_of(QD + KD + slot, HD), HD)]
    fill_rows(x_ref, parts)
    values = x_ref[...].astype(F32)
    normed_ref[...] = (values * inverse_norm(values) * gain_v[...]).astype(BF)
    for copy in copies:
        copy.wait()
    joint = dot_nn(normed_ref[...], w_ref[...]) + bias_v[...]
    tok_rows = parts[0].shape[0]
    blocks = x_ref.shape[0] // tok_rows
    half_rows = x_ref.shape[0] // 2
    for j in range(heads + 2):
        part = joint[:, j * HD : (j + 1) * HD]
        if j <= heads:
            part = part * cos_ref[...] + pltpu.roll(part, HD // 2, 1) * sin_ref[...]
        part = part.astype(BF)
        for half, low, row, count in head_rows(tok_rows, blocks):
            piece = part[row : row + count]
            if j < heads:
                q_ref[half, j * half_rows + low : j * half_rows + low + count, :] = piece
            else:
                kv_ref[j - heads, half, low : low + count, :] = piece


def project(own, head, parts, cos, sin, near, other, heads, gain_cols, bias_cols):
    width = parts[0].shape[1]
    rows = cos.shape[0]
    cols = near.shape[2]
    return pl.pallas_call(
        functools.partial(project_kernel, heads, gain_cols, bias_cols),
        in_specs=[smem()] * 2 + [vmem()] * 6 + [anywhere()] * 2,
        out_specs=[vmem()] * 5,
        out_shape=[
            shape_of((2, heads * rows // 2, HD)),
            shape_of((2, 2, rows // 2, HD)),
            shape_of((rows, width)),
            shape_of((rows, width)),
            shape_of((width, cols)),
        ],
        scratch_shapes=[
            pltpu.VMEM((2 * near.shape[0], MORE_ROWS, cols), BF),
            pltpu.VMEM((1, width), F32),
            pltpu.VMEM((1, QKV), F32),
            pltpu.VMEM((1, cols), F32),
            pltpu.SemaphoreType.DMA((2, near.shape[0])),
            pltpu.SemaphoreType.DMA((2, near.shape[0])),
        ],
        compiler_params=params(60),
        cost_estimate=cost(TUNE["project"]),
        name="project",
    )(own, head, *parts, cos, sin, near, other)


def project_back_kernel(heads, orders, others, own_ref, head_ref, *refs):
    refs = refs[:13] + refs[13 + others :]
    dq_ref, dkv_ref, cos_ref, sin_ref, normed_ref, x_ref, w_ref, mixed_ref = refs[:8]
    parts = refs[8:12]
    gain_two_ref = refs[12]
    dn_refs = refs[13:17]
    cols_kept, outs_kept, wide_sent = refs[17:20]
    cols, branch, wide, wide_out, bias_v, small_v = refs[20:]
    rows = cos_ref.shape[0]
    half_rows = rows // 2
    tok_rows = parts[0].shape[0]
    blocks = rows // tok_rows
    head = head_ref[0]
    odd = (head & 1) == 1
    for half, low, row, count in head_rows(tok_rows, blocks):
        here = slice(row, row + count)
        for j in range(heads + 1):
            if j < heads:
                start = j * half_rows + low
                part = dq_ref[half, start : start + count, :]
            else:
                part = dkv_ref[half, low : low + count, :]
            part = part.astype(BF).astype(F32)
            turned = part * cos_ref[here, :] - pltpu.roll(part, HD // 2, 1) * sin_ref[here, :]
            if j == heads:
                turned = jnp.where(odd, part, turned)
            cols[here, j * HD : (j + 1) * HD] = turned.astype(BF)
    last = heads * HD
    bias = jnp.sum(cols[...].astype(F32), axis=0, keepdims=True)
    bias_v[...] = jnp.zeros(bias_v.shape, F32)
    bias_v[:, pl.ds(pl.multiple_of(head * last, HD), last)] = bias[:, :last]
    copies = (QD // last) // KV_HEADS
    slot = QD + (head & 1) * KD + (head // copies) * HD
    bias_v[:, pl.ds(pl.multiple_of(slot, HD), HD)] = bias[:, last:]
    key_w = jnp.where(odd, w_ref[:, last + HD :], w_ref[:, last : last + HD])
    grad = dot_nt(cols[:, :last], w_ref[:, :last]) + dot_nt(cols[:, last:], key_w)
    store_rows(dn_refs, slice(None), grad)
    values = x_ref[...].astype(F32)
    gain_one = jnp.sum(grad * (values * inverse_norm(values)), axis=0, keepdims=True)
    seq_dev = small_v.shape[0]
    small_v[...] = jnp.zeros(small_v.shape, BF)
    for row, vectors in enumerate(
        ((gain_one, gain_two_ref[...]), (bias_v[:, : QD + KD], bias_v[:, QD + KD :]))
    ):
        for i in range(seq_dev):
            at = 0
            for vector in vectors:
                size = vector.shape[1] // seq_dev
                small_v[i, row : row + 1, at : at + size] = vector[:, i * size : (i + 1) * size].astype(BF)
                at += size
    count = outs_kept.shape[1]
    fill_rows(branch, parts)
    wide[...] = dot_tn(normed_ref[...], cols[...]).astype(BF)
    wide_out[...] = dot_tn(branch[...], mixed_ref[...]).astype(BF)
    split = cols.shape[1]
    wide_sent[:, count:, split:] = jnp.zeros((wide_sent.shape[0], MORE_ROWS, wide_sent.shape[2] - split), BF)
    for i in range(cols_kept.shape[0]):
        for source, order, kept, lanes in (
            (wide, orders[0], cols_kept, slice(0, split)),
            (wide_out, orders[1], outs_kept, slice(split, wide_sent.shape[2])),
        ):
            for side in range(2):
                block = own_ref[0] ^ order[i] ^ side
                rows = source[pl.ds(pl.multiple_of(block * count, 16), count), :]
                if side == 0:
                    kept[i, :count] = rows
                else:
                    wide_sent[i, :count, lanes] = rows
                if source is wide:
                    small = small_v[block]
                    if side == 0:
                        kept[i, count:] = small
                    else:
                        wide_sent[i, count:, lanes] = small


def project_back(own, head, orders, dq, dkv, cos, sin, normed, x, w, mixed, parts, gain_two, others):
    rows, width = normed.shape
    heads = dq.shape[1] // (rows // 2)
    cols = (heads + 1) * HD
    tok_rows = parts[0].shape[0]
    far = len(orders[0])
    part_rows = width // (2 * far)
    return pl.pallas_call(
        functools.partial(project_back_kernel, heads, orders, len(others)),
        in_specs=[smem()] * 2 + [vmem()] * 13 + [anywhere()] * len(others),
        out_specs=[vmem()] * 7,
        out_shape=[
            *row_shapes(tok_rows, width),
            shape_of((far, part_rows + MORE_ROWS, cols)),
            shape_of((far, part_rows, heads * HD)),
            shape_of((far, part_rows + MORE_ROWS, cols + heads * HD)),
        ],
        scratch_shapes=[
            pltpu.VMEM((rows, cols), BF),
            pltpu.VMEM((rows, width), BF),
            pltpu.VMEM((width, cols), BF),
            pltpu.VMEM((width, heads * HD), BF),
            pltpu.VMEM((1, QKV), F32),
            pltpu.VMEM((2 * far, MORE_ROWS, cols), BF),
        ],
        compiler_params=params(60),
        cost_estimate=cost(TUNE["project_back"]),
        name="project_back",
    )(own, head, dq, dkv, cos, sin, normed, x, w, mixed, *parts, gain_two, *others)


def visible_of(key_code, query_code, half):
    seen = key_code <= query_code
    if half == 1:
        seen &= key_code >= (query_code & -SEG_STEP)
    return seen


PAIRS = ((0, 0), (0, 1), (1, 1))
SEQ_STEP = 4


def pick_side(first_steps, near_ref, other_ref, which, half):
    near = near_ref[:, which, half]
    other = other_ref[:, which, half]
    block = jnp.where(pl.program_id(0) < first_steps, near, other)
    return block.reshape(block.shape[0] * block.shape[1], block.shape[2])


def codes(code_ref, half):
    block = code_ref[:, half]
    return block.reshape(block.shape[0] * block.shape[1], 1)


def attend_kernel(scale, first_steps, tok_rows, q_ref, near_ref, other_ref, kc_ref, qc_ref, *refs):
    mixed_ref, wide_ref, lse_ref, top, total, acc = refs[-6:]
    step = pl.program_id(0)

    @pl.when(step == 0)
    def _():
        top[...] = jnp.full(top.shape, LOWEST, F32)
        total[...] = jnp.zeros(total.shape, F32)
        acc[...] = jnp.zeros(acc.shape, F32)

    for key_half, query_half in PAIRS:
        keys = pick_side(first_steps, near_ref, other_ref, 0, key_half)
        values = pick_side(first_steps, near_ref, other_ref, 1, key_half)
        scores = dot_nt(keys, q_ref[query_half])
        if key_half == query_half:
            seen = visible_of(codes(kc_ref, key_half), qc_ref[query_half], key_half)
            scores = jnp.where(seen, scores, MASKED)
        old = top[query_half]
        new = jnp.maximum(old, jnp.max(scores, axis=0, keepdims=True))
        weights = jnp.exp2((scores - new) * scale)
        factor = jnp.exp2((old - new) * scale)
        top[query_half] = new
        total[query_half] = total[query_half] * factor + jnp.sum(weights, axis=0, keepdims=True)
        acc[query_half] = acc[query_half] * factor + dot_tn(values, weights.astype(BF))

    @pl.when(step == pl.num_programs(0) - 1)
    def _():
        blocks = mixed_ref.shape[0] // tok_rows
        half_rows = mixed_ref.shape[0] // 2
        for half in range(2):
            wide_ref[half] = jnp.transpose(acc[half] / total[half])
            lse_ref[half] = top[half] * scale + jnp.log2(total[half])
        for half, low, row, count in head_rows(tok_rows, blocks):
            for j in range(mixed_ref.shape[1] // HD):
                at = j * half_rows + low
                mixed_ref[row : row + count, j * HD : (j + 1) * HD] = wide_ref[
                    half, at : at + count, :
                ].astype(BF)


def side_specs(shape, first_steps):
    block = (SEQ_STEP,) + shape[1:]
    rest = (0,) * (len(shape) - 1)
    return [
        pl.BlockSpec(block, lambda i: (jnp.minimum(i, first_steps - 1),) + rest),
        pl.BlockSpec(block, lambda i: (jnp.maximum(i - first_steps, 0),) + rest),
    ]


def code_spec(shape):
    return pl.BlockSpec((SEQ_STEP,) + shape[1:], lambda i: (i,) + (0,) * (len(shape) - 1))


def attend(queries, near, other, key_code, query_code, tok_rows, others):
    _, rows, _ = queries.shape
    half_rows = near.shape[3]
    heads = rows // half_rows
    first_steps = near.shape[0] // SEQ_STEP
    return pl.pallas_call(
        functools.partial(attend_kernel, HD**-0.5 * math.log2(math.e), first_steps, tok_rows),
        grid=(2 * first_steps,),
        in_specs=[fixed(queries.shape)]
        + side_specs(near.shape, first_steps)
        + [code_spec(key_code.shape), fixed(query_code.shape)]
        + [anywhere()] * len(others),
        out_specs=[fixed((2 * half_rows, heads * HD)), fixed((2, rows, HD)), fixed((2, 1, rows))],
        out_shape=[
            shape_of((2 * half_rows, heads * HD)),
            shape_of((2, rows, HD), F32),
            shape_of((2, 1, rows), F32),
        ],
        scratch_shapes=[
            pltpu.VMEM((2, 1, rows), F32),
            pltpu.VMEM((2, 1, rows), F32),
            pltpu.VMEM((2, HD, rows), F32),
        ],
        compiler_params=params(60),
        cost_estimate=cost(TUNE["attend"]),
        name="attend",
    )(queries, near, other, key_code, query_code, *others)


def attend_back_kernel(scale, first_steps, others, q_ref, *refs):
    grads = refs[:4]
    wide_ref, near_ref, other_ref, kc_ref, qc_ref, lse_ref = refs[4:10]
    dq_ref, own_ref, sent_ref, acc, do, delta = refs[10 + others :]
    step = pl.program_id(0)
    half_rows = near_ref.shape[3]
    tok_rows = grads[0].shape[0]

    @pl.when(step == 0)
    def _():
        acc[...] = jnp.zeros(acc.shape, F32)
        for u, grad in enumerate(grads):
            for half, low, row, count in head_rows(tok_rows, 1):
                for j in range(grad.shape[1] // HD):
                    at = j * half_rows + u * (tok_rows // 2)
                    do[half, at : at + count, :] = grad[row : row + count, j * HD : (j + 1) * HD]
        for half in range(2):
            product = do[half].astype(F32) * wide_ref[half]
            delta[half] = jnp.sum(jnp.transpose(product), axis=0, keepdims=True)

    results = []
    for key_half in range(2):
        keys = pick_side(first_steps, near_ref, other_ref, 0, key_half)
        values = pick_side(first_steps, near_ref, other_ref, 1, key_half)
        grad_keys, grad_values = None, None
        for query_half in range(key_half, 2):
            queries = q_ref[query_half]
            grad = do[query_half]
            scores = dot_nt(keys, queries) * (scale * math.log2(math.e))
            weights = jnp.exp2(scores - lse_ref[query_half])
            if key_half == query_half:
                seen = visible_of(codes(kc_ref, key_half), qc_ref[query_half], key_half)
                weights = jnp.where(seen, weights, 0.0)
            grad_weights = dot_nt(values, grad)
            grad_scores = (weights * (grad_weights - delta[query_half])).astype(BF)
            value_term = dot_nn(weights.astype(BF), grad)
            key_term = dot_nn(grad_scores, queries)
            grad_keys = key_term if grad_keys is None else grad_keys + key_term
            grad_values = value_term if grad_values is None else grad_values + value_term
            acc[query_half] += dot_tn(keys, grad_scores)
        shape = (SEQ_STEP, half_rows, HD)
        results.append((grad_keys * scale).reshape(shape).astype(BF))
        results.append(grad_values.reshape(shape).astype(BF))

    def store(ref):
        for key_half in range(2):
            ref[:, 0, key_half] = results[2 * key_half]
            ref[:, 1, key_half] = results[2 * key_half + 1]

    pl.when(step < first_steps)(lambda: store(own_ref))
    pl.when(step >= first_steps)(lambda: store(sent_ref))

    @pl.when(step == pl.num_programs(0) - 1)
    def _():
        for half in range(2):
            dq_ref[half] = jnp.transpose(acc[half] * scale)


def attend_back(queries, grads, wide, near, other, key_code, query_code, log_total, others):
    _, rows, _ = queries.shape
    first_steps = near.shape[0] // SEQ_STEP
    sides = side_specs(near.shape, first_steps)
    return pl.pallas_call(
        functools.partial(attend_back_kernel, HD**-0.5, first_steps, len(others)),
        grid=(2 * first_steps,),
        in_specs=[fixed(queries.shape)]
        + [fixed(grad.shape) for grad in grads]
        + [fixed(wide.shape)]
        + sides
        + [code_spec(key_code.shape), fixed(query_code.shape), fixed(log_total.shape)]
        + [anywhere()] * len(others),
        out_specs=[fixed((2, rows, HD))] + sides,
        out_shape=[shape_of((2, rows, HD), F32), shape_of(near.shape), shape_of(near.shape)],
        scratch_shapes=[
            pltpu.VMEM((2, HD, rows), F32),
            pltpu.VMEM((2, rows, HD), BF),
            pltpu.VMEM((2, 1, rows), F32),
        ],
        compiler_params=params(60),
        cost_estimate=cost(TUNE["attend_back"]),
        name="attend_back",
    )(queries, *grads, wide, near, other, key_code, query_code, log_total, *others)


OUT_TILE = 256
FEED_TILE = 512


def feed_forward_kernel(own_ref, gain_ref, *refs):
    x_hbm = refs[0]
    cot_parts = refs[1:5]
    mixed_parts = refs[5:9]
    near_w, other_w, joined_w = refs[9:12]
    refs = refs[12:]
    acts_ref, hidden_ref, middle_ref, cot_ref = refs[:4]
    dx_refs = refs[4:8]
    x_v, out_v, gate_v, up_v, down_v, mixed_v, normed_v, middle_v, dg_v, du_v, cot_v = refs[8:19]
    in_sem, cot_sem, out_sem, w_sem, s_sem = refs[19:]
    rows, width = x_v.shape
    units = gate_v.shape[1]
    tok_rows = hidden_ref.shape[0]
    half = tok_rows // 2
    blocks = rows // tok_rows
    chunks = cut(units, FEED_TILE)
    cols = mixed_parts[0].shape[1]

    def begin(source, target, sem):
        copy = pltpu.make_async_copy(source, target, sem)
        copy.start()
        return copy

    first = [begin(x_hbm, x_v, in_sem.at[0])]
    for t, part in enumerate(mixed_parts):
        for b in range(blocks):
            u = (b + t) % blocks
            first.append(
                begin(
                    part.at[pl.ds(b * tok_rows, tok_rows), :],
                    mixed_v.at[pl.ds(u * tok_rows, tok_rows), pl.ds(t * cols, cols)],
                    in_sem.at[len(first)],
                )
            )
    first += start_blocks(own_ref, near_w, other_w, out_v, out_sem)
    cots, step = [], cot_parts[0].shape[0] // 2
    for part in cot_parts:
        for low in range(0, part.shape[0], step):
            i = len(cots)
            cots.append(
                begin(
                    part.at[pl.ds(low, half), :], cot_v.at[pl.ds(i * half, half), :], cot_sem.at[i]
                )
            )
    for copy in first:
        copy.wait()
    loads = [
        [
            begin(
                joined_w.at[:, pl.ds(j * units + at, size)], dst.at[:, pl.ds(at, size)], w_sem.at[i, j]
            )
            for j, dst in enumerate((gate_v, up_v, down_v))
        ]
        for i, (at, size) in enumerate(chunks)
    ]
    hidden = x_v[...].astype(F32) + dot_nt(mixed_v[...], out_v[...])
    hidden_ref[...] = hidden[:tok_rows]
    normed_v[...] = (hidden * inverse_norm(hidden) * gain_ref[...]).astype(BF)
    for copy in cots:
        copy.wait()
    normed_to = acts_ref.at[:, pl.ds(2 * units, width)]
    stores = [begin(normed_v, normed_to, s_sem.at[0]), begin(cot_v, cot_ref, s_sem.at[1])]
    for i, (at, size) in enumerate(chunks):
        for copy in loads[i]:
            copy.wait()
        here = slice(at, at + size)
        gate = dot_nn(normed_v[...], gate_v[:, here])
        up = dot_nn(normed_v[...], up_v[:, here])
        grad = dot_nn(cot_v[...], down_v[:, here])
        sig = 1.0 / (1.0 + jnp.exp(-gate))
        active = gate * sig
        middle_v[:, here] = (active * up).astype(BF)
        dg_v[:, here] = (grad * up * sig * (1.0 + gate * (1.0 - sig))).astype(BF)
        du_v[:, here] = (grad * active).astype(BF)
    for j, (src, dst) in enumerate(
        (
            (dg_v, acts_ref.at[:, pl.ds(0, units)]),
            (du_v, acts_ref.at[:, pl.ds(units, units)]),
            (middle_v, middle_ref),
        )
    ):
        stores.append(begin(src, dst, s_sem.at[2 + j]))
    for at, size in cut(width, OUT_TILE):
        here = slice(at, at + size)
        grad = dot_nt(dg_v[...], gate_v[here, :]) + dot_nt(du_v[...], up_v[here, :])
        store_rows(dx_refs, here, grad)
    for copy in stores:
        copy.wait()


def feed_forward(own, x, gain, cot_parts, mixed_parts, near, other, joined_all, tok_rows):
    rows, width = x.shape
    units = joined_all.shape[1] // 3
    blocks = rows // tok_rows
    return pl.pallas_call(
        feed_forward_kernel,
        in_specs=[smem(), vmem()] + [anywhere()] * 12,
        out_specs=[anywhere(), vmem()] + [anywhere()] * 2 + [vmem()] * 4,
        out_shape=[
            shape_of((rows, 2 * units + width)),
            shape_of((tok_rows, width), F32),
            shape_of((rows, units)),
            shape_of((rows, width)),
            *row_shapes(tok_rows, width),
        ],
        scratch_shapes=[
            pltpu.VMEM((rows, width), BF),
            pltpu.VMEM((width, QD), BF),
            pltpu.VMEM((width, units), BF),
            pltpu.VMEM((width, units), BF),
            pltpu.VMEM((width, units), BF),
            pltpu.VMEM((rows, QD), BF),
            pltpu.VMEM((rows, width), BF),
            pltpu.VMEM((rows, units), BF),
            pltpu.VMEM((rows, units), BF),
            pltpu.VMEM((rows, units), BF),
            pltpu.VMEM((rows, width), BF),
            pltpu.SemaphoreType.DMA((1 + blocks * blocks,)),
            pltpu.SemaphoreType.DMA((2 * blocks,)),
            pltpu.SemaphoreType.DMA((2, near.shape[0])),
            pltpu.SemaphoreType.DMA((len(cut(units, FEED_TILE)), 3)),
            pltpu.SemaphoreType.DMA((5,)),
        ],
        compiler_params=params(60),
        cost_estimate=cost(TUNE["feed_forward"]),
        name="feed_forward",
    )(own, gain, x, *cot_parts, *mixed_parts, near, other, joined_all)


def down_product_kernel(others, down_w, middle_ref, *refs):
    refs = refs[others:]
    acc = refs[-1]
    step = pl.program_id(0)

    @pl.when(step == 0)
    def _():
        acc[...] = jnp.zeros(acc.shape, F32)

    acc[...] += dot_nt(middle_ref[...], down_w[...])

    @pl.when(step == pl.num_programs(0) - 1)
    def _():
        store_rows(refs[:-1], slice(None), acc)


def down_product(middle, joined_all, tok_rows, others):
    rows, units = middle.shape
    full = joined_all.shape[0]
    steps = units // TILE
    outs = row_shapes(tok_rows, full)
    return pl.pallas_call(
        functools.partial(down_product_kernel, len(others)),
        grid=(steps,),
        in_specs=[
            pl.BlockSpec((full, TILE), lambda i: (0, 2 * steps + i)),
            pl.BlockSpec((rows, TILE), lambda i: (0, i)),
        ]
        + [anywhere()] * len(others),
        out_specs=[fixed(out.shape) for out in outs],
        out_shape=outs,
        scratch_shapes=[pltpu.VMEM((rows, full), F32)],
        compiler_params=params(60),
        cost_estimate=cost(TUNE["down_product"]),
        name="down_product",
    )(joined_all, middle, *others)


def wide_grads_kernel(x_ref, acts_ref, out_ref, turned):
    @pl.when(pl.program_id(0) == 0)
    def _():
        turned[...] = jnp.transpose(x_ref[...])

    out_ref[...] = dot_nn(turned[...], acts_ref[...]).astype(BF)


def wide_grads(acts, width):
    rows = acts.shape[0]
    units = acts.shape[1] - width
    return pl.pallas_call(
        wide_grads_kernel,
        grid=(units // TILE,),
        in_specs=[
            pl.BlockSpec((rows, width), lambda i: (0, units // width)),
            pl.BlockSpec((rows, TILE), lambda i: (0, i)),
        ],
        out_specs=pl.BlockSpec((width, TILE), lambda i: (0, i)),
        out_shape=shape_of((width, units)),
        scratch_shapes=[pltpu.VMEM((width, rows), BF)],
        compiler_params=params(60),
        cost_estimate=cost(TUNE["wide_grads"]),
        name="wide_grads",
    )(acts, acts)


def pair_grads_kernel(orders, others, own_ref, *refs):
    cots, middles = refs[:2], refs[2:4]
    outs = refs[4 + others : -2]
    one, two, turned = refs[-3:]
    count = len(outs) // 2
    blocks = len(orders[0])
    rows = one.shape[0] // blocks
    tokens = cots[0].shape[0]
    cols = outs[0].shape[1]
    for side, cot_ref in enumerate(cots):
        turned[side] = jnp.transpose(cot_ref[...])
        for left, order in ((one, orders[0]), (two, orders[1])):
            for j in range(blocks):
                at = pl.multiple_of((own_ref[0] ^ order[j]) * rows, 16)
                left[j * rows : (j + 1) * rows, side * tokens : (side + 1) * tokens] = turned[
                    side, pl.ds(at, rows), :
                ]
    for which, left in enumerate((one, two)):
        here = slice(which * cols, (which + 1) * cols)
        result = dot_nn(left[:, :tokens], middles[0][:, here]) + dot_nn(left[:, tokens:], middles[1][:, here])
        store_rows(outs[which * count : (which + 1) * count], slice(None), result)


def pair_grads(own, orders, cots, middles, others):
    rows, full = cots[0].shape
    cols = middles[0].shape[1] // 2
    outs = [shape_of((n, cols)) for n in (full // 8, full // 8, full // 4)] * 2
    return pl.pallas_call(
        functools.partial(pair_grads_kernel, orders, len(others)),
        in_specs=[smem()] + [vmem()] * 4 + [anywhere()] * len(others),
        out_specs=[vmem()] * 6,
        out_shape=outs,
        scratch_shapes=[pltpu.VMEM((full // 2, 2 * rows), BF)] * 2 + [pltpu.VMEM((2, full, rows), BF)],
        compiler_params=params(60),
        cost_estimate=cost(TUNE["pair_grads"]),
        name="pair_grads",
    )(own, *cots, *middles, *others)


def norm_back_kernel(others, own_ref, *refs):
    near_w, other_w = refs[6:8]
    refs = refs[:6] + refs[8 + others :]
    first_ref, down_ref, up_ref, hidden_ref, gain_ref, cot_ref, dh_ref, branch_ref = refs[:8]
    mixed_refs = refs[8:-3]
    gain_grad_ref, out_v, sem = refs[-3:]
    copies = start_blocks(own_ref, near_w, other_w, out_v, sem)
    grad = first_ref[...] + down_ref[...].astype(F32) + up_ref[...].astype(F32)
    hidden = hidden_ref[...]
    inv = inverse_norm(hidden)
    scaled = grad * gain_ref[...]
    gain_grad_ref[...] = jnp.sum(grad * (hidden * inv), axis=0, keepdims=True)
    inner = jnp.mean(scaled * hidden, axis=-1, keepdims=True)
    d_hidden = cot_ref[...].astype(F32) + inv * scaled - hidden * (inv * inv * inv * inner)
    dh_ref[...] = d_hidden
    branch_ref[...] = d_hidden.astype(BF)
    for copy in copies:
        copy.wait()
    d_mixed = dot_nn(branch_ref[...], out_v[...]).astype(BF)
    cols = mixed_refs[0].shape[1]
    for t, ref in enumerate(mixed_refs):
        ref[...] = d_mixed[:, t * cols : (t + 1) * cols]


def norm_back(own, first, down, up, hidden, gain, cotangent, near, other, blocks, others):
    rows, width = hidden.shape
    return pl.pallas_call(
        functools.partial(norm_back_kernel, len(others)),
        in_specs=[smem()] + [vmem()] * 6 + [anywhere()] * (2 + len(others)),
        out_specs=[vmem()] * (3 + blocks),
        out_shape=[shape_of((rows, width), F32), shape_of((rows, width))]
        + [shape_of((rows, QD // blocks))] * blocks
        + [shape_of((1, width), F32)],
        scratch_shapes=[
            pltpu.VMEM((width, QD), BF),
            pltpu.SemaphoreType.DMA((2, near.shape[0])),
        ],
        compiler_params=params(60),
        cost_estimate=cost(TUNE["norm_back"]),
        name="norm_back",
    )(own, first, down, up, hidden, gain, cotangent, near, other, *others)


def per_device(
    inputs,
    norm_gain_attn,
    qkv_weight,
    qkv_bias,
    out_weight,
    norm_gain_mlp,
    gate_weight,
    up_weight,
    down_weight,
    cotangent,
    segment_ids,
    positions,
):
    tok_rows = inputs.shape[0]
    width = inputs.shape[1]
    seq_dev = lax.axis_size("seq")
    heads_dev = lax.axis_size("head")
    heads_here = HEADS // heads_dev
    copies = heads_dev // KV_HEADS
    group_rows = heads_dev * tok_rows
    half_rows = group_rows // 2
    query_cols = heads_here * HD
    head_index = lax.axis_index("head")
    seq_index = lax.axis_index("seq")
    odd = head_index % 2 == 1
    seq_bits = bits_of("seq")
    head_bits = bits_of("head")
    far = seq_dev // 2
    bits_down = list(range(seq_bits - 1, 0, -1))
    bits_up = bits_down[::-1]
    orders = (masks_of(bits_down), masks_of(bits_up))
    seq_own = seq_index.astype(jnp.int32).reshape(1)
    head_own = head_index.astype(jnp.int32).reshape(1)

    units = gate_weight.shape[1]
    padded = -(-units // TILE) * TILE
    joined = jnp.concatenate(
        [
            jnp.pad(part, ((0, 0), (0, padded - units)))
            for part in (gate_weight, up_weight, down_weight.T)
        ],
        axis=1,
    )
    joined_all = plain(lax.all_gather(plain(joined), "seq", axis=0, tiled=True))


    gain_cols = norm_gain_attn.shape[0]
    bias_cols = qkv_bias.shape[0]
    cols_here = query_cols + 2 * HD
    small = jnp.concatenate(
        [
            norm_gain_attn,
            norm_gain_mlp,
            qkv_bias,
            (positions >> 7).astype(BF),
            (positions & 127).astype(BF),
            segment_ids.astype(BF),
        ]
    )
    small_row = jnp.pad(small[None], ((0, MORE_ROWS - 1), (0, cols_here - small.shape[0])))

    def head_columns(values, head):
        last = values.ndim - 1
        slot = head // copies
        return [
            lax.dynamic_slice_in_dim(values, head * query_cols, query_cols, last),
            lax.dynamic_slice_in_dim(values, QD + slot * HD, HD, last),
            lax.dynamic_slice_in_dim(values, QD + KD + slot * HD, HD, last),
        ]

    own_wide = qkv_weight.shape[0]
    own_rows = own_wide * heads_dev
    rows_of = []
    for apart in range(heads_dev):
        target = (head_index - apart) % heads_dev
        block = jnp.concatenate(head_columns(qkv_weight, target), axis=1)
        block = jnp.concatenate([block, small_row])
        rows_of.append(from_next(block, "head", apart) if apart else block)
    inputs_parts = gather_blocks(tie(inputs, *rows_of[1:]), "head", micros=TUNE["x1"])
    cols_own = arrange(head_own, rows_of)
    small_grp = cols_own[own_rows : own_rows + heads_dev]
    cols_near, _ = far_last(cols_own, far_first(cols_own, "seq"), "seq")
    inputs_parts[2:4] = tie_all(inputs_parts[2:4], micros=TUNE["x2"])
    cols_other = swap(tie(cols_near, *inputs_parts[2:4]), "seq", 0)

    def cut_small(values):
        cuts, start = [], 0
        for size in (gain_cols, gain_cols, bias_cols, tok_rows, tok_rows, tok_rows):
            cuts.append(values[..., start : start + size])
            start += size
        return cuts

    def places(cuts):
        pos = (cuts[3].astype(jnp.int32) << 7) + cuts[4].astype(jnp.int32)
        pos = roll_blocks(pos, head_index, pos.ndim - 2)
        seg = roll_blocks(cuts[5].astype(jnp.int32), head_index, pos.ndim - 2)
        return pos, seg * SEG_STEP + pos

    small_all = jnp.concatenate(
        [part[:, own_rows : own_rows + heads_dev] for part in (cols_near, cols_other)]
    )
    cuts = cut_small(small_all)
    _, key_code = places(cuts)
    query_pos, query_code = places(cut_small(small_grp))
    query_pos = query_pos.reshape(-1)

    def in_order(values):
        masks = [seq_index ^ j for j in range(seq_dev)]
        return jnp.stack(
            [
                lax.dynamic_index_in_dim(values, (m & 1) * far + (m >> 1), 0, keepdims=False)
                for m in masks
            ]
        ).reshape(-1)

    gain_attn = in_order(cuts[0]).reshape(1, -1).astype(F32)
    gain_mlp = in_order(cuts[1]).reshape(1, -1).astype(F32)

    def halves_first(values):
        tail = values.shape[1:]
        return jnp.swapaxes(
            values.reshape((heads_dev, 2, tok_rows // 2) + tail), 0, 1
        ).reshape((2, half_rows) + tail)

    query_code = jnp.broadcast_to(
        halves_first(query_code.reshape(-1))[:, None, None, :], (2, 1, heads_here, half_rows)
    ).reshape(2, 1, heads_here * half_rows)
    key_code = jnp.swapaxes(
        key_code.reshape(seq_dev, heads_dev, 2, tok_rows // 2), 1, 2
    ).reshape(seq_dev, 2, half_rows, 1)
    freq_index = jnp.arange(HD // 2, dtype=F32) * 2.0 / HD
    angles = query_pos.astype(F32)[:, None] * (1.0 / ROPE_BASE**freq_index)[None, :]
    cosine, sine = jnp.cos(angles), jnp.sin(angles)
    cosine_part = jnp.concatenate([cosine, cosine], axis=1)
    sine_part = jnp.concatenate([-sine, sine], axis=1)

    queries, kv_own, inputs_grp, normed_one, cols_weight = project(
        seq_own,
        head_own,
        inputs_parts,
        cosine_part,
        sine_part,
        cols_near,
        cols_other,
        heads_here,
        gain_cols,
        bias_cols,
    )
    half = tok_rows // 2
    out_flat = out_weight.reshape(-1, width)
    out_half = out_flat.shape[0] // 2
    out_pad = -out_half % 16
    cot_mixed = jnp.concatenate(
        [
            part
            for i in range(2)
            for part in (
                cotangent[i * half : (i + 1) * half],
                jnp.pad(out_flat[i * out_half : (i + 1) * out_half], ((0, out_pad), (0, 0))),
            )
        ]
    )
    cot_late = tie(plain(cot_mixed), inputs_parts[2], inputs_parts[3])
    kv_first = far_first(kv_own, "seq")
    cot_parts = gather_blocks(cot_late, "head", kv_first)
    kv_near, _ = far_last(kv_own, kv_first, "seq")
    cot_parts[2:4] = tie_all(cot_parts[2:4], micros=TUNE["c2"])
    kv_other = swap(kv_near, "seq", 0)

    mixed, mixed_wide, log_total = attend(
        queries, kv_near, kv_other, key_code, query_code, tok_rows, cot_parts[2:4]
    )
    late = tie_all([cot_mixed, *cot_parts[1:]], mixed)
    halves = jnp.concatenate(late).reshape(2 * heads_dev, half + out_half + out_pad, width)
    out_rows = plain(halves[:, half : half + out_half].reshape(QD, -1).T)
    out_first = far_first(out_rows, "seq")
    mixed_parts = gather_blocks(mixed, "head", micros=TUNE["mx"])
    out_near, _ = far_last(out_rows, out_first, "seq", [mixed_parts[1], mixed_parts[3]])
    out_other = swap(tie(out_near, *mixed_parts[2:4]), "seq", 0)

    acts, own_hidden, middle, cot_grp, *d_two = feed_forward(
        seq_own,
        inputs_grp,
        gain_mlp,
        cot_parts,
        mixed_parts,
        out_near,
        out_other,
        joined_all,
        tok_rows,
    )

    cots, middles = [[part, swap(part, "seq", 0)] for part in (cot_grp, middle)]
    moved = from_next(d_two[2], "head")
    up = to_next(d_two[1], "head")
    wide_term = wide_grads(acts, width)
    wide_late = tie(wide_term, moved)
    down = sum_payload(d_two[3], moved, others=[cots[1], middles[1]])
    wide_sum = plain(lax.psum_scatter(plain(wide_late), "seq", scatter_dimension=0, tiled=True))
    out_term = down_product(middle, joined_all, tok_rows, [down])
    one_low, one_high, one_sent, two_low, two_high, two_sent = [
        part.reshape(-1, width // seq_dev, part.shape[1])
        for part in pair_grads(seq_own, orders, cots, middles, [down])
    ]
    d_hidden, d_branch, *d_mixed_own, grad_gain_two = norm_back(
        seq_own,
        d_two[0],
        from_next(down, "head"),
        up,
        own_hidden,
        gain_mlp,
        cotangent,
        out_near,
        out_other,
        heads_dev,
        [one_low, out_term[0]],
    )
    d_mixed = [d_mixed_own[0]]
    for apart in range(1, heads_dev):
        d_mixed.append(from_next(d_mixed_own[heads_dev - apart], "head", apart))

    one_moved = swap(one_sent, "seq", bits_down[0])
    two_moved = swap(two_sent, "seq", bits_up[0])
    branch_late = tie(d_branch, *d_mixed[1:])
    above, below = from_next(branch_late, "head"), to_next(branch_late, "head")
    d_queries, d_kv_own, d_kv_sent = attend_back(
        queries,
        d_mixed,
        mixed_wide,
        kv_near,
        kv_other,
        key_code,
        query_code,
        log_total,
        [],
    )
    d_kv_moved = swap(tie(d_kv_sent, above, below), "seq", 0)
    half = tok_rows // 2
    above, below = tie_all([above, below], d_queries)
    out_up = to_next(tie(out_term[1], *d_mixed[1:]), "head")
    far_both = from_next(jnp.concatenate([above, out_term[2]]), "head")
    far_both = tie_all([far_both], micros=TUNE["far"])[0]
    branch_parts = [d_branch, above, far_both, below]
    down = sum_payload(out_term[3], far_both[tok_rows:], others=[out_up])
    out_moved = [from_next(down, "head"), out_up]
    one_moved, two_moved = tie_all([one_moved, two_moved], micros=TUNE["g1"])
    d_kv_moved = tie(d_kv_moved, one_moved, two_moved)
    d_kv = total([d_kv_own, d_kv_moved])
    d_keys, keys_last = sum_xor([d_kv[i, 0] for i in range(far)], "seq", bits_down)
    d_values, values_last = sum_xor([d_kv[i, 1] for i in range(far)], "seq", bits_up)
    d_other_raw = jnp.where(odd, d_keys, d_values).astype(BF)
    d_other_sent = d_other_raw
    d_other_raw = swap(d_other_sent, "head", 0)
    d_other = d_other_raw.reshape(2, heads_dev, tok_rows // 2, HD)
    d_other = roll_blocks(d_other, jnp.where(odd, 1, heads_dev - 1), 1).reshape(2, half_rows, HD)
    d_kv_total = jnp.where(odd, d_values, d_keys) + d_other.astype(F32)


    def second(low, high, moved, bit):
        half = high.shape[0]
        moved = tie(moved, d_other_sent)
        return [low, moved[:half], swap(total([high, moved[half:]]).astype(BF), "seq", bit)]

    one_terms = second(one_low, one_high, one_moved, bits_down[1])
    two_terms = second(two_low, two_high, two_moved, bits_up[1])
    one_terms[-1], two_terms[-1] = tie_all([one_terms[-1], two_terms[-1]], micros=TUNE["s2"])
    *d_one, cols_kept, outs_kept, wide_sent = project_back(
        seq_own,
        head_own,
        orders,
        d_queries,
        d_kv_total,
        cosine_part,
        sine_part,
        normed_one,
        inputs_grp,
        cols_weight,
        mixed,
        branch_parts,
        grad_gain_two,
        out_moved,
    )
    ahead, across = tie_all(d_one[1:3], one_terms[-1], two_terms[-1])
    moved = from_next(across, "head")
    up = to_next(ahead, "head")
    wide_moved = tie_all([swap(wide_sent, "seq", 0)], micros=TUNE["wm"])[0]
    down = sum_payload(d_one[3], moved, others=[wide_moved, up])
    one_terms[-1], two_terms[-1] = tie(one_terms[-1], down), tie(two_terms[-1], down)
    output = total([own_hidden, out_term[0], *out_moved]).astype(BF)
    cols_moved = wide_moved[:, :, : query_cols + HD]
    outs_moved = wide_moved[:, :own_rows, query_cols + HD :]
    cols_terms = sum_step([cols_kept, cols_moved], "seq", bits_down[0])
    outs_terms = sum_step([outs_kept, outs_moved], "seq", bits_up[0])
    cols_terms[-1], outs_terms[-1] = tie_all([cols_terms[-1], outs_terms[-1]], micros=TUNE["ct"])
    down = from_next(down, "head")
    d_normed_one = total([d_one[0], tie(down, cols_terms[-1], outs_terms[-1]), up])
    grad_cols = sum_halving(cols_terms, "seq", bits_down[1:]).astype(BF)
    grad_outs = sum_halving(outs_terms, "seq", bits_up[1:])
    inputs_f = inputs.astype(F32)
    inv_one = inverse_norm(inputs_f)
    scaled = d_normed_one * gain_attn
    inner = jnp.mean(scaled * inputs_f, axis=-1, keepdims=True)
    grad_inputs = (d_hidden + inv_one * scaled - inputs_f * (inv_one**3 * inner)).astype(BF)

    grad_out = grad_outs.T
    cols_wide = query_cols + HD
    more_rows = jnp.broadcast_to(grad_cols[own_rows:], (heads_dev, MORE_ROWS, cols_wide))
    grad_blocks = jnp.concatenate(
        [grad_cols[:own_rows].reshape(heads_dev, own_wide, cols_wide), more_rows], axis=1
    )
    grad_qkv = jnp.zeros((own_wide, QKV), F32)
    small_parts = []
    for apart in range(heads_dev):
        source = (head_index + apart) % heads_dev
        target = (head_index - apart) % heads_dev
        block = lax.dynamic_index_in_dim(grad_blocks, target, 0, keepdims=False)
        if apart:
            block = from_next(tie(block, wide_sum), "head", apart)
        small_parts.append(block[own_wide : own_wide + 2])
        block = block[:own_wide].astype(F32)
        kv_place = QD + source % 2 * KD + source // copies * HD
        grad_qkv = lax.dynamic_update_slice_in_dim(
            grad_qkv, block[:, :query_cols], source * query_cols, 1
        )
        grad_qkv = lax.dynamic_update_slice_in_dim(grad_qkv, block[:, query_cols:], kv_place, 1)
    small_grads = total(small_parts)

    def own_part(row, start, size):
        return lax.dynamic_slice(small_grads, (row, start + head_index * size), (1, size)).reshape(size)

    key_bias = (QD + KD) // (seq_dev * heads_dev)
    value_bias = KD // (seq_dev * heads_dev)

    grad_down = jnp.concatenate(
        [
            sum_halving(one_terms, "seq", bits_down[2:]),
            sum_halving(two_terms, "seq", bits_up[2:]),
        ],
        axis=1,
    )[:, :units].T

    return (
        output,
        grad_inputs,
        own_part(0, 0, gain_cols),
        grad_qkv,
        own_part(1, 0, key_bias),
        own_part(1, heads_dev * key_bias, value_bias),
        grad_out,
        own_part(0, heads_dev * gain_cols, gain_cols),
        wide_sum[:, :units].astype(F32),
        wide_sum[:, padded : padded + units].astype(F32),
        grad_down,
    )


def solution(mesh):
    both = ("seq", "head")
    in_specs = (
        P(both, None),
        P(both),
        P(both, None),
        P(both),
        P("head", "seq"),
        P(both),
        P("seq", "head"),
        P("seq", "head"),
        P("head", "seq"),
        P(both, None),
        P(both),
        P(both),
    )
    out_specs = (
        P(both, None),
        P(both, None),
        P(both),
        P(both, None),
        P(both),
        P(both),
        P("head", "seq"),
        P(both),
        P("seq", "head"),
        P("seq", "head"),
        P("head", "seq"),
    )
    return jax.shard_map(
        per_device, mesh=mesh, in_specs=in_specs, out_specs=out_specs, check_vma=False
    )
```

```python
import functools
import math

import jax
import jax.numpy as jnp
from jax import lax
from jax.experimental import pallas as pl
from jax.experimental.layout import Layout, with_layout_constraint
from jax.experimental.pallas import tpu as pltpu
from jax.sharding import PartitionSpec as P

HEADS = 12
KV_HEADS = 2
HD = 128
MORE_ROWS = 16
QD = 1536
KD = 256
QKV = 2048


EPS = 1e-06
ROPE_BASE = 1000000.0
MASKED = -1e30
LOWEST = -1e29
SEG_STEP = 1 << 20
TILE = 768
MIB = 2**20

TUNE = dict(x1=10, x2=30, mx=10, c2=8, g1=25, wm=0, ct=0, s2=20, project=7, project_back=9, attend=16, attend_back=18, feed_forward=36, down_product=8, pair_grads=7, wide_grads=11, norm_back=5.5, payload=2, far=25)

BF = jnp.bfloat16
F32 = jnp.float32


def plain(values):
    return with_layout_constraint(values, Layout(major_to_minor=tuple(range(values.ndim))))


def bits_of(axis):
    return (lax.axis_size(axis) - 1).bit_length()


def bit_value(axis, bit):
    return (lax.axis_index(axis) >> bit) & 1


def send(block, axis, target):
    count = lax.axis_size(axis)
    return plain(lax.ppermute(plain(block), axis, [(j, target(j) % count) for j in range(count)]))


def swap(block, axis, bit):
    return send(block, axis, lambda j: j ^ (1 << bit))


def from_next(block, axis, apart=1):
    return send(block, axis, lambda j: j - apart)


def to_next(block, axis):
    return send(block, axis, lambda j: j + 1)


def tie_kernel(*refs):
    del refs


def tie_all(blocks, *others, micros=0):
    count = len(blocks)
    return pl.pallas_call(
        tie_kernel,
        in_specs=[pl.BlockSpec(memory_space=pl.ANY)] * (count + len(others)),
        out_specs=[pl.BlockSpec(memory_space=pl.ANY)] * count,
        out_shape=[jax.ShapeDtypeStruct(block.shape, block.dtype) for block in blocks],
        input_output_aliases={i: i for i in range(count)},
        compiler_params=pltpu.CompilerParams(
            vmem_limit_bytes=60 * MIB if max(block.size for block in blocks) > MIB else MIB
        ),
        cost_estimate=cost(micros),
        name="tie",
    )(*blocks, *others)


def tie(block, *others):
    return tie_all([block], *others)[0]


def gather_blocks(block, axis, last=(), micros=0):
    above = from_next(block, axis)
    below = to_next(block, axis)
    above, below = tie_all([above, below], *last, micros=micros)
    return [block, above, from_next(above, axis), below]


def payload_kernel(behind_ref, moved_ref, *refs):
    refs[-1][...] = (behind_ref[...].astype(F32) + moved_ref[...].astype(F32)).astype(BF)


def sum_payload(behind, moved, others=()):
    return pl.pallas_call(
        payload_kernel,
        in_specs=[vmem()] * 2 + [anywhere()] * len(others),
        out_specs=vmem(),
        out_shape=shape_of(behind.shape),
        compiler_params=params(16),
        cost_estimate=cost(TUNE["payload"]),
        name="payload",
    )(behind, moved, *others)


def far_first(block, axis):
    return swap(block, axis, 1), swap(block, axis, 2)


def far_last(block, first, axis, last=()):
    count = lax.axis_size(axis) // 2
    one, two = tie_all(first, *last)
    if count == 4:
        half = block.shape[0] // 2
        parts = [swap(one[:half], axis, 2), swap(two[half:], axis, 1)]
        blocks = [block, one, two, jnp.concatenate(parts)]
    else:
        more = [send(block, axis, lambda j: j ^ 2 * i) for i in range(3, count)]
        blocks, parts = [block, one, two, *more], [one]
    return plain(jnp.stack(blocks)), parts


def total(terms):
    result = terms[0].astype(F32)
    for term in terms[1:]:
        result = result + term.astype(F32)
    return result


def sum_step(terms, axis, bit, last=()):
    half = terms[0].shape[0] // 2
    sent = total([term[half:] for term in terms]).astype(BF)
    moved = swap(tie(sent, *last) if last else sent, axis, bit)
    return [term[:half] for term in terms] + [moved]


def sum_halving(terms, axis, bits):
    for bit in bits:
        terms = sum_step(terms, axis, bit)
    return total([term[0] for term in terms])


def sum_xor(blocks, axis, bits):
    blocks = dict(enumerate(blocks))
    for bit in bits:
        place = 1 << bit - 1
        sent = [m for m in sorted(blocks) if m & place]
        moved = swap(jnp.stack([blocks[m].astype(BF) for m in sent]), axis, bit)
        for i, m in enumerate(sent):
            blocks[m ^ place] = blocks[m ^ place] + moved[i].astype(F32)
            del blocks[m]
    return blocks[0], moved


def roll_blocks(stacked, shift, axis=0):
    count = stacked.shape[axis]
    return lax.dynamic_slice_in_dim(
        jnp.concatenate([stacked, stacked], axis=axis), shift, count, axis
    )


def dot_nn(left, right):
    return jnp.dot(left, right, preferred_element_type=F32)


def dot_nt(left, right):
    return lax.dot_general(left, right, (((1,), (1,)), ((), ())), preferred_element_type=F32)


def dot_tn(left, right):
    return lax.dot_general(left, right, (((0,), (0,)), ((), ())), preferred_element_type=F32)


def inverse_norm(values):
    return lax.rsqrt(jnp.mean(values * values, axis=-1, keepdims=True) + EPS)


def vmem():
    return pl.BlockSpec(memory_space=pltpu.VMEM)


def smem():
    return pl.BlockSpec(memory_space=pltpu.SMEM)


def anywhere():
    return pl.BlockSpec(memory_space=pl.ANY)


def shape_of(shape, dtype=BF):
    return jax.ShapeDtypeStruct(shape, dtype)


def fixed(shape):
    return pl.BlockSpec(shape, lambda *i: (0,) * len(shape))


def params(mib):
    return pltpu.CompilerParams(vmem_limit_bytes=mib * MIB)


def cost(micros):
    return pl.CostEstimate(flops=int(micros * 1153e6), bytes_accessed=0, transcendentals=0)


def cut(size, tile):
    return [(at, min(tile, size - at)) for at in range(0, size, tile)]


def start_blocks(own_ref, near_ref, other_ref, to_ref, sem):
    count = near_ref.shape[0]
    rows = to_ref.shape[0] // (2 * count)
    copies = []
    for side, source in enumerate((near_ref, other_ref)):
        for i in range(count):
            at = pl.multiple_of((own_ref[0] ^ (2 * i + side)) * rows, 16)
            copy = pltpu.make_async_copy(
                source.at[i, pl.ds(0, rows), :], to_ref.at[pl.ds(at, rows), :], sem.at[side, i]
            )
            copy.start()
            copies.append(copy)
    return copies


def masks_of(bits):
    masks = [0]
    for bit in bits[::-1]:
        masks += [mask | 1 << bit for mask in masks]
    return masks


def store_rows(refs, cols, values):
    at = 0
    for ref in refs:
        ref[:, cols] = values[at : at + ref.shape[0], :].astype(ref.dtype)
        at += ref.shape[0]


def row_shapes(tok_rows, width):
    return [shape_of((tok_rows, width), F32)] + [shape_of((tok_rows, width))] * 3


def fill_rows(to_ref, parts):
    size = parts[0].shape[0]
    for t, part in enumerate(parts):
        to_ref[t * size : (t + 1) * size, :] = part[:size, :]


def head_rows(tok_rows, blocks):
    half_block = tok_rows // 2
    return [
        (half, u * half_block, u * tok_rows + half * half_block, half_block)
        for u in range(blocks)
        for half in range(2)
    ]


def arrange_kernel(head_ref, *refs):
    to_ref = refs[-1]
    count = len(refs) - 1
    rows = refs[0].shape[0] - MORE_ROWS
    line = lax.broadcasted_iota(jnp.int32, (MORE_ROWS, to_ref.shape[1]), 0)
    small = jnp.zeros(line.shape, F32)
    for apart, ref in enumerate(refs[:-1]):
        place = lax.rem(head_ref[0] + apart, count)
        to_ref[pl.ds(pl.multiple_of(place * rows, rows), rows), :] = ref[:rows, :]
        small = jnp.where(line == place, ref[rows : rows + 1, :].astype(F32), small)
    to_ref[count * rows : count * rows + MORE_ROWS, :] = small.astype(BF)
    to_ref[count * rows + MORE_ROWS :, :] = jnp.zeros(line.shape, BF)


def arrange(head, blocks):
    rows, cols = blocks[0].shape
    if (rows - MORE_ROWS) % 16:
        count = len(blocks)
        ordered = roll_blocks(jnp.stack(blocks), (count - head[0]) % count)
        small = jnp.pad(ordered[:, rows - MORE_ROWS], ((0, 2 * MORE_ROWS - count), (0, 0)))
        return jnp.concatenate([ordered[:, : rows - MORE_ROWS].reshape(-1, cols), small])
    return pl.pallas_call(
        arrange_kernel,
        in_specs=[smem()] + [vmem()] * len(blocks),
        out_specs=vmem(),
        out_shape=shape_of((len(blocks) * (rows - MORE_ROWS) + 2 * MORE_ROWS, cols)),
        compiler_params=params(60),
        cost_estimate=cost(1),
        name="arrange",
    )(head, *blocks)


def project_kernel(heads, gain_cols, bias_cols, own_ref, head_ref, *refs):
    parts = refs[:4]
    cos_ref, sin_ref, near, other = refs[4:8]
    q_ref, kv_ref, x_ref, normed_ref, w_ref, small_v, gain_v, all_v, bias_v, sem, small_sem = refs[8:]
    rows = w_ref.shape[0] // small_v.shape[0]
    smalls = []
    for side, source in enumerate((near, other)):
        for i in range(source.shape[0]):
            copy = pltpu.make_async_copy(
                source.at[i, pl.ds(rows, MORE_ROWS), :],
                small_v.at[own_ref[0] ^ (2 * i + side)],
                small_sem.at[side, i],
            )
            copy.start()
            smalls.append(copy)
    copies = start_blocks(own_ref, near, other, w_ref, sem)
    for copy in smalls:
        copy.wait()
    devices = gain_v.shape[1] // gain_cols
    per = devices // small_v.shape[0]
    for d in range(devices):
        row = small_v[d // per, d % per : d % per + 1, :].astype(F32)
        gain_v[:, d * gain_cols : (d + 1) * gain_cols] = row[:, :gain_cols]
        all_v[:, d * bias_cols : (d + 1) * bias_cols] = row[:, 2 * gain_cols : 2 * gain_cols + bias_cols]
    head = head_ref[0]
    last = heads * HD
    slot = (head // ((QD // last) // KV_HEADS)) * HD
    bias_v[:, :last] = all_v[:, pl.ds(pl.multiple_of(head * last, HD), last)]
    bias_v[:, last : last + HD] = all_v[:, pl.ds(pl.multiple_of(QD + slot, HD), HD)]
    bias_v[:, last + HD :] = all_v[:, pl.ds(pl.multiple_of(QD + KD + slot, HD), HD)]
    fill_rows(x_ref, parts)
    values = x_ref[...].astype(F32)
    normed_ref[...] = (values * inverse_norm(values) * gain_v[...]).astype(BF)
    for copy in copies:
        copy.wait()
    joint = dot_nn(normed_ref[...], w_ref[...]) + bias_v[...]
    tok_rows = parts[0].shape[0]
    blocks = x_ref.shape[0] // tok_rows
    half_rows = x_ref.shape[0] // 2
    for j in range(heads + 2):
        part = joint[:, j * HD : (j + 1) * HD]
        if j <= heads:
            part = part * cos_ref[...] + pltpu.roll(part, HD // 2, 1) * sin_ref[...]
        part = part.astype(BF)
        for half, low, row, count in head_rows(tok_rows, blocks):
            piece = part[row : row + count]
            if j < heads:
                q_ref[half, j * half_rows + low : j * half_rows + low + count, :] = piece
            else:
                kv_ref[j - heads, half, low : low + count, :] = piece


def project(own, head, parts, cos, sin, near, other, heads, gain_cols, bias_cols):
    width = parts[0].shape[1]
    rows = cos.shape[0]
    cols = near.shape[2]
    return pl.pallas_call(
        functools.partial(project_kernel, heads, gain_cols, bias_cols),
        in_specs=[smem()] * 2 + [vmem()] * 6 + [anywhere()] * 2,
        out_specs=[vmem()] * 5,
        out_shape=[
            shape_of((2, heads * rows // 2, HD)),
            shape_of((2, 2, rows // 2, HD)),
            shape_of((rows, width)),
            shape_of((rows, width)),
            shape_of((width, cols)),
        ],
        scratch_shapes=[
            pltpu.VMEM((2 * near.shape[0], MORE_ROWS, cols), BF),
            pltpu.VMEM((1, width), F32),
            pltpu.VMEM((1, QKV), F32),
            pltpu.VMEM((1, cols), F32),
            pltpu.SemaphoreType.DMA((2, near.shape[0])),
            pltpu.SemaphoreType.DMA((2, near.shape[0])),
        ],
        compiler_params=params(60),
        cost_estimate=cost(TUNE["project"]),
        name="project",
    )(own, head, *parts, cos, sin, near, other)


def project_back_kernel(heads, orders, others, own_ref, head_ref, *refs):
    refs = refs[:13] + refs[13 + others :]
    dq_ref, dkv_ref, cos_ref, sin_ref, normed_ref, x_ref, w_ref, mixed_ref = refs[:8]
    parts = refs[8:12]
    gain_two_ref = refs[12]
    dn_refs = refs[13:17]
    cols_kept, outs_kept, wide_sent = refs[17:20]
    cols, branch, wide, wide_out, bias_v, small_v = refs[20:]
    rows = cos_ref.shape[0]
    half_rows = rows // 2
    tok_rows = parts[0].shape[0]
    blocks = rows // tok_rows
    head = head_ref[0]
    odd = (head & 1) == 1
    for half, low, row, count in head_rows(tok_rows, blocks):
        here = slice(row, row + count)
        for j in range(heads + 1):
            if j < heads:
                start = j * half_rows + low
                part = dq_ref[half, start : start + count, :]
            else:
                part = dkv_ref[half, low : low + count, :]
            part = part.astype(BF).astype(F32)
            turned = part * cos_ref[here, :] - pltpu.roll(part, HD // 2, 1) * sin_ref[here, :]
            if j == heads:
                turned = jnp.where(odd, part, turned)
            cols[here, j * HD : (j + 1) * HD] = turned.astype(BF)
    last = heads * HD
    bias = jnp.sum(cols[...].astype(F32), axis=0, keepdims=True)
    bias_v[...] = jnp.zeros(bias_v.shape, F32)
    bias_v[:, pl.ds(pl.multiple_of(head * last, HD), last)] = bias[:, :last]
    copies = (QD // last) // KV_HEADS
    slot = QD + (head & 1) * KD + (head // copies) * HD
    bias_v[:, pl.ds(pl.multiple_of(slot, HD), HD)] = bias[:, last:]
    key_w = jnp.where(odd, w_ref[:, last + HD :], w_ref[:, last : last + HD])
    grad = dot_nt(cols[:, :last], w_ref[:, :last]) + dot_nt(cols[:, last:], key_w)
    store_rows(dn_refs, slice(None), grad)
    values = x_ref[...].astype(F32)
    gain_one = jnp.sum(grad * (values * inverse_norm(values)), axis=0, keepdims=True)
    seq_dev = small_v.shape[0]
    small_v[...] = jnp.zeros(small_v.shape, BF)
    for row, vectors in enumerate(
        ((gain_one, gain_two_ref[...]), (bias_v[:, : QD + KD], bias_v[:, QD + KD :]))
    ):
        for i in range(seq_dev):
            at = 0
            for vector in vectors:
                size = vector.shape[1] // seq_dev
                small_v[i, row : row + 1, at : at + size] = vector[:, i * size : (i + 1) * size].astype(BF)
                at += size
    count = outs_kept.shape[1]
    fill_rows(branch, parts)
    wide[...] = dot_tn(normed_ref[...], cols[...]).astype(BF)
    wide_out[...] = dot_tn(branch[...], mixed_ref[...]).astype(BF)
    split = cols.shape[1]
    wide_sent[:, count:, split:] = jnp.zeros((wide_sent.shape[0], MORE_ROWS, wide_sent.shape[2] - split), BF)
    for i in range(cols_kept.shape[0]):
        for source, order, kept, lanes in (
            (wide, orders[0], cols_kept, slice(0, split)),
            (wide_out, orders[1], outs_kept, slice(split, wide_sent.shape[2])),
        ):
            for side in range(2):
                block = own_ref[0] ^ order[i] ^ side
                rows = source[pl.ds(pl.multiple_of(block * count, 16), count), :]
                if side == 0:
                    kept[i, :count] = rows
                else:
                    wide_sent[i, :count, lanes] = rows
                if source is wide:
                    small = small_v[block]
                    if side == 0:
                        kept[i, count:] = small
                    else:
                        wide_sent[i, count:, lanes] = small


def project_back(own, head, orders, dq, dkv, cos, sin, normed, x, w, mixed, parts, gain_two, others):
    rows, width = normed.shape
    heads = dq.shape[1] // (rows // 2)
    cols = (heads + 1) * HD
    tok_rows = parts[0].shape[0]
    far = len(orders[0])
    part_rows = width // (2 * far)
    return pl.pallas_call(
        functools.partial(project_back_kernel, heads, orders, len(others)),
        in_specs=[smem()] * 2 + [vmem()] * 13 + [anywhere()] * len(others),
        out_specs=[vmem()] * 7,
        out_shape=[
            *row_shapes(tok_rows, width),
            shape_of((far, part_rows + MORE_ROWS, cols)),
            shape_of((far, part_rows, heads * HD)),
            shape_of((far, part_rows + MORE_ROWS, cols + heads * HD)),
        ],
        scratch_shapes=[
            pltpu.VMEM((rows, cols), BF),
            pltpu.VMEM((rows, width), BF),
            pltpu.VMEM((width, cols), BF),
            pltpu.VMEM((width, heads * HD), BF),
            pltpu.VMEM((1, QKV), F32),
            pltpu.VMEM((2 * far, MORE_ROWS, cols), BF),
        ],
        compiler_params=params(60),
        cost_estimate=cost(TUNE["project_back"]),
        name="project_back",
    )(own, head, dq, dkv, cos, sin, normed, x, w, mixed, *parts, gain_two, *others)


def visible_of(key_code, query_code, half):
    seen = key_code <= query_code
    if half == 1:
        seen &= key_code >= (query_code & -SEG_STEP)
    return seen


PAIRS = ((0, 0), (0, 1), (1, 1))
SEQ_STEP = 4


def pick_side(first_steps, near_ref, other_ref, which, half):
    near = near_ref[:, which, half]
    other = other_ref[:, which, half]
    block = jnp.where(pl.program_id(0) < first_steps, near, other)
    return block.reshape(block.shape[0] * block.shape[1], block.shape[2])


def codes(code_ref, half):
    block = code_ref[:, half]
    return block.reshape(block.shape[0] * block.shape[1], 1)


def attend_kernel(scale, first_steps, tok_rows, q_ref, near_ref, other_ref, kc_ref, qc_ref, *refs):
    mixed_ref, wide_ref, lse_ref, top, total, acc = refs[-6:]
    step = pl.program_id(0)

    @pl.when(step == 0)
    def _():
        top[...] = jnp.full(top.shape, LOWEST, F32)
        total[...] = jnp.zeros(total.shape, F32)
        acc[...] = jnp.zeros(acc.shape, F32)

    for key_half, query_half in PAIRS:
        keys = pick_side(first_steps, near_ref, other_ref, 0, key_half)
        values = pick_side(first_steps, near_ref, other_ref, 1, key_half)
        scores = dot_nt(keys, q_ref[query_half])
        if key_half == query_half:
            seen = visible_of(codes(kc_ref, key_half), qc_ref[query_half], key_half)
            scores = jnp.where(seen, scores, MASKED)
        old = top[query_half]
        new = jnp.maximum(old, jnp.max(scores, axis=0, keepdims=True))
        weights = jnp.exp2((scores - new) * scale)
        factor = jnp.exp2((old - new) * scale)
        top[query_half] = new
        total[query_half] = total[query_half] * factor + jnp.sum(weights, axis=0, keepdims=True)
        acc[query_half] = acc[query_half] * factor + dot_tn(values, weights.astype(BF))

    @pl.when(step == pl.num_programs(0) - 1)
    def _():
        blocks = mixed_ref.shape[0] // tok_rows
        half_rows = mixed_ref.shape[0] // 2
        for half in range(2):
            wide_ref[half] = jnp.transpose(acc[half] / total[half])
            lse_ref[half] = top[half] * scale + jnp.log2(total[half])
        for half, low, row, count in head_rows(tok_rows, blocks):
            for j in range(mixed_ref.shape[1] // HD):
                at = j * half_rows + low
                mixed_ref[row : row + count, j * HD : (j + 1) * HD] = wide_ref[
                    half, at : at + count, :
                ].astype(BF)


def side_specs(shape, first_steps):
    block = (SEQ_STEP,) + shape[1:]
    rest = (0,) * (len(shape) - 1)
    return [
        pl.BlockSpec(block, lambda i: (jnp.minimum(i, first_steps - 1),) + rest),
        pl.BlockSpec(block, lambda i: (jnp.maximum(i - first_steps, 0),) + rest),
    ]


def code_spec(shape):
    return pl.BlockSpec((SEQ_STEP,) + shape[1:], lambda i: (i,) + (0,) * (len(shape) - 1))


def attend(queries, near, other, key_code, query_code, tok_rows, others):
    _, rows, _ = queries.shape
    half_rows = near.shape[3]
    heads = rows // half_rows
    first_steps = near.shape[0] // SEQ_STEP
    return pl.pallas_call(
        functools.partial(attend_kernel, HD**-0.5 * math.log2(math.e), first_steps, tok_rows),
        grid=(2 * first_steps,),
        in_specs=[fixed(queries.shape)]
        + side_specs(near.shape, first_steps)
        + [code_spec(key_code.shape), fixed(query_code.shape)]
        + [anywhere()] * len(others),
        out_specs=[fixed((2 * half_rows, heads * HD)), fixed((2, rows, HD)), fixed((2, 1, rows))],
        out_shape=[
            shape_of((2 * half_rows, heads * HD)),
            shape_of((2, rows, HD), F32),
            shape_of((2, 1, rows), F32),
        ],
        scratch_shapes=[
            pltpu.VMEM((2, 1, rows), F32),
            pltpu.VMEM((2, 1, rows), F32),
            pltpu.VMEM((2, HD, rows), F32),
        ],
        compiler_params=params(60),
        cost_estimate=cost(TUNE["attend"]),
        name="attend",
    )(queries, near, other, key_code, query_code, *others)


def attend_back_kernel(scale, first_steps, others, q_ref, *refs):
    grads = refs[:4]
    wide_ref, near_ref, other_ref, kc_ref, qc_ref, lse_ref = refs[4:10]
    dq_ref, own_ref, sent_ref, acc, do, delta = refs[10 + others :]
    step = pl.program_id(0)
    half_rows = near_ref.shape[3]
    tok_rows = grads[0].shape[0]

    @pl.when(step == 0)
    def _():
        acc[...] = jnp.zeros(acc.shape, F32)
        for u, grad in enumerate(grads):
            for half, low, row, count in head_rows(tok_rows, 1):
                for j in range(grad.shape[1] // HD):
                    at = j * half_rows + u * (tok_rows // 2)
                    do[half, at : at + count, :] = grad[row : row + count, j * HD : (j + 1) * HD]
        for half in range(2):
            product = do[half].astype(F32) * wide_ref[half]
            delta[half] = jnp.sum(jnp.transpose(product), axis=0, keepdims=True)

    results = []
    for key_half in range(2):
        keys = pick_side(first_steps, near_ref, other_ref, 0, key_half)
        values = pick_side(first_steps, near_ref, other_ref, 1, key_half)
        grad_keys, grad_values = None, None
        for query_half in range(key_half, 2):
            queries = q_ref[query_half]
            grad = do[query_half]
            scores = dot_nt(keys, queries) * (scale * math.log2(math.e))
            weights = jnp.exp2(scores - lse_ref[query_half])
            if key_half == query_half:
                seen = visible_of(codes(kc_ref, key_half), qc_ref[query_half], key_half)
                weights = jnp.where(seen, weights, 0.0)
            grad_weights = dot_nt(values, grad)
            grad_scores = (weights * (grad_weights - delta[query_half])).astype(BF)
            value_term = dot_nn(weights.astype(BF), grad)
            key_term = dot_nn(grad_scores, queries)
            grad_keys = key_term if grad_keys is None else grad_keys + key_term
            grad_values = value_term if grad_values is None else grad_values + value_term
            acc[query_half] += dot_tn(keys, grad_scores)
        shape = (SEQ_STEP, half_rows, HD)
        results.append((grad_keys * scale).reshape(shape).astype(BF))
        results.append(grad_values.reshape(shape).astype(BF))

    def store(ref):
        for key_half in range(2):
            ref[:, 0, key_half] = results[2 * key_half]
            ref[:, 1, key_half] = results[2 * key_half + 1]

    pl.when(step < first_steps)(lambda: store(own_ref))
    pl.when(step >= first_steps)(lambda: store(sent_ref))

    @pl.when(step == pl.num_programs(0) - 1)
    def _():
        for half in range(2):
            dq_ref[half] = jnp.transpose(acc[half] * scale)


def attend_back(queries, grads, wide, near, other, key_code, query_code, log_total, others):
    _, rows, _ = queries.shape
    first_steps = near.shape[0] // SEQ_STEP
    sides = side_specs(near.shape, first_steps)
    return pl.pallas_call(
        functools.partial(attend_back_kernel, HD**-0.5, first_steps, len(others)),
        grid=(2 * first_steps,),
        in_specs=[fixed(queries.shape)]
        + [fixed(grad.shape) for grad in grads]
        + [fixed(wide.shape)]
        + sides
        + [code_spec(key_code.shape), fixed(query_code.shape), fixed(log_total.shape)]
        + [anywhere()] * len(others),
        out_specs=[fixed((2, rows, HD))] + sides,
        out_shape=[shape_of((2, rows, HD), F32), shape_of(near.shape), shape_of(near.shape)],
        scratch_shapes=[
            pltpu.VMEM((2, HD, rows), F32),
            pltpu.VMEM((2, rows, HD), BF),
            pltpu.VMEM((2, 1, rows), F32),
        ],
        compiler_params=params(60),
        cost_estimate=cost(TUNE["attend_back"]),
        name="attend_back",
    )(queries, *grads, wide, near, other, key_code, query_code, log_total, *others)


OUT_TILE = 256
FEED_TILE = 512


def feed_forward_kernel(own_ref, gain_ref, *refs):
    x_hbm = refs[0]
    cot_parts = refs[1:5]
    mixed_parts = refs[5:9]
    near_w, other_w, joined_w = refs[9:12]
    refs = refs[12:]
    acts_ref, hidden_ref, middle_ref, cot_ref = refs[:4]
    dx_refs = refs[4:8]
    x_v, out_v, gate_v, up_v, down_v, mixed_v, normed_v, middle_v, dg_v, du_v, cot_v = refs[8:19]
    in_sem, cot_sem, out_sem, w_sem, s_sem = refs[19:]
    rows, width = x_v.shape
    units = gate_v.shape[1]
    tok_rows = hidden_ref.shape[0]
    half = tok_rows // 2
    blocks = rows // tok_rows
    chunks = cut(units, FEED_TILE)
    cols = mixed_parts[0].shape[1]

    def begin(source, target, sem):
        copy = pltpu.make_async_copy(source, target, sem)
        copy.start()
        return copy

    first = [begin(x_hbm, x_v, in_sem.at[0])]
    for t, part in enumerate(mixed_parts):
        for b in range(blocks):
            u = (b + t) % blocks
            first.append(
                begin(
                    part.at[pl.ds(b * tok_rows, tok_rows), :],
                    mixed_v.at[pl.ds(u * tok_rows, tok_rows), pl.ds(t * cols, cols)],
                    in_sem.at[len(first)],
                )
            )
    first += start_blocks(own_ref, near_w, other_w, out_v, out_sem)
    cots, step = [], cot_parts[0].shape[0] // 2
    for part in cot_parts:
        for low in range(0, part.shape[0], step):
            i = len(cots)
            cots.append(
                begin(
                    part.at[pl.ds(low, half), :], cot_v.at[pl.ds(i * half, half), :], cot_sem.at[i]
                )
            )
    for copy in first:
        copy.wait()
    loads = [
        [
            begin(
                joined_w.at[:, pl.ds(j * units + at, size)], dst.at[:, pl.ds(at, size)], w_sem.at[i, j]
            )
            for j, dst in enumerate((gate_v, up_v, down_v))
        ]
        for i, (at, size) in enumerate(chunks)
    ]
    hidden = x_v[...].astype(F32) + dot_nt(mixed_v[...], out_v[...])
    hidden_ref[...] = hidden[:tok_rows]
    normed_v[...] = (hidden * inverse_norm(hidden) * gain_ref[...]).astype(BF)
    for copy in cots:
        copy.wait()
    normed_to = acts_ref.at[:, pl.ds(2 * units, width)]
    stores = [begin(normed_v, normed_to, s_sem.at[0]), begin(cot_v, cot_ref, s_sem.at[1])]
    for i, (at, size) in enumerate(chunks):
        for copy in loads[i]:
            copy.wait()
        here = slice(at, at + size)
        gate = dot_nn(normed_v[...], gate_v[:, here])
        up = dot_nn(normed_v[...], up_v[:, here])
        grad = dot_nn(cot_v[...], down_v[:, here])
        sig = 1.0 / (1.0 + jnp.exp(-gate))
        active = gate * sig
        middle_v[:, here] = (active * up).astype(BF)
        dg_v[:, here] = (grad * up * sig * (1.0 + gate * (1.0 - sig))).astype(BF)
        du_v[:, here] = (grad * active).astype(BF)
    for j, (src, dst) in enumerate(
        (
            (dg_v, acts_ref.at[:, pl.ds(0, units)]),
            (du_v, acts_ref.at[:, pl.ds(units, units)]),
            (middle_v, middle_ref),
        )
    ):
        stores.append(begin(src, dst, s_sem.at[2 + j]))
    for at, size in cut(width, OUT_TILE):
        here = slice(at, at + size)
        grad = dot_nt(dg_v[...], gate_v[here, :]) + dot_nt(du_v[...], up_v[here, :])
        store_rows(dx_refs, here, grad)
    for copy in stores:
        copy.wait()


def feed_forward(own, x, gain, cot_parts, mixed_parts, near, other, joined_all, tok_rows):
    rows, width = x.shape
    units = joined_all.shape[1] // 3
    blocks = rows // tok_rows
    return pl.pallas_call(
        feed_forward_kernel,
        in_specs=[smem(), vmem()] + [anywhere()] * 12,
        out_specs=[anywhere(), vmem()] + [anywhere()] * 2 + [vmem()] * 4,
        out_shape=[
            shape_of((rows, 2 * units + width)),
            shape_of((tok_rows, width), F32),
            shape_of((rows, units)),
            shape_of((rows, width)),
            *row_shapes(tok_rows, width),
        ],
        scratch_shapes=[
            pltpu.VMEM((rows, width), BF),
            pltpu.VMEM((width, QD), BF),
            pltpu.VMEM((width, units), BF),
            pltpu.VMEM((width, units), BF),
            pltpu.VMEM((width, units), BF),
            pltpu.VMEM((rows, QD), BF),
            pltpu.VMEM((rows, width), BF),
            pltpu.VMEM((rows, units), BF),
            pltpu.VMEM((rows, units), BF),
            pltpu.VMEM((rows, units), BF),
            pltpu.VMEM((rows, width), BF),
            pltpu.SemaphoreType.DMA((1 + blocks * blocks,)),
            pltpu.SemaphoreType.DMA((2 * blocks,)),
            pltpu.SemaphoreType.DMA((2, near.shape[0])),
            pltpu.SemaphoreType.DMA((len(cut(units, FEED_TILE)), 3)),
            pltpu.SemaphoreType.DMA((5,)),
        ],
        compiler_params=params(60),
        cost_estimate=cost(TUNE["feed_forward"]),
        name="feed_forward",
    )(own, gain, x, *cot_parts, *mixed_parts, near, other, joined_all)


def down_product_kernel(others, down_w, middle_ref, *refs):
    refs = refs[others:]
    acc = refs[-1]
    step = pl.program_id(0)

    @pl.when(step == 0)
    def _():
        acc[...] = jnp.zeros(acc.shape, F32)

    acc[...] += dot_nt(middle_ref[...], down_w[...])

    @pl.when(step == pl.num_programs(0) - 1)
    def _():
        store_rows(refs[:-1], slice(None), acc)


def down_product(middle, joined_all, tok_rows, others):
    rows, units = middle.shape
    full = joined_all.shape[0]
    steps = units // TILE
    outs = row_shapes(tok_rows, full)
    return pl.pallas_call(
        functools.partial(down_product_kernel, len(others)),
        grid=(steps,),
        in_specs=[
            pl.BlockSpec((full, TILE), lambda i: (0, 2 * steps + i)),
            pl.BlockSpec((rows, TILE), lambda i: (0, i)),
        ]
        + [anywhere()] * len(others),
        out_specs=[fixed(out.shape) for out in outs],
        out_shape=outs,
        scratch_shapes=[pltpu.VMEM((rows, full), F32)],
        compiler_params=params(60),
        cost_estimate=cost(TUNE["down_product"]),
        name="down_product",
    )(joined_all, middle, *others)


def wide_grads_kernel(x_ref, acts_ref, out_ref, turned):
    @pl.when(pl.program_id(0) == 0)
    def _():
        turned[...] = jnp.transpose(x_ref[...])

    out_ref[...] = dot_nn(turned[...], acts_ref[...]).astype(BF)


def wide_grads(acts, width):
    rows = acts.shape[0]
    units = acts.shape[1] - width
    return pl.pallas_call(
        wide_grads_kernel,
        grid=(units // TILE,),
        in_specs=[
            pl.BlockSpec((rows, width), lambda i: (0, units // width)),
            pl.BlockSpec((rows, TILE), lambda i: (0, i)),
        ],
        out_specs=pl.BlockSpec((width, TILE), lambda i: (0, i)),
        out_shape=shape_of((width, units)),
        scratch_shapes=[pltpu.VMEM((width, rows), BF)],
        compiler_params=params(60),
        cost_estimate=cost(TUNE["wide_grads"]),
        name="wide_grads",
    )(acts, acts)


def pair_grads_kernel(orders, others, own_ref, *refs):
    cots, middles = refs[:2], refs[2:4]
    outs = refs[4 + others : -5]
    one, two, turned, middles_v, sem = refs[-5:]
    count = len(outs) // 2
    copies = [
        pltpu.make_async_copy(ref, middles_v.at[side], sem.at[side])
        for side, ref in enumerate(middles)
    ]
    for copy in copies:
        copy.start()
    blocks = len(orders[0])
    rows = one.shape[0] // blocks
    tokens = cots[0].shape[0]
    cols = outs[0].shape[1]
    for side, cot_ref in enumerate(cots):
        turned[side] = jnp.transpose(cot_ref[...])
        for left, order in ((one, orders[0]), (two, orders[1])):
            for j in range(blocks):
                at = pl.multiple_of((own_ref[0] ^ order[j]) * rows, 16)
                left[j * rows : (j + 1) * rows, side * tokens : (side + 1) * tokens] = turned[
                    side, pl.ds(at, rows), :
                ]
    for copy in copies:
        copy.wait()
    for which, left in enumerate((one, two)):
        here = slice(which * cols, (which + 1) * cols)
        result = dot_nn(left[:, :tokens], middles_v[0, :, here]) + dot_nn(
            left[:, tokens:], middles_v[1, :, here]
        )
        store_rows(outs[which * count : (which + 1) * count], slice(None), result)


def pair_grads(own, orders, cots, middles, others):
    rows, full = cots[0].shape
    cols = middles[0].shape[1] // 2
    outs = [shape_of((n, cols)) for n in (full // 8, full // 8, full // 4)] * 2
    return pl.pallas_call(
        functools.partial(pair_grads_kernel, orders, len(others)),
        in_specs=[smem()] + [vmem()] * 2 + [anywhere()] * (2 + len(others)),
        out_specs=[vmem()] * 6,
        out_shape=outs,
        scratch_shapes=[pltpu.VMEM((full // 2, 2 * rows), BF)] * 2 + [
            pltpu.VMEM((2, full, rows), BF),
            pltpu.VMEM((2,) + middles[0].shape, BF),
            pltpu.SemaphoreType.DMA((2,)),
        ],
        compiler_params=params(60),
        cost_estimate=cost(TUNE["pair_grads"]),
        name="pair_grads",
    )(own, *cots, *middles, *others)


def norm_back_kernel(others, own_ref, *refs):
    near_w, other_w = refs[6:8]
    refs = refs[:6] + refs[8 + others :]
    first_ref, down_ref, up_ref, hidden_ref, gain_ref, cot_ref, dh_ref, branch_ref = refs[:8]
    mixed_refs = refs[8:-3]
    gain_grad_ref, out_v, sem = refs[-3:]
    copies = start_blocks(own_ref, near_w, other_w, out_v, sem)
    grad = first_ref[...] + down_ref[...].astype(F32) + up_ref[...].astype(F32)
    hidden = hidden_ref[...]
    inv = inverse_norm(hidden)
    scaled = grad * gain_ref[...]
    gain_grad_ref[...] = jnp.sum(grad * (hidden * inv), axis=0, keepdims=True)
    inner = jnp.mean(scaled * hidden, axis=-1, keepdims=True)
    d_hidden = cot_ref[...].astype(F32) + inv * scaled - hidden * (inv * inv * inv * inner)
    dh_ref[...] = d_hidden
    branch_ref[...] = d_hidden.astype(BF)
    for copy in copies:
        copy.wait()
    d_mixed = dot_nn(branch_ref[...], out_v[...]).astype(BF)
    cols = mixed_refs[0].shape[1]
    for t, ref in enumerate(mixed_refs):
        ref[...] = d_mixed[:, t * cols : (t + 1) * cols]


def norm_back(own, first, down, up, hidden, gain, cotangent, near, other, blocks, others):
    rows, width = hidden.shape
    return pl.pallas_call(
        functools.partial(norm_back_kernel, len(others)),
        in_specs=[smem()] + [vmem()] * 6 + [anywhere()] * (2 + len(others)),
        out_specs=[vmem()] * (3 + blocks),
        out_shape=[shape_of((rows, width), F32), shape_of((rows, width))]
        + [shape_of((rows, QD // blocks))] * blocks
        + [shape_of((1, width), F32)],
        scratch_shapes=[
            pltpu.VMEM((width, QD), BF),
            pltpu.SemaphoreType.DMA((2, near.shape[0])),
        ],
        compiler_params=params(60),
        cost_estimate=cost(TUNE["norm_back"]),
        name="norm_back",
    )(own, first, down, up, hidden, gain, cotangent, near, other, *others)


def per_device(
    inputs,
    norm_gain_attn,
    qkv_weight,
    qkv_bias,
    out_weight,
    norm_gain_mlp,
    gate_weight,
    up_weight,
    down_weight,
    cotangent,
    segment_ids,
    positions,
):
    tok_rows = inputs.shape[0]
    width = inputs.shape[1]
    seq_dev = lax.axis_size("seq")
    heads_dev = lax.axis_size("head")
    heads_here = HEADS // heads_dev
    copies = heads_dev // KV_HEADS
    group_rows = heads_dev * tok_rows
    half_rows = group_rows // 2
    query_cols = heads_here * HD
    head_index = lax.axis_index("head")
    seq_index = lax.axis_index("seq")
    odd = head_index % 2 == 1
    seq_bits = bits_of("seq")
    head_bits = bits_of("head")
    far = seq_dev // 2
    bits_down = list(range(seq_bits - 1, 0, -1))
    bits_up = bits_down[::-1]
    orders = (masks_of(bits_down), masks_of(bits_up))
    seq_own = seq_index.astype(jnp.int32).reshape(1)
    head_own = head_index.astype(jnp.int32).reshape(1)

    units = gate_weight.shape[1]
    padded = -(-units // TILE) * TILE
    joined = jnp.concatenate(
        [
            jnp.pad(part, ((0, 0), (0, padded - units)))
            for part in (gate_weight, up_weight, down_weight.T)
        ],
        axis=1,
    )
    joined_all = plain(lax.all_gather(plain(joined), "seq", axis=0, tiled=True))


    gain_cols = norm_gain_attn.shape[0]
    bias_cols = qkv_bias.shape[0]
    cols_here = query_cols + 2 * HD
    small = jnp.concatenate(
        [
            norm_gain_attn,
            norm_gain_mlp,
            qkv_bias,
            (positions >> 7).astype(BF),
            (positions & 127).astype(BF),
            segment_ids.astype(BF),
        ]
    )
    small_row = jnp.pad(small[None], ((0, MORE_ROWS - 1), (0, cols_here - small.shape[0])))

    def head_columns(values, head):
        last = values.ndim - 1
        slot = head // copies
        return [
            lax.dynamic_slice_in_dim(values, head * query_cols, query_cols, last),
            lax.dynamic_slice_in_dim(values, QD + slot * HD, HD, last),
            lax.dynamic_slice_in_dim(values, QD + KD + slot * HD, HD, last),
        ]

    own_wide = qkv_weight.shape[0]
    own_rows = own_wide * heads_dev
    rows_of = []
    for apart in range(heads_dev):
        target = (head_index - apart) % heads_dev
        block = jnp.concatenate(head_columns(qkv_weight, target), axis=1)
        block = jnp.concatenate([block, small_row])
        rows_of.append(from_next(block, "head", apart) if apart else block)
    inputs_parts = gather_blocks(tie(inputs, *rows_of[1:]), "head", micros=TUNE["x1"])
    cols_own = arrange(head_own, rows_of)
    small_grp = cols_own[own_rows : own_rows + heads_dev]
    cols_near, _ = far_last(cols_own, far_first(cols_own, "seq"), "seq")
    inputs_parts[2:4] = tie_all(inputs_parts[2:4], micros=TUNE["x2"])
    cols_other = swap(tie(cols_near, *inputs_parts[2:4]), "seq", 0)

    def cut_small(values):
        cuts, start = [], 0
        for size in (gain_cols, gain_cols, bias_cols, tok_rows, tok_rows, tok_rows):
            cuts.append(values[..., start : start + size])
            start += size
        return cuts

    def places(cuts):
        pos = (cuts[3].astype(jnp.int32) << 7) + cuts[4].astype(jnp.int32)
        pos = roll_blocks(pos, head_index, pos.ndim - 2)
        seg = roll_blocks(cuts[5].astype(jnp.int32), head_index, pos.ndim - 2)
        return pos, seg * SEG_STEP + pos

    small_all = jnp.concatenate(
        [part[:, own_rows : own_rows + heads_dev] for part in (cols_near, cols_other)]
    )
    cuts = cut_small(small_all)
    _, key_code = places(cuts)
    query_pos, query_code = places(cut_small(small_grp))
    query_pos = query_pos.reshape(-1)

    def in_order(values):
        masks = [seq_index ^ j for j in range(seq_dev)]
        return jnp.stack(
            [
                lax.dynamic_index_in_dim(values, (m & 1) * far + (m >> 1), 0, keepdims=False)
                for m in masks
            ]
        ).reshape(-1)

    gain_attn = in_order(cuts[0]).reshape(1, -1).astype(F32)
    gain_mlp = in_order(cuts[1]).reshape(1, -1).astype(F32)

    def halves_first(values):
        tail = values.shape[1:]
        return jnp.swapaxes(
            values.reshape((heads_dev, 2, tok_rows // 2) + tail), 0, 1
        ).reshape((2, half_rows) + tail)

    query_code = jnp.broadcast_to(
        halves_first(query_code.reshape(-1))[:, None, None, :], (2, 1, heads_here, half_rows)
    ).reshape(2, 1, heads_here * half_rows)
    key_code = jnp.swapaxes(
        key_code.reshape(seq_dev, heads_dev, 2, tok_rows // 2), 1, 2
    ).reshape(seq_dev, 2, half_rows, 1)
    freq_index = jnp.arange(HD // 2, dtype=F32) * 2.0 / HD
    angles = query_pos.astype(F32)[:, None] * (1.0 / ROPE_BASE**freq_index)[None, :]
    cosine, sine = jnp.cos(angles), jnp.sin(angles)
    cosine_part = jnp.concatenate([cosine, cosine], axis=1)
    sine_part = jnp.concatenate([-sine, sine], axis=1)

    queries, kv_own, inputs_grp, normed_one, cols_weight = project(
        seq_own,
        head_own,
        inputs_parts,
        cosine_part,
        sine_part,
        cols_near,
        cols_other,
        heads_here,
        gain_cols,
        bias_cols,
    )
    half = tok_rows // 2
    out_flat = out_weight.reshape(-1, width)
    out_half = out_flat.shape[0] // 2
    out_pad = -out_half % 16
    cot_mixed = jnp.concatenate(
        [
            part
            for i in range(2)
            for part in (
                cotangent[i * half : (i + 1) * half],
                jnp.pad(out_flat[i * out_half : (i + 1) * out_half], ((0, out_pad), (0, 0))),
            )
        ]
    )
    cot_late = tie(plain(cot_mixed), inputs_parts[2], inputs_parts[3])
    kv_first = far_first(kv_own, "seq")
    cot_parts = gather_blocks(cot_late, "head", kv_first)
    kv_near, _ = far_last(kv_own, kv_first, "seq")
    cot_parts[2:4] = tie_all(cot_parts[2:4], micros=TUNE["c2"])
    kv_other = swap(kv_near, "seq", 0)

    mixed, mixed_wide, log_total = attend(
        queries, kv_near, kv_other, key_code, query_code, tok_rows, cot_parts[2:4]
    )
    late = tie_all([cot_mixed, *cot_parts[1:]], mixed)
    halves = jnp.concatenate(late).reshape(2 * heads_dev, half + out_half + out_pad, width)
    out_rows = plain(halves[:, half : half + out_half].reshape(QD, -1).T)
    out_first = far_first(out_rows, "seq")
    mixed_parts = gather_blocks(mixed, "head", micros=TUNE["mx"])
    out_near, _ = far_last(out_rows, out_first, "seq", [mixed_parts[1], mixed_parts[3]])
    out_other = swap(tie(out_near, *mixed_parts[2:4]), "seq", 0)

    acts, own_hidden, middle, cot_grp, *d_two = feed_forward(
        seq_own,
        inputs_grp,
        gain_mlp,
        cot_parts,
        mixed_parts,
        out_near,
        out_other,
        joined_all,
        tok_rows,
    )

    cots, middles = [[part, swap(part, "seq", 0)] for part in (cot_grp, middle)]
    moved = from_next(d_two[2], "head")
    up = to_next(d_two[1], "head")
    wide_term = wide_grads(acts, width)
    wide_late = tie(wide_term, moved)
    down = sum_payload(d_two[3], moved, others=[cots[1], middles[1]])
    wide_sum = plain(lax.psum_scatter(plain(wide_late), "seq", scatter_dimension=0, tiled=True))
    out_term = down_product(middle, joined_all, tok_rows, [down])
    one_low, one_high, one_sent, two_low, two_high, two_sent = [
        part.reshape(-1, width // seq_dev, part.shape[1])
        for part in pair_grads(seq_own, orders, cots, middles, [down])
    ]
    d_hidden, d_branch, *d_mixed_own, grad_gain_two = norm_back(
        seq_own,
        d_two[0],
        from_next(down, "head"),
        up,
        own_hidden,
        gain_mlp,
        cotangent,
        out_near,
        out_other,
        heads_dev,
        [one_low, out_term[0]],
    )
    d_mixed = [d_mixed_own[0]]
    for apart in range(1, heads_dev):
        d_mixed.append(from_next(d_mixed_own[heads_dev - apart], "head", apart))

    one_moved = swap(one_sent, "seq", bits_down[0])
    two_moved = swap(two_sent, "seq", bits_up[0])
    branch_late = tie(d_branch, *d_mixed[1:])
    above, below = from_next(branch_late, "head"), to_next(branch_late, "head")
    d_queries, d_kv_own, d_kv_sent = attend_back(
        queries,
        d_mixed,
        mixed_wide,
        kv_near,
        kv_other,
        key_code,
        query_code,
        log_total,
        [],
    )
    d_kv_moved = swap(tie(d_kv_sent, above, below), "seq", 0)
    half = tok_rows // 2
    above, below = tie_all([above, below], d_queries)
    out_up = to_next(tie(out_term[1], *d_mixed[1:]), "head")
    far_both = from_next(jnp.concatenate([above, out_term[2]]), "head")
    far_both = tie_all([far_both], micros=TUNE["far"])[0]
    branch_parts = [d_branch, above, far_both, below]
    down = sum_payload(out_term[3], far_both[tok_rows:], others=[out_up])
    out_moved = [from_next(down, "head"), out_up]
    one_moved, two_moved = tie_all([one_moved, two_moved], micros=TUNE["g1"])
    d_kv_moved = tie(d_kv_moved, one_moved, two_moved)
    d_kv = total([d_kv_own, d_kv_moved])
    d_keys, keys_last = sum_xor([d_kv[i, 0] for i in range(far)], "seq", bits_down)
    d_values, values_last = sum_xor([d_kv[i, 1] for i in range(far)], "seq", bits_up)
    d_other_raw = jnp.where(odd, d_keys, d_values).astype(BF)
    d_other_sent = d_other_raw
    d_other_raw = swap(d_other_sent, "head", 0)
    d_other = d_other_raw.reshape(2, heads_dev, tok_rows // 2, HD)
    d_other = roll_blocks(d_other, jnp.where(odd, 1, heads_dev - 1), 1).reshape(2, half_rows, HD)
    d_kv_total = jnp.where(odd, d_values, d_keys) + d_other.astype(F32)


    def second(low, high, moved, bit):
        half = high.shape[0]
        moved = tie(moved, d_other_sent)
        return [low, moved[:half], swap(total([high, moved[half:]]).astype(BF), "seq", bit)]

    one_terms = second(one_low, one_high, one_moved, bits_down[1])
    two_terms = second(two_low, two_high, two_moved, bits_up[1])
    one_terms[-1], two_terms[-1] = tie_all([one_terms[-1], two_terms[-1]], micros=TUNE["s2"])
    *d_one, cols_kept, outs_kept, wide_sent = project_back(
        seq_own,
        head_own,
        orders,
        d_queries,
        d_kv_total,
        cosine_part,
        sine_part,
        normed_one,
        inputs_grp,
        cols_weight,
        mixed,
        branch_parts,
        grad_gain_two,
        out_moved,
    )
    ahead, across = tie_all(d_one[1:3], one_terms[-1], two_terms[-1])
    moved = from_next(across, "head")
    up = to_next(ahead, "head")
    wide_moved = tie_all([swap(wide_sent, "seq", 0)], micros=TUNE["wm"])[0]
    down = sum_payload(d_one[3], moved, others=[wide_moved, up])
    one_terms[-1], two_terms[-1] = tie(one_terms[-1], down), tie(two_terms[-1], down)
    output = total([own_hidden, out_term[0], *out_moved]).astype(BF)
    cols_moved = wide_moved[:, :, : query_cols + HD]
    outs_moved = wide_moved[:, :own_rows, query_cols + HD :]
    cols_terms = sum_step([cols_kept, cols_moved], "seq", bits_down[0])
    outs_terms = sum_step([outs_kept, outs_moved], "seq", bits_up[0])
    cols_terms[-1], outs_terms[-1] = tie_all([cols_terms[-1], outs_terms[-1]], micros=TUNE["ct"])
    down = from_next(down, "head")
    d_normed_one = total([d_one[0], tie(down, cols_terms[-1], outs_terms[-1]), up])
    grad_cols = sum_halving(cols_terms, "seq", bits_down[1:]).astype(BF)
    grad_outs = sum_halving(outs_terms, "seq", bits_up[1:])
    inputs_f = inputs.astype(F32)
    inv_one = inverse_norm(inputs_f)
    scaled = d_normed_one * gain_attn
    inner = jnp.mean(scaled * inputs_f, axis=-1, keepdims=True)
    grad_inputs = (d_hidden + inv_one * scaled - inputs_f * (inv_one**3 * inner)).astype(BF)

    grad_out = grad_outs.T
    cols_wide = query_cols + HD
    more_rows = jnp.broadcast_to(grad_cols[own_rows:], (heads_dev, MORE_ROWS, cols_wide))
    grad_blocks = jnp.concatenate(
        [grad_cols[:own_rows].reshape(heads_dev, own_wide, cols_wide), more_rows], axis=1
    )
    grad_qkv = jnp.zeros((own_wide, QKV), F32)
    small_parts = []
    for apart in range(heads_dev):
        source = (head_index + apart) % heads_dev
        target = (head_index - apart) % heads_dev
        block = lax.dynamic_index_in_dim(grad_blocks, target, 0, keepdims=False)
        if apart:
            block = from_next(tie(block, wide_sum), "head", apart)
        small_parts.append(block[own_wide : own_wide + 2])
        block = block[:own_wide].astype(F32)
        kv_place = QD + source % 2 * KD + source // copies * HD
        grad_qkv = lax.dynamic_update_slice_in_dim(
            grad_qkv, block[:, :query_cols], source * query_cols, 1
        )
        grad_qkv = lax.dynamic_update_slice_in_dim(grad_qkv, block[:, query_cols:], kv_place, 1)
    small_grads = total(small_parts)

    def own_part(row, start, size):
        return lax.dynamic_slice(small_grads, (row, start + head_index * size), (1, size)).reshape(size)

    key_bias = (QD + KD) // (seq_dev * heads_dev)
    value_bias = KD // (seq_dev * heads_dev)

    grad_down = jnp.concatenate(
        [
            sum_halving(one_terms, "seq", bits_down[2:]),
            sum_halving(two_terms, "seq", bits_up[2:]),
        ],
        axis=1,
    )[:, :units].T

    return (
        output,
        grad_inputs,
        own_part(0, 0, gain_cols),
        grad_qkv,
        own_part(1, 0, key_bias),
        own_part(1, heads_dev * key_bias, value_bias),
        grad_out,
        own_part(0, heads_dev * gain_cols, gain_cols),
        wide_sum[:, :units].astype(F32),
        wide_sum[:, padded : padded + units].astype(F32),
        grad_down,
    )


def solution(mesh):
    both = ("seq", "head")
    in_specs = (
        P(both, None),
        P(both),
        P(both, None),
        P(both),
        P("head", "seq"),
        P(both),
        P("seq", "head"),
        P("seq", "head"),
        P("head", "seq"),
        P(both, None),
        P(both),
        P(both),
    )
    out_specs = (
        P(both, None),
        P(both, None),
        P(both),
        P(both, None),
        P(both),
        P(both),
        P("head", "seq"),
        P(both),
        P("seq", "head"),
        P("seq", "head"),
        P("head", "seq"),
    )
    return jax.shard_map(
        per_device, mesh=mesh, in_specs=in_specs, out_specs=out_specs, check_vma=False
    )
```
